128 devices in a mesh: gx: 8 (over x_hi, z), af: 16 (over x_lo, y, core).
Axes of the slice: x: 4 (x_hi: 2, x_lo: 2; x = x_hi * 2 + x_lo), y: 4, z: 4, core: 2. Of those that a mesh axis runs over, the one named last changes fastest.
Arguments:
- displace: bfloat16 [32, 20, 36, 128], P('gx'), may hold values from -6 to 6
- weight_in: bfloat16 [3, 3, 3, 128, 512], P(None, None, None, None, 'af'), may hold values from -0.109375 to 0.109375
- weight_out: bfloat16 [3, 3, 3, 512, 128], P(None, None, None, 'af'), may hold values from -0.109375 to 0.109375
- cotangent: bfloat16 [32, 16, 32, 128], P('gx'), may hold values from -6 to 6
Outputs:
- out_field: bfloat16 [32, 16, 32, 128], P('gx')
- field_grad: float32 [32, 20, 36, 128], P('gx')
- inner_grad: float32 [3, 3, 3, 128, 512], P(None, None, None, None, 'af')
- outer_grad: float32 [3, 3, 3, 512, 128], P(None, None, None, 'af')
The draws below stay inside these ranges and needn't reach their ends.
All inputs are finite; a program needn't handle non-finite values.
Results may differ from the reference program's by a relative error of at most 0.018.
Values may be sent and summed in bfloat16 or wider, within the bound.
A program may use at most 256 MiB of HBM per device.

```python
import jax
import jax.numpy as jnp

C = 128
M = 512
Y = 16
Z = 32
X = 32


def levels(key, dims, pieces, low, high):
    factor_of, own = 1.0, jax.random.fold_in(key, 6)
    for position, parts in pieces:
        steps = jnp.exp(jax.random.uniform(jax.random.fold_in(own, position), (parts,), jnp.float32, low / len(pieces), high / len(pieces)))
        factor_of = factor_of * jnp.repeat(steps, dims[position] // parts).reshape([-1 if axis == position else 1 for axis in range(len(dims))])
    return factor_of


def bell_draw(rng, dims, deviation, most, pieces=(), dtype=jnp.bfloat16):
    array = deviation * jax.random.normal(rng, dims, jnp.float32)
    if pieces:
        array = array * levels(rng, dims, pieces, -0.22, 0.18)
    return jnp.clip(array, -most, most).astype(dtype)


def setup_inputs(seed: int = 0) -> dict:
    key_list = jax.random.split(jax.random.key(seed), 5)
    return {
        "displace": bell_draw(key_list[0], (X, Y + 4, Z + 4, C), 1.0, 6.0, ((0, 8),)),
        "weight_in": bell_draw(key_list[1], (3, 3, 3, C, M), (27 * C) ** -0.5, 0.109375, ((4, 16),)),
        "weight_out": bell_draw(key_list[2], (3, 3, 3, M, C), (27 * M // 4) ** -0.5, 0.109375, ((3, 16),)),
        "cotangent": bell_draw(key_list[3], (X, Y, Z, C), 1.0, 6.0, ((0, 8),)),
    }


def activate(values):
    return 0.505 * values + 0.495 * jnp.sqrt(values * values + 0.01)

def slope_of(values):
    return 0.505 + 0.495 * values / jnp.sqrt(values * values + 0.01)

def reference(displace, weight_in, weight_out, cotangent):
    field_in = displace.astype(jnp.float32)
    inner_w = weight_in.astype(jnp.float32)
    outer_w = weight_out.astype(jnp.float32)
    preact = jnp.zeros((X, Y + 2, Z + 2, M), jnp.float32)
    for tap_x in range(3):
        rolled = jnp.roll(field_in, 1 - tap_x, axis=0)
        for tap_y in range(3):
            for tap_z in range(3):
                window = rolled[:, tap_y:tap_y + Y + 2, tap_z:tap_z + Z + 2, :]
                preact = preact + jnp.einsum('xyzc,cm->xyzm', window, inner_w[tap_x, tap_y, tap_z])
    hidden = activate(preact).astype(jnp.bfloat16)
    hidden_f = hidden.astype(jnp.float32)
    convolved = jnp.zeros((X, Y, Z, C), jnp.float32)
    outer_list = []
    cot_f = cotangent.astype(jnp.float32)
    for tap_x in range(3):
        rolled = jnp.roll(hidden_f, 1 - tap_x, axis=0)
        for tap_y in range(3):
            for tap_z in range(3):
                window = rolled[:, tap_y:tap_y + Y, tap_z:tap_z + Z, :]
                convolved = convolved + jnp.einsum('xyzm,mc->xyzc', window, outer_w[tap_x, tap_y, tap_z])
                outer_list.append(jnp.einsum('xyzm,xyzc->mc', window, cot_f))
    interior = field_in[:, 2:2 + Y, 2:2 + Z, :]
    out_field = (interior + convolved).astype(jnp.bfloat16)
    cot_padded = jnp.pad(cot_f, ((0, 0), (2, 2), (2, 2), (0, 0)))
    hidden_grad = jnp.zeros((X, Y + 2, Z + 2, M), jnp.float32)
    for tap_x in range(3):
        rolled = jnp.roll(cot_padded, tap_x - 1, axis=0)
        for tap_y in range(3):
            for tap_z in range(3):
                window = rolled[:, 2 - tap_y:2 - tap_y + Y + 2, 2 - tap_z:2 - tap_z + Z + 2, :]
                hidden_grad = hidden_grad + jnp.einsum('xyzc,mc->xyzm', window, outer_w[tap_x, tap_y, tap_z])
    pre_grad = (hidden_grad * slope_of(preact)).astype(jnp.bfloat16)
    pre_f = pre_grad.astype(jnp.float32)
    inner_list = []
    for tap_x in range(3):
        rolled = jnp.roll(field_in, 1 - tap_x, axis=0)
        for tap_y in range(3):
            for tap_z in range(3):
                window = rolled[:, tap_y:tap_y + Y + 2, tap_z:tap_z + Z + 2, :]
                inner_list.append(jnp.einsum('xyzc,xyzm->cm', window, pre_f))
    grad_padded = jnp.pad(pre_f, ((0, 0), (2, 2), (2, 2), (0, 0)))
    field_grad = cot_padded
    for tap_x in range(3):
        rolled = jnp.roll(grad_padded, tap_x - 1, axis=0)
        for tap_y in range(3):
            for tap_z in range(3):
                window = rolled[:, 2 - tap_y:2 - tap_y + Y + 4, 2 - tap_z:2 - tap_z + Z + 4, :]
                field_grad = field_grad + jnp.einsum('xyzm,cm->xyzc', window, inner_w[tap_x, tap_y, tap_z])
    inner_grad = jnp.stack(inner_list).reshape(3, 3, 3, C, M)
    outer_grad = jnp.stack(outer_list).reshape(3, 3, 3, M, C)
    return (out_field, field_grad, inner_grad, outer_grad)
```

```python
import functools

import jax
import jax.numpy as jnp
from jax import lax
from jax.experimental import pallas as pl
from jax.experimental.pallas import tpu as pltpu
from jax.sharding import PartitionSpec as P

MESH = pl.DeviceIdType.MESH
BF = jnp.bfloat16
F32 = jnp.float32

SLAB = 4
CY, CZ = 16, 32
PITCH = 48
LANES = 128
MID = 32
TAPS = 9
YC = 9

OUT_PIECES = 2
FIELD_PIECES = 3
PIECE = 1024
AF_PIECES = OUT_PIECES + FIELD_PIECES
WROWS = 896
FIELD_ROWS = 20 * 36 * SLAB
FIELD_LINES = ((0, 8), (8, 15), (15, 20))


def kernel(
    disp, cot, win, wout,
    out_ref, field_ref, inner_ref, outer_ref,
    D, C, H3, P3, W1T, W1, W2T, W2, AI, AO, FS, IN, B, R, WB, WR,
    rcore, rone, rtwo, rthree, wone, wtwo, wthree,
    load_sem, halo_s, halo_r, rs_s, rs_r, ag_s, ag_r, ws_s, ws_r, wg_s, wg_r,
):
    gx = lax.axis_index("gx")
    af = lax.axis_index("af")
    core = lax.rem(af, 2)
    y = lax.rem(lax.div(af, 2), 4)
    xl = lax.div(af, 8)
    z = lax.rem(gx, 4)
    xh = lax.div(gx, 4)

    def gray(v):
        s = lax.div(v, 2)
        t = lax.rem(s + lax.rem(v, 2), 2)
        return t, s

    yt, ys = gray(y)
    zt, zs = gray(z)

    def af_id(xl_, y_, core_):
        return (gx, (xl_ * 4 + y_) * 2 + core_)

    def gx_id(xh_, z_):
        return (xh_ * 4 + z_, af)

    def flip(v):
        return v + 1 - 2 * lax.rem(v, 2)

    dim_core = (core, af_id(xl, y, 1 - core))
    dim_yt = (yt, af_id(xl, flip(y), core))
    dim_ys = (ys, af_id(xl, 3 - y, core))
    dim_xl = (xl, af_id(1 - xl, y, core))
    dim_zt = (zt, gx_id(xh, flip(z)))
    dim_zs = (zs, gx_id(xh, 3 - z))
    dim_xh = (xh, gx_id(1 - xh, z))
    right = (lax.rem(gx + 1, 8), af)
    left = (lax.rem(gx + 7, 8), af)

    loads = [
        pltpu.make_async_copy(disp, D.at[pl.ds(1, SLAB)], load_sem.at[0]),
        pltpu.make_async_copy(cot, C.at[pl.ds(1, SLAB), pl.ds(2, CY)], load_sem.at[1]),
    ]
    for load in loads:
        load.start()

    barrier = pltpu.get_barrier_semaphore()
    peers = [dim[1] for dim in (dim_core, dim_yt, dim_ys, dim_xl, dim_zt, dim_zs, dim_xh)] + [left, right]
    for peer in peers:
        pl.semaphore_signal(barrier, inc=1, device_id=peer, device_id_type=MESH)

    zero_rows = jnp.zeros((LANES - 3 * MID, LANES), BF)
    for tap in range(TAPS):
        rows = pl.ds(tap * LANES, LANES)
        for src, straight, turned in ((win, W1, W1T), (wout, W2, W2T)):
            block = jnp.concatenate([src[tap], zero_rows], axis=0)
            straight[rows, :] = block
            turned[rows, :] = block.T

    C[:, 0:2] = jnp.zeros((6, 2, CZ, LANES), BF)
    C[:, 18:20] = jnp.zeros((6, 2, CZ, LANES), BF)
    P3[:, 0:2] = jnp.zeros((6, 2, PITCH, LANES), BF)
    P3[:, 20:22] = jnp.zeros((6, 2, PITCH, LANES), BF)
    FS[FIELD_ROWS:, :] = jnp.zeros((FIELD_PIECES * PIECE - FIELD_ROWS, LANES), F32)
    AI[...] = jnp.zeros_like(AI)
    AO[...] = jnp.zeros_like(AO)
    zero_tail = jnp.zeros((WROWS - TAPS * 3 * MID, LANES), BF)
    WB[0, TAPS * 3 * MID:, :] = zero_tail
    WB[1, TAPS * 3 * MID:, :] = zero_tail

    for load in loads:
        load.wait()
    pl.semaphore_wait(barrier, len(peers))

    def halo(index, src, dst, peer):
        copy = pltpu.make_async_remote_copy(
            src_ref=src, dst_ref=dst, send_sem=halo_s.at[index], recv_sem=halo_r.at[index],
            device_id=peer, device_id_type=MESH,
        )
        copy.start()
        return copy

    halos = [
        halo(0, D.at[SLAB], D.at[0], right),
        halo(1, D.at[1], D.at[SLAB + 1], left),
        halo(2, C.at[SLAB, pl.ds(2, CY)], C.at[0, pl.ds(2, CY)], right),
        halo(3, C.at[1, pl.ds(2, CY)], C.at[SLAB + 1, pl.ds(2, CY)], left),
    ]

    rows_n = YC * PITCH
    lane = lax.broadcasted_iota(jnp.int32, (rows_n, LANES), 1)
    first = lane < MID

    def gather(values, direction):
        one = pltpu.roll(pltpu.roll(values, LANES - MID, 1), (-direction) % rows_n, 0)
        two = pltpu.roll(pltpu.roll(values, LANES - 2 * MID, 1), (-2 * direction) % rows_n, 0)
        return values + one + two

    def spread(values, direction):
        one = pltpu.roll(pltpu.roll(values, MID, 1), (-direction) % rows_n, 0)
        two = pltpu.roll(pltpu.roll(values, 2 * MID, 1), (-2 * direction) % rows_n, 0)
        return values + one + two

    def stage_one(x, y0):
        lhs = jnp.concatenate(
            [D[x + a, pl.ds(y0 + b, YC)].reshape(rows_n, LANES) for a in range(3) for b in range(3)], axis=1
        )
        pre = gather(jnp.dot(lhs, W1T[...], preferred_element_type=F32), 1)
        lhs = jnp.concatenate(
            [
                C[x + 2 - a, pl.ds(y0 + 2 - b, YC)].reshape(YC * CZ, LANES)
                for a in range(3)
                for b in range(3)
            ],
            axis=1,
        )
        back = jnp.dot(lhs, W2T[...], preferred_element_type=F32).reshape(YC, CZ, LANES)
        back = jnp.concatenate([back, jnp.zeros((YC, PITCH - CZ, LANES), F32)], axis=1)
        grad = gather(back.reshape(rows_n, LANES), -1)
        square = pre * pre + 0.01
        inverse = lax.rsqrt(square)
        hidden = 0.505 * pre + 0.495 * (square * inverse)
        slope = 0.505 + 0.495 * (pre * inverse)
        hidden = spread(jnp.where(first, hidden, 0.0), 1)
        H3[x + 1, pl.ds(y0, YC)] = hidden.reshape(YC, PITCH, LANES)[:, :CZ].astype(BF)
        grad = spread(jnp.where(first, grad * slope, 0.0), -1)
        P3[x + 1, pl.ds(y0 + 2, YC)] = grad.reshape(YC, PITCH, LANES).astype(BF)

    steps = 18 // YC

    def inner_planes(i, _):
        stage_one(1 + lax.div(i, steps), lax.rem(i, steps) * YC)
        return 0

    def outer_planes(i, _):
        stage_one(3 * lax.div(i, steps), lax.rem(i, steps) * YC)
        return 0

    lax.fori_loop(0, 2 * steps, inner_planes, 0)
    for copy in halos[:4]:
        copy.wait_recv()
    lax.fori_loop(0, 2 * steps, outer_planes, 0)

    own = pl.ds(2, 18)
    halos += [
        halo(4, H3.at[SLAB], H3.at[0], right),
        halo(5, H3.at[1], H3.at[SLAB + 1], left),
        halo(6, P3.at[SLAB, own], P3.at[0, own], right),
        halo(7, P3.at[1, own], P3.at[SLAB + 1, own], left),
    ]

    sends = []

    def exchange(copy_args, peer):
        copy = pltpu.make_async_remote_copy(device_id=peer, device_id_type=MESH, **copy_args)
        copy.start()
        sends.append(copy)
        return copy

    class Sum:
        def __init__(self, rows, dims, part, landing, full, rs, ag, finish):
            self.rows, self.dims, self.part, self.landing, self.full = rows, dims, part, landing, full
            self.rs, self.ag, self.finish = rs, ag, finish
            self.offs, self.size, self.copy, self.step = [0], rows, None, 0

        def advance(self):
            n = len(self.dims)
            if self.step > 0:
                self.copy.wait_recv()
            if 0 < self.step <= n:
                k = self.step - 1
                half = self.size
                off = self.offs[-1]
                mine = self.part(off, half)
                total = mine[...].astype(F32) + self.landing(k)[...].astype(F32)
                if self.step < n:
                    mine[...] = total.astype(BF)
                else:
                    self.full(off, half)[...] = self.finish(total, off, half).astype(BF)
            if self.step < n:
                bit, peer = self.dims[self.step]
                half = self.size // 2
                base = self.offs[-1]
                keep = pl.multiple_of(base + bit * half, 16)
                give = pl.multiple_of(base + (1 - bit) * half, 16)
                self.copy = exchange(
                    dict(
                        src_ref=self.part(give, half), dst_ref=self.landing(self.step),
                        send_sem=self.rs[0](self.step), recv_sem=self.rs[1](self.step),
                    ),
                    peer,
                )
                self.offs.append(keep)
                self.size = half
            elif self.step < 2 * n:
                k = 2 * n - 1 - self.step
                bit, peer = self.dims[k]
                off = self.offs[k + 1]
                block = self.full(off, self.size)
                self.copy = exchange(
                    dict(src_ref=block, dst_ref=block, send_sem=self.ag[0](k), recv_sem=self.ag[1](k)), peer
                )
                self.size *= 2
            self.step += 1

    af_landing = (rcore, rone, rtwo, rthree)
    orders = (
        (dim_core, dim_yt, dim_ys, dim_xl),
        (dim_core, dim_ys, dim_yt, dim_xl),
        (dim_core, dim_yt, dim_ys, dim_xl),
        (dim_core, dim_ys, dim_xl, dim_yt),
        (dim_core, dim_xl, dim_yt, dim_ys),
    )

    def af_sum(p):
        def full(off, size):
            if p < OUT_PIECES:
                return out_ref.at[pl.ds(pl.multiple_of(p * PIECE + off, 16), size)]
            return R.at[pl.ds(pl.multiple_of((p - OUT_PIECES) * PIECE + off, 16), size)]

        def finish(total, off, size):
            if p < OUT_PIECES:
                return total + IN[pl.ds(pl.multiple_of(p * PIECE + off, 16), size), :]
            return total

        return Sum(
            PIECE, orders[p],
            lambda off, size: B.at[pl.ds(pl.multiple_of(p * PIECE + off, 16), size)],
            lambda k: af_landing[k].at[p],
            full,
            (lambda k: rs_s.at[p, k], lambda k: rs_r.at[p, k]),
            (lambda k: ag_s.at[p, k], lambda k: ag_r.at[p, k]),
            finish,
        )

    w_landing = (wone, wtwo, wthree)

    def gx_sum(p):
        return Sum(
            WROWS, ((dim_zt, dim_zs, dim_xh), (dim_zs, dim_zt, dim_xh))[p],
            lambda off, size: WB.at[p, pl.ds(off, size)],
            lambda k: w_landing[k].at[p],
            lambda off, size: WR.at[p, pl.ds(off, size)],
            (lambda k: ws_s.at[p, k], lambda k: ws_r.at[p, k]),
            (lambda k: wg_s.at[p, k], lambda k: wg_r.at[p, k]),
            lambda total, off, size: total,
        )

    af_sums = [af_sum(p) for p in range(AF_PIECES)]
    gx_sums = [gx_sum(p) for p in range(2)]
    over_rows = (((0,), (0,)), ((), ()))

    def outer_terms(i, _):
        left_side = jnp.concatenate(
            [H3[i + 1, pl.ds(b, CY)].reshape(CY * CZ, LANES) for b in range(3)], axis=1
        )
        right_side = jnp.concatenate(
            [C[i + 2 - a, pl.ds(2, CY)].reshape(CY * CZ, LANES) for a in range(3)], axis=1
        )
        AO[...] += lax.dot_general(left_side, right_side, over_rows, preferred_element_type=F32)
        return 0

    def inner_terms(i, _):
        left_side = jnp.concatenate(
            [P3[i + 1, pl.ds(2 - b, 20)].reshape(20 * PITCH, LANES) for b in range(3)], axis=1
        )
        right_side = jnp.concatenate([D[i + a].reshape(20 * PITCH, LANES) for a in range(3)], axis=1)
        AI[...] += lax.dot_general(left_side, right_side, over_rows, preferred_element_type=F32)
        return 0

    def collect(acc, p):
        for a in range(3):
            for b in range(3):
                WB[p, pl.ds((a * 3 + b) * 3 * MID, 3 * MID), :] = acc[
                    b * LANES : b * LANES + 3 * MID, a * LANES : (a + 1) * LANES
                ].astype(BF)

    lax.fori_loop(0, SLAB, outer_terms, 0)
    collect(AO, 1)
    gx_sums[1].advance()
    lax.fori_loop(0, SLAB, inner_terms, 0)
    collect(AI, 0)
    gx_sums[0].advance()

    for copy in halos[4:6]:
        copy.wait_recv()

    def out_plane(i, _):
        lhs = jnp.concatenate(
            [H3[i + a, pl.ds(b, CY)].reshape(CY * CZ, LANES) for a in range(3) for b in range(3)], axis=1
        )
        B[pl.ds(pl.multiple_of(i * CY * CZ, 16), CY * CZ), :] = jnp.dot(
            lhs, W2[...], preferred_element_type=F32
        ).astype(BF)
        return 0

    for p in range(OUT_PIECES):
        lax.fori_loop(2 * p, 2 * p + 2, out_plane, 0)
        af_sums[p].advance()

    def interior(i, _):
        block = D[i + 1, pl.ds(2, CY)].astype(F32)[:, 2 : 2 + CZ, :]
        IN[pl.ds(pl.multiple_of(i * CY * CZ, 16), CY * CZ), :] = block.reshape(CY * CZ, LANES)
        return 0

    lax.fori_loop(0, SLAB, interior, 0)

    for copy in halos[6:8]:
        copy.wait_recv()

    for p, (low, high) in enumerate(FIELD_LINES):
        count = high - low

        def field_lines(i, _):
            lhs = jnp.concatenate(
                [
                    P3[i + 2 - a, pl.ds(low + 2 - b, count)].reshape(count * PITCH, LANES)
                    for a in range(3)
                    for b in range(3)
                ],
                axis=1,
            )
            block = jnp.dot(lhs, W1[...], preferred_element_type=F32).reshape(count, PITCH, LANES)
            for line in range(count):
                FS[pl.ds((low + line) * 36 * SLAB + i, 36, stride=SLAB), :] = block[line, :36]
            return 0

        lax.fori_loop(0, SLAB, field_lines, 0)
        B[pl.ds((OUT_PIECES + p) * PIECE, PIECE), :] = FS[pl.ds(p * PIECE, PIECE), :].astype(BF)
        af_sums[OUT_PIECES + p].advance()
        for item in af_sums[:OUT_PIECES + p] + gx_sums:
            item.advance()

    field_ref[...] = jnp.zeros_like(field_ref)

    def cot_plane(i, _):
        for line in range(CY):
            field_ref[pl.ds((line + 2) * 36 * SLAB + 2 * SLAB + i, CZ, stride=SLAB), :] = C[
                i + 1, line + 2
            ].astype(F32)
        return 0

    lax.fori_loop(0, SLAB, cot_plane, 0)

    everything = gx_sums + af_sums
    while any(item.step <= 2 * len(item.dims) for item in everything):
        for item in everything:
            if item.step <= 2 * len(item.dims):
                item.advance()
                if item.step > 2 * len(item.dims):
                    if item in gx_sums:
                        p = gx_sums.index(item)
                        (inner_ref, outer_ref)[p][...] = WR[p, : TAPS * 3 * MID].astype(F32)
                    else:
                        p = af_sums.index(item) - OUT_PIECES
                        if p >= 0:
                            rows = pl.ds(p * PIECE, min(PIECE, FIELD_ROWS - p * PIECE))
                            field_ref[rows, :] = field_ref[rows, :] + R[rows, :].astype(F32)
    for copy in halos + sends:
        copy.wait_send()


def shards(displace, weight_in, weight_out, cotangent):
    vmem = pl.BlockSpec(memory_space=pltpu.VMEM)
    hbm = pl.BlockSpec(memory_space=pl.ANY)
    padded = jnp.pad(displace, ((0, 0), (0, 0), (0, PITCH - 36), (0, 0)))
    win = jnp.transpose(weight_in, (0, 1, 2, 4, 3)).reshape(TAPS, 3 * MID, LANES)
    wout = weight_out.reshape(TAPS, 3 * MID, LANES)
    dma = pltpu.SemaphoreType.DMA
    out, field, inner, outer = pl.pallas_call(
        kernel,
        out_shape=(
            jax.ShapeDtypeStruct((SLAB * CY * CZ, LANES), BF),
            jax.ShapeDtypeStruct((FIELD_ROWS, LANES), F32),
            jax.ShapeDtypeStruct((TAPS * 3 * MID, LANES), F32),
            jax.ShapeDtypeStruct((TAPS * 3 * MID, LANES), F32),
        ),
        in_specs=[hbm, hbm, vmem, vmem],
        out_specs=[vmem] * 4,
        scratch_shapes=[
            pltpu.VMEM((SLAB + 2, 20, PITCH, LANES), BF),
            pltpu.VMEM((SLAB + 2, 20, CZ, LANES), BF),
            pltpu.VMEM((SLAB + 2, 18, CZ, LANES), BF),
            pltpu.VMEM((SLAB + 2, 22, PITCH, LANES), BF),
            pltpu.VMEM((TAPS * LANES, LANES), BF),
            pltpu.VMEM((TAPS * LANES, LANES), BF),
            pltpu.VMEM((TAPS * LANES, LANES), BF),
            pltpu.VMEM((TAPS * LANES, LANES), BF),
            pltpu.VMEM((3 * LANES, 3 * LANES), F32),
            pltpu.VMEM((3 * LANES, 3 * LANES), F32),
            pltpu.VMEM((FIELD_PIECES * PIECE, LANES), F32),
            pltpu.VMEM((SLAB * CY * CZ, LANES), F32),
            pltpu.VMEM((AF_PIECES * PIECE, LANES), BF),
            pltpu.VMEM((FIELD_PIECES * PIECE, LANES), BF),
            pltpu.VMEM((2, WROWS, LANES), BF),
            pltpu.VMEM((2, WROWS, LANES), BF),
            pltpu.VMEM((AF_PIECES, PIECE // 2, LANES), BF),
            pltpu.VMEM((AF_PIECES, PIECE // 4, LANES), BF),
            pltpu.VMEM((AF_PIECES, PIECE // 8, LANES), BF),
            pltpu.VMEM((AF_PIECES, PIECE // 16, LANES), BF),
            pltpu.VMEM((2, WROWS // 2, LANES), BF),
            pltpu.VMEM((2, WROWS // 4, LANES), BF),
            pltpu.VMEM((2, WROWS // 8, LANES), BF),
            dma((2,)), dma((8,)), dma((8,)),
            dma((AF_PIECES, 4)), dma((AF_PIECES, 4)), dma((AF_PIECES, 4)), dma((AF_PIECES, 4)),
            dma((2, 3)), dma((2, 3)), dma((2, 3)), dma((2, 3)),
        ],
        compiler_params=pltpu.CompilerParams(
            collective_id=0, has_side_effects=True, vmem_limit_bytes=56 * 1024 * 1024
        ),
        cost_estimate=pl.CostEstimate(flops=4_000_000_000, bytes_accessed=8_000_000, transcendentals=400_000),
    )(padded, cotangent, win, wout)
    out_field = out.reshape(SLAB, CY, CZ, LANES)
    field_grad = jnp.transpose(field.reshape(20, 36, SLAB, LANES), (2, 0, 1, 3))
    inner_grad = jnp.transpose(inner.reshape(3, 3, 3, MID, LANES), (0, 1, 2, 4, 3))
    outer_grad = outer.reshape(3, 3, 3, MID, LANES)
    return (out_field, field_grad, inner_grad, outer_grad)


def solution(mesh):
    return jax.shard_map(
        shards,
        mesh=mesh,
        in_specs=(
            P("gx", None, None, None),
            P(None, None, None, None, "af"),
            P(None, None, None, "af", None),
            P("gx", None, None, None),
        ),
        out_specs=(
            P("gx", None, None, None),
            P("gx", None, None, None),
            P(None, None, None, None, "af"),
            P(None, None, None, "af", None),
        ),
        check_vma=False,
    )
```

```python
import jax
import jax.numpy as jnp
from jax import lax
from jax.experimental import pallas as pl
from jax.experimental.pallas import tpu as pltpu
from jax.sharding import PartitionSpec as P

MESH = pl.DeviceIdType.MESH
BF = jnp.bfloat16
F32 = jnp.float32

SLAB = 4
CY, CZ = 16, 32
PITCH = 48
LANES = 128
MID = 32
TAPS = 9
HY, HALF = 18, 9
FY, FZ = 20, 36
PLANE = FY * FZ
CELLS = CY * CZ
ORDER = (1, 2, 0, 3)

OUT_PIECE = 2 * CELLS
FIELD_PIECE = 1536
AF_ROWS = (OUT_PIECE, OUT_PIECE, FIELD_PIECE, FIELD_PIECE)
AF_BASE = (0, OUT_PIECE, 2 * OUT_PIECE, 2 * OUT_PIECE + FIELD_PIECE)
AF_TOTAL = sum(AF_ROWS)
GRAD = 3 * TAPS * MID
W_ROWS = 1792


def align(value, by=16):
    return pl.multiple_of(value, by)


def kernel(
    disp, cot, win, wout,
    full_ref, grads_ref,
    raw, D, C, H3, P3, W1T, W1, W2T, W2, AI, AO, DF, FS, EXTRA, B, R, WB, WR, QS, QR,
    land_core, land_out, land_field, land_w,
    load_sem, halo_s, halo_r, core_s, core_r, rs_s, rs_r, ag_s, ag_r, ws_s, ws_r, wg_s, wg_r, store_sem,
):
    gx = lax.axis_index("gx")
    af = lax.axis_index("af")
    core = lax.rem(af, 2)
    y = lax.rem(lax.div(af, 2), 4)
    xl = lax.div(af, 8)
    z = lax.rem(gx, 4)
    xh = lax.div(gx, 4)

    order = ((1, 2), (0, 2), (1, 1), (1, 3), (0, 1), (0, 3), (1, 0))
    af_peers, gx_peers = [], []
    for dx, dy in order:
        x2, y2 = lax.rem(xl + dx, 2), lax.rem(y + dy, 4)
        af_peers.append(((gx, (x2 * 4 + y2) * 2 + core), x2 * 4 + y2))
        x2, z2 = lax.rem(xh + dx, 2), lax.rem(z + dy, 4)
        gx_peers.append(((x2 * 4 + z2, af), x2 * 4 + z2))
    other_core = (gx, af + 1 - 2 * core)
    right = (lax.rem(gx + 1, 8), af)
    left = (lax.rem(gx + 7, 8), af)

    loads = [
        pltpu.make_async_copy(disp, raw, load_sem.at[0]),
        pltpu.make_async_copy(cot, C.at[pl.ds(1, SLAB), pl.ds(2, CY)], load_sem.at[1]),
    ]
    for load in loads:
        load.start()
    barrier = pltpu.get_barrier_semaphore()
    peers = [peer for peer, _ in af_peers + gx_peers] + [other_core, left, right]
    for peer in peers:
        pl.semaphore_signal(barrier, inc=1, device_id=peer, device_id_type=MESH)

    C[:, 0:2] = jnp.zeros((6, 2, CZ, LANES), BF)
    C[:, 18:20] = jnp.zeros((6, 2, CZ, LANES), BF)
    P3[:, 0:2] = jnp.zeros((6, 2, PITCH, LANES), BF)
    P3[:, 20:22] = jnp.zeros((6, 2, PITCH, LANES), BF)
    DF[SLAB * PLANE:, :] = jnp.zeros((SLAB * (PITCH - FZ), LANES), F32)

    loads[0].wait()
    line_row = lax.broadcasted_iota(jnp.int32, (PITCH, LANES), 0)

    def widen(i, _):
        rows = pl.ds(align(i * 4 * FZ * SLAB), 4 * FZ * SLAB)
        DF[rows, :] = raw[rows, :].astype(F32)
        return 0

    lax.fori_loop(0, FY // 4, widen, 0)

    def part(i, _):
        for x in range(SLAB):
            line = DF[pl.ds(i * FZ * SLAB + x, PITCH, stride=SLAB), :]
            D[x + 1, i] = jnp.where(line_row < FZ, line, 0.0).astype(BF)
        return 0

    lax.fori_loop(0, FY, part, 0)
    loads[1].wait()
    pl.semaphore_wait(barrier, len(peers))

    def halo(index, src, dst, peer):
        copy = pltpu.make_async_remote_copy(
            src_ref=src, dst_ref=dst, send_sem=halo_s.at[index], recv_sem=halo_r.at[index],
            device_id=peer, device_id_type=MESH,
        )
        copy.start()
        return copy

    halos = [
        halo(0, D.at[SLAB], D.at[0], right),
        halo(1, D.at[1], D.at[SLAB + 1], left),
        halo(2, C.at[SLAB, pl.ds(2, CY)], C.at[0, pl.ds(2, CY)], right),
        halo(3, C.at[1, pl.ds(2, CY)], C.at[SLAB + 1, pl.ds(2, CY)], left),
    ]

    zero_rows = jnp.zeros((LANES - 3 * MID, LANES), BF)
    for tap in range(TAPS):
        rows = pl.ds(tap * LANES, LANES)
        for src, straight, turned in ((win, W1, W1T), (wout, W2, W2T)):
            block = jnp.concatenate([src[tap], zero_rows], axis=0)
            straight[rows, :] = block
            turned[rows, :] = block.T
    AI[...] = jnp.zeros_like(AI)
    AO[...] = jnp.zeros_like(AO)
    WB[2 * GRAD:, :] = jnp.zeros((W_ROWS - 2 * GRAD, LANES), BF)
    FS[2 * PLANE:, :] = jnp.zeros((FIELD_PIECE - 2 * PLANE, LANES), F32)

    def lane_roll(values, count):
        count = count % LANES
        return pltpu.roll(values, count, 1) if count else values

    def row_roll(values, count):
        return pltpu.roll(values, count % values.shape[0], 0)

    def gather(values, direction):
        one = row_roll(lane_roll(values, -MID), -direction)
        two = row_roll(lane_roll(values, -2 * MID), -2 * direction)
        return values + one + two

    def spread(values, direction):
        one = row_roll(lane_roll(values, MID), -direction)
        two = row_roll(lane_roll(values, 2 * MID), -2 * direction)
        return values + one + two

    def first_mids(values):
        lane = lax.broadcasted_iota(jnp.int32, values.shape, 1)
        return jnp.where(lane < MID, values, 0.0)

    def stage_one(x):
        rows = HY * PITCH
        lhs = jnp.concatenate(
            [D[x + a, pl.ds(b, HY)].reshape(rows, LANES) for a in range(3) for b in range(3)], axis=1
        )
        pre = gather(jnp.dot(lhs, W1T[...], preferred_element_type=F32), 1)
        lhs = jnp.concatenate(
            [
                C[x + 2 - a, pl.ds(2 - b, HY)].reshape(HY * CZ, LANES)
                for a in range(3)
                for b in range(3)
            ],
            axis=1,
        )
        back = jnp.dot(lhs, W2T[...], preferred_element_type=F32).reshape(HY, CZ, LANES)
        back = jnp.concatenate([back, jnp.zeros((HY, PITCH - CZ, LANES), F32)], axis=1)
        grad = gather(back.reshape(rows, LANES), -1)
        square = pre * pre + 0.01
        inverse = lax.rsqrt(square)
        hidden = first_mids(0.505 * pre + 0.495 * (square * inverse))
        grad = first_mids(grad * (0.505 + 0.495 * (pre * inverse)))
        H3[x + 1] = spread(hidden, 1).reshape(HY, PITCH, LANES)[:, :CZ].astype(BF)
        P3[x + 1, pl.ds(2, HY)] = spread(grad, -1).reshape(HY, PITCH, LANES).astype(BF)
        return hidden, grad

    def inner_planes(i, _):
        stage_one(1 + i)
        return 0

    def outer_planes(i, _):
        hidden, grad = stage_one(3 * i)
        half = HALF * PITCH
        packed = hidden[:half] + lane_roll(hidden[half:], MID)
        packed = packed + lane_roll(grad[:half], 2 * MID) + lane_roll(grad[half:], 3 * MID)
        QS[i] = packed.astype(BF)
        return 0

    over_rows = (((0,), (0,)), ((), ()))

    def weight_terms(i):
        left_side = jnp.concatenate([H3[i + 1, pl.ds(b, CY)].reshape(CELLS, LANES) for b in range(3)], axis=1)
        right_side = jnp.concatenate(
            [C[i + 2 - a, pl.ds(2, CY)].reshape(CELLS, LANES) for a in range(3)], axis=1
        )
        AO[...] += lax.dot_general(left_side, right_side, over_rows, preferred_element_type=F32)
        left_side = jnp.concatenate(
            [P3[i + 1, pl.ds(2 - b, FY)].reshape(FY * PITCH, LANES) for b in range(3)], axis=1
        )
        right_side = jnp.concatenate([D[i + a].reshape(FY * PITCH, LANES) for a in range(3)], axis=1)
        AI[...] += lax.dot_general(left_side, right_side, over_rows, preferred_element_type=F32)

    def inner_weights(i, _):
        weight_terms(1 + i)
        return 0

    def outer_weights(i, _):
        weight_terms(3 * i)
        return 0

    lax.fori_loop(0, 2, inner_planes, 0)
    lax.fori_loop(0, 2, inner_weights, 0)
    for copy in halos[:4]:
        copy.wait_recv()
    lax.fori_loop(0, 2, outer_planes, 0)
    halos += [
        halo(4, QS.at[1], QR.at[0], right),
        halo(5, QS.at[0], QR.at[1], left),
    ]

    sends = []

    def send(src, dst, send_sem, recv_sem, peer):
        copy = pltpu.make_async_remote_copy(
            src_ref=src, dst_ref=dst, send_sem=send_sem, recv_sem=recv_sem, device_id=peer, device_id_type=MESH
        )
        copy.start()
        sends.append(copy)
        return copy

    def scatter(peers, piece, landing, size, sems):
        return [
            send(piece(align(place * size), size), landing(j), sems[0](j), sems[1](j), peer)
            for j, (peer, place) in enumerate(peers)
        ]

    def total(copies, piece, landing, me, size):
        for copy in copies:
            copy.wait_recv()
        value = piece(align(me * size), size)[...].astype(F32)
        for j in range(len(copies)):
            value = value + landing(j)[...].astype(F32)
        return value

    def spread_out(peers, whole, me, size, sems):
        rows = whole(align(me * size), size)
        return [send(rows, rows, sems[0](j), sems[1](j), peer) for j, (peer, _) in enumerate(peers)]

    class AfSum:
        def __init__(self, p):
            self.p, self.half, self.size = p, AF_ROWS[p] // 2, AF_ROWS[p] // 16
            self.base = AF_BASE[p] + core * self.half
            self.me = xl * 4 + y
            self.landing = (lambda j: land_out.at[p, j]) if p < 2 else (lambda j: land_field.at[p - 2, j])
            self.core_land = land_core.at[pl.ds(AF_BASE[p] // 2, self.half)]
            self.step = 0

        def piece(self, off, size):
            return B.at[pl.ds(align(self.base + off), size)]

        def whole(self, off, size):
            return R.at[pl.ds(align(self.base + off), size)]

        def advance(self):
            p, me, size = self.p, self.me, self.size
            if self.step == 0:
                give = B.at[pl.ds(align(AF_BASE[p] + (1 - core) * self.half), self.half)]
                self.copies = [send(give, self.core_land, core_s.at[p, 0], core_r.at[p, 0], other_core)]
            elif self.step == 1:
                self.copies[0].wait_recv()
                mine = self.piece(0, self.half)
                mine[...] = (mine[...].astype(F32) + self.core_land[...].astype(F32)).astype(BF)
                sems = (lambda j: rs_s.at[p, j], lambda j: rs_r.at[p, j])
                self.copies = scatter(af_peers, self.piece, self.landing, size, sems)
            elif self.step == 2:
                value = total(self.copies, self.piece, self.landing, me, size)
                value = value + EXTRA[pl.ds(align(self.base + me * size), size), :]
                self.whole(align(me * size), size)[...] = value.astype(BF)
                sems = (lambda j: ag_s.at[p, j], lambda j: ag_r.at[p, j])
                self.copies = spread_out(af_peers, self.whole, me, size, sems)
            elif self.step == 3:
                for copy in self.copies:
                    copy.wait_recv()
                rows = self.whole(0, self.half)
                self.copies = [send(rows, rows, core_s.at[p, 1], core_r.at[p, 1], other_core)]
            else:
                self.copies[0].wait_recv()
                rows = pl.ds(AF_BASE[p], AF_ROWS[p])
                store = pltpu.make_async_copy(R.at[rows], full_ref.at[rows], store_sem.at[p])
                store.start()
                stores.append(store)
            self.step += 1

    class GxSum:
        def __init__(self):
            self.me, self.size = xh * 4 + z, W_ROWS // 8
            self.step = 0

        def piece(self, off, size):
            return WB.at[pl.ds(off, size)]

        def whole(self, off, size):
            return WR.at[pl.ds(off, size)]

        def advance(self):
            me, size = self.me, self.size
            if self.step == 0:
                sems = (lambda j: ws_s.at[j], lambda j: ws_r.at[j])
                self.copies = scatter(gx_peers, self.piece, lambda j: land_w.at[j], size, sems)
            elif self.step == 1:
                value = total(self.copies, self.piece, lambda j: land_w.at[j], me, size)
                self.whole(align(me * size), size)[...] = value.astype(BF)
                sems = (lambda j: wg_s.at[j], lambda j: wg_r.at[j])
                self.copies = spread_out(gx_peers, self.whole, me, size, sems)
            else:
                for copy in self.copies:
                    copy.wait_recv()
                store = pltpu.make_async_copy(WR, grads_ref, store_sem.at[4])
                store.start()
                stores.append(store)
            self.step += 1

    stores = []
    out_a, out_b, field_a, field_b = [AfSum(p) for p in range(4)]
    grads = GxSum()

    lax.fori_loop(0, 2, outer_weights, 0)
    for acc, base in ((AI, 0), (AO, GRAD)):
        for a in range(3):
            for b in range(3):
                WB[pl.ds(base + (a * 3 + b) * 3 * MID, 3 * MID), :] = acc[
                    b * LANES : b * LANES + 3 * MID, a * LANES : (a + 1) * LANES
                ].astype(BF)
    grads.advance()

    def out_plane(slot):
        i = ORDER[slot]
        lhs = jnp.concatenate(
            [H3[i + a, pl.ds(b, CY)].reshape(CELLS, LANES) for a in range(3) for b in range(3)], axis=1
        )
        B[pl.ds(slot * CELLS, CELLS), :] = jnp.dot(lhs, W2[...], preferred_element_type=F32).astype(BF)

    def field_plane(slot):
        i = ORDER[slot]
        lhs = jnp.concatenate(
            [
                P3[i + 2 - a, pl.ds(2 - b, FY)].reshape(FY * PITCH, LANES)
                for a in range(3)
                for b in range(3)
            ],
            axis=1,
        )
        block = jnp.dot(lhs, W1[...], preferred_element_type=F32).reshape(FY, PITCH, LANES)
        for line in range(FY):
            FS[pl.ds((slot % 2) * PLANE + line * FZ, FZ), :] = block[line, :FZ]

    def field_rows(p):
        B[pl.ds(AF_BASE[p], FIELD_PIECE), :] = FS[...].astype(BF)

    def extra_out(i, _):
        for slot in range(SLAB):
            EXTRA[pl.ds(align(slot * CELLS + i * CZ), CZ), :] = DF[
                pl.ds((i + 2) * FZ * SLAB + 2 * SLAB + ORDER[slot], CZ, stride=SLAB), :
            ]
        return 0

    def extra_field():
        EXTRA[2 * OUT_PIECE:, :] = jnp.zeros((2 * FIELD_PIECE, LANES), F32)
        for slot in range(SLAB):
            base = 2 * OUT_PIECE + (slot // 2) * FIELD_PIECE + (slot % 2) * PLANE
            for line in range(CY):
                EXTRA[pl.ds(base + (line + 2) * FZ + 2, CZ), :] = C[ORDER[slot] + 1, line + 2].astype(F32)

    out_plane(0)
    out_plane(1)
    out_a.advance()
    field_plane(0)
    out_a.advance()
    field_plane(1)
    field_rows(2)
    field_a.advance()
    lax.fori_loop(0, CY, extra_out, 0)
    extra_field()
    field_a.advance()

    for copy in halos[4:6]:
        copy.wait_recv()

    def unpack(i, _):
        packed = QR[i].astype(F32)
        for r in range(2):
            hidden = first_mids(lane_roll(packed, -r * MID))
            grad = first_mids(lane_roll(packed, -(2 + r) * MID))
            hidden = spread(hidden, 1).reshape(HALF, PITCH, LANES)[:, :CZ]
            H3[5 * i, pl.ds(r * HALF, HALF)] = hidden.astype(BF)
            grad = spread(grad, -1).reshape(HALF, PITCH, LANES)
            P3[5 * i, pl.ds(2 + r * HALF, HALF)] = grad.astype(BF)
        return 0

    lax.fori_loop(0, 2, unpack, 0)
    out_plane(2)
    out_plane(3)
    out_b.advance()
    out_a.advance()
    field_plane(2)
    out_b.advance()
    field_a.advance()
    field_plane(3)
    field_rows(3)
    field_b.advance()
    grads.advance()
    field_b.advance()
    out_b.advance()
    out_a.advance()
    field_a.advance()
    field_b.advance()
    out_b.advance()
    grads.advance()
    out_a.advance()
    field_a.advance()
    out_b.advance()
    field_b.advance()
    field_b.advance()
    for store in stores:
        store.wait()
    for copy in halos + sends:
        copy.wait_send()


def finish(full, grads, out_ref, field_ref, inner_ref, outer_ref, f_in, g_in, f_out, w_out, in_sem, out_sem):
    lines = 4
    steps = FY // lines
    rows = lines * FZ

    def source(step, slot):
        base = 2 * OUT_PIECE + (slot // 2) * FIELD_PIECE + (slot % 2) * PLANE
        return pltpu.make_async_copy(
            full.at[pl.ds(base + step * rows, rows)], f_in.at[step, slot], in_sem.at[step, slot]
        )

    inputs = [[source(step, slot) for slot in range(SLAB)] for step in range(steps)]
    whole = pltpu.make_async_copy(grads, g_in, in_sem.at[steps, 0])
    for copies in inputs:
        for copy in copies:
            copy.start()
    whole.start()
    stores = []

    def store(src, dst):
        copy = pltpu.make_async_copy(src, dst, out_sem.at[len(stores)])
        copy.start()
        stores.append(copy)

    for slot in range(SLAB):
        store(full.at[pl.ds(slot * CELLS, CELLS)], out_ref.at[pl.ds(ORDER[slot] * CELLS, CELLS)])
    for step in range(steps):
        for slot in range(SLAB):
            inputs[step][slot].wait()
            f_out[pl.ds(step * rows * SLAB + ORDER[slot], rows, stride=SLAB), :] = f_in[step, slot].astype(F32)
        part = pl.ds(step * rows * SLAB, rows * SLAB)
        store(f_out.at[part], field_ref.at[part])
    whole.wait()
    for p, ref in enumerate((inner_ref, outer_ref)):
        part = pl.ds(p * GRAD, GRAD)
        w_out[part, :] = g_in[part, :].astype(F32)
        store(w_out.at[part], ref)
    for copy in stores:
        copy.wait()


def shards(displace, weight_in, weight_out, cotangent):
    vmem = pl.BlockSpec(memory_space=pltpu.VMEM)
    hbm = pl.BlockSpec(memory_space=pl.ANY)
    rows = jnp.transpose(displace, (1, 2, 0, 3)).reshape(SLAB * PLANE, LANES)
    win = jnp.transpose(weight_in, (0, 1, 2, 4, 3)).reshape(TAPS, 3 * MID, LANES)
    wout = weight_out.reshape(TAPS, 3 * MID, LANES)
    dma = pltpu.SemaphoreType.DMA
    full, grads = pl.pallas_call(
        kernel,
        out_shape=(
            jax.ShapeDtypeStruct((AF_TOTAL, LANES), BF),
            jax.ShapeDtypeStruct((W_ROWS, LANES), BF),
        ),
        in_specs=[hbm, hbm, vmem, vmem],
        out_specs=[hbm] * 2,
        scratch_shapes=[
            pltpu.VMEM((SLAB * PLANE, LANES), BF),
            pltpu.VMEM((SLAB + 2, FY, PITCH, LANES), BF),
            pltpu.VMEM((SLAB + 2, FY, CZ, LANES), BF),
            pltpu.VMEM((SLAB + 2, HY, CZ, LANES), BF),
            pltpu.VMEM((SLAB + 2, HY + 4, PITCH, LANES), BF),
            pltpu.VMEM((TAPS * LANES, LANES), BF),
            pltpu.VMEM((TAPS * LANES, LANES), BF),
            pltpu.VMEM((TAPS * LANES, LANES), BF),
            pltpu.VMEM((TAPS * LANES, LANES), BF),
            pltpu.VMEM((3 * LANES, 3 * LANES), F32),
            pltpu.VMEM((3 * LANES, 3 * LANES), F32),
            pltpu.VMEM((SLAB * (PLANE + PITCH - FZ), LANES), F32),
            pltpu.VMEM((FIELD_PIECE, LANES), F32),
            pltpu.VMEM((AF_TOTAL, LANES), F32),
            pltpu.VMEM((AF_TOTAL, LANES), BF),
            pltpu.VMEM((AF_TOTAL, LANES), BF),
            pltpu.VMEM((W_ROWS, LANES), BF),
            pltpu.VMEM((W_ROWS, LANES), BF),
            pltpu.VMEM((2, HALF * PITCH, LANES), BF),
            pltpu.VMEM((2, HALF * PITCH, LANES), BF),
            pltpu.VMEM((AF_TOTAL // 2, LANES), BF),
            pltpu.VMEM((2, 7, OUT_PIECE // 16, LANES), BF),
            pltpu.VMEM((2, 7, FIELD_PIECE // 16, LANES), BF),
            pltpu.VMEM((7, W_ROWS // 8, LANES), BF),
            dma((2,)), dma((6,)), dma((6,)),
            dma((4, 2)), dma((4, 2)), dma((4, 7)), dma((4, 7)), dma((4, 7)), dma((4, 7)),
            dma((7,)), dma((7,)), dma((7,)), dma((7,)), dma((5,)),
        ],
        compiler_params=pltpu.CompilerParams(
            collective_id=0, has_side_effects=True, vmem_limit_bytes=48 * 1024 * 1024
        ),
        cost_estimate=pl.CostEstimate(flops=4_000_000_000, bytes_accessed=8_000_000, transcendentals=400_000),
    )(rows, cotangent, win, wout)
    out, field, inner, outer = pl.pallas_call(
        finish,
        out_shape=(
            jax.ShapeDtypeStruct((SLAB * CELLS, LANES), BF),
            jax.ShapeDtypeStruct((SLAB * PLANE, LANES), F32),
            jax.ShapeDtypeStruct((GRAD, LANES), F32),
            jax.ShapeDtypeStruct((GRAD, LANES), F32),
        ),
        in_specs=[hbm] * 2,
        out_specs=[hbm] * 4,
        scratch_shapes=[
            pltpu.VMEM((5, SLAB, 4 * FZ, LANES), BF),
            pltpu.VMEM((W_ROWS, LANES), BF),
            pltpu.VMEM((SLAB * PLANE, LANES), F32),
            pltpu.VMEM((2 * GRAD, LANES), F32),
            dma((6, SLAB)), dma((11,)),
        ],
        compiler_params=pltpu.CompilerParams(vmem_limit_bytes=16 * 1024 * 1024),
        cost_estimate=pl.CostEstimate(flops=0, bytes_accessed=5_000_000, transcendentals=0),
    )(full, grads)
    out_field = out.reshape(SLAB, CY, CZ, LANES)
    field_grad = jnp.transpose(field.reshape(FY, FZ, SLAB, LANES), (2, 0, 1, 3))
    inner_grad = jnp.transpose(inner.reshape(3, 3, 3, MID, LANES), (0, 1, 2, 4, 3))
    outer_grad = outer.reshape(3, 3, 3, MID, LANES)
    return (out_field, field_grad, inner_grad, outer_grad)


def solution(mesh):
    return jax.shard_map(
        shards,
        mesh=mesh,
        in_specs=(
            P("gx", None, None, None),
            P(None, None, None, None, "af"),
            P(None, None, None, "af", None),
            P("gx", None, None, None),
        ),
        out_specs=(
            P("gx", None, None, None),
            P("gx", None, None, None),
            P(None, None, None, None, "af"),
            P(None, None, None, "af", None),
        ),
        check_vma=False,
    )
```

```python
import jax
import jax.numpy as jnp
from jax import lax
from jax.experimental import pallas as pl
from jax.experimental.pallas import tpu as pltpu
from jax.sharding import PartitionSpec as P

MESH = pl.DeviceIdType.MESH
BF = jnp.bfloat16
F32 = jnp.float32

SLAB = 4
CY, CZ = 16, 32
PITCH = 48
LANES = 128
MID = 32
TAPS = 9
HY, HALF = 18, 9
FY, FZ = 20, 36
PLANE = FY * FZ
CELLS = CY * CZ
ORDER = (1, 2, 0, 3)

OUT_PIECE = 2 * CELLS
FIELD_SLOT = 768
FIELD_BASE = 2 * OUT_PIECE
AF_ROWS = (OUT_PIECE, OUT_PIECE, 2 * FIELD_SLOT, FIELD_SLOT, FIELD_SLOT)
AF_BASE = tuple(sum(AF_ROWS[:p]) for p in range(5))
AF_TOTAL = sum(AF_ROWS)
AF_LAND = tuple(7 * base // 16 for base in AF_BASE)
HALO = 368
GRAD = 3 * TAPS * MID
W_ROWS = 1792
W_PART = W_ROWS // 4


def align(value, by=16):
    return pl.multiple_of(value, by)


def kernel(
    disp, cot, win, wout,
    full_ref, grads_ref,
    raw, D, C, H3, P3, W1T, W1, W2T, W2, AI, AO, DF, FS, EXTRA, B, R, WB, WZ, WR, QS, QR, HS, HL, HF,
    land_core, land_af, land_z, land_x,
    load_sem, halo_s, halo_r, core_s, core_r, rs_s, rs_r, ag_s, ag_r, ws_s, ws_r, wx_s, wx_r, wg_s, wg_r, store_sem,
):
    gx = lax.axis_index("gx")
    af = lax.axis_index("af")
    core = lax.rem(af, 2)
    y = lax.rem(lax.div(af, 2), 4)
    xl = lax.div(af, 8)
    z = lax.rem(gx, 4)
    xh = lax.div(gx, 4)

    af_peers, z_peers = [], []
    for dx, dy in ((1, 2), (0, 2), (1, 1), (1, 3), (0, 1), (0, 3), (1, 0)):
        x2, y2 = lax.rem(xl + dx, 2), lax.rem(y + dy, 4)
        af_peers.append(((gx, (x2 * 4 + y2) * 2 + core), x2 * 4 + y2))
    for dz in (2, 1, 3):
        z2 = lax.rem(z + dz, 4)
        z_peers.append(((xh * 4 + z2, af), z2))
    x_peer = ((1 - xh) * 4 + z, af)
    other_core = (gx, af + 1 - 2 * core)
    right = (lax.rem(gx + 1, 8), af)
    left = (lax.rem(gx + 7, 8), af)

    loads = [
        pltpu.make_async_copy(disp, raw, load_sem.at[0]),
        pltpu.make_async_copy(cot, C.at[pl.ds(1, SLAB), pl.ds(2, CY)], load_sem.at[1]),
        pltpu.make_async_copy(win, W1.at[:, pl.ds(0, 3 * MID)], load_sem.at[2]),
        pltpu.make_async_copy(wout, W2.at[:, pl.ds(0, 3 * MID)], load_sem.at[3]),
    ]
    for load in loads:
        load.start()
    barrier = pltpu.get_barrier_semaphore()
    peers = [peer for peer, _ in af_peers + z_peers] + [x_peer, other_core, left, right]
    for peer in peers:
        pl.semaphore_signal(barrier, inc=1, device_id=peer, device_id_type=MESH)

    C[:, 0:2] = jnp.zeros((6, 2, CZ, LANES), BF)
    C[:, 18:20] = jnp.zeros((6, 2, CZ, LANES), BF)
    P3[:, 0:2] = jnp.zeros((6, 2, PITCH, LANES), BF)
    P3[:, 20:22] = jnp.zeros((6, 2, PITCH, LANES), BF)
    DF[SLAB * PLANE:, :] = jnp.zeros((SLAB * (PITCH - FZ), LANES), F32)
    HF[PLANE:, :] = jnp.zeros((16, LANES), F32)
    zero_rows = jnp.zeros((TAPS, LANES - 3 * MID, LANES), BF)
    W1[:, 3 * MID:] = zero_rows
    W2[:, 3 * MID:] = zero_rows
    AI[...] = jnp.zeros_like(AI)
    AO[...] = jnp.zeros_like(AO)
    WB[2 * GRAD:, :] = jnp.zeros((W_ROWS - 2 * GRAD, LANES), BF)
    FS[2 * PLANE:, :] = jnp.zeros((2 * FIELD_SLOT - 2 * PLANE, LANES), F32)

    loads[0].wait()
    line_row = lax.broadcasted_iota(jnp.int32, (PITCH, LANES), 0)

    def widen(i, _):
        rows = pl.ds(align(i * 4 * FZ * SLAB), 4 * FZ * SLAB)
        DF[rows, :] = raw[rows, :].astype(F32)
        return 0

    lax.fori_loop(0, FY // 4, widen, 0)
    for side, x in enumerate((0, SLAB - 1)):
        HS[side] = DF[pl.ds(x, PLANE, stride=SLAB), :].astype(BF)

    def part(i, _):
        for x in range(SLAB):
            line = DF[pl.ds(i * FZ * SLAB + x, PITCH, stride=SLAB), :]
            D[x + 1, i] = jnp.where(line_row < FZ, line, 0.0).astype(BF)
        return 0

    lax.fori_loop(0, FY, part, 0)
    for load in loads[1:]:
        load.wait()
    for straight, turned in ((W1, W1T), (W2, W2T)):
        for tap in range(TAPS):
            turned[pl.ds(tap * LANES, LANES), :] = straight[tap].T

    def lane_roll(values, count):
        count = count % LANES
        return pltpu.roll(values, count, 1) if count else values

    def row_roll(values, count):
        return pltpu.roll(values, count % values.shape[0], 0)

    def gather(values, direction):
        one = row_roll(lane_roll(values, -MID), -direction)
        two = row_roll(lane_roll(values, -2 * MID), -2 * direction)
        return values + one + two

    def spread(values, direction):
        one = row_roll(lane_roll(values, MID), -direction)
        two = row_roll(lane_roll(values, 2 * MID), -2 * direction)
        return values + one + two

    def first_mids(values):
        lane = lax.broadcasted_iota(jnp.int32, values.shape, 1)
        return jnp.where(lane < MID, values, 0.0)

    def stage_one(x):
        rows = HY * PITCH
        lhs = jnp.concatenate(
            [D[x + a, pl.ds(b, HY)].reshape(rows, LANES) for a in range(3) for b in range(3)], axis=1
        )
        pre = gather(jnp.dot(lhs, W1T[...], preferred_element_type=F32), 1)
        lhs = jnp.concatenate(
            [
                C[x + 2 - a, pl.ds(2 - b, HY)].reshape(HY * CZ, LANES)
                for a in range(3)
                for b in range(3)
            ],
            axis=1,
        )
        back = jnp.dot(lhs, W2T[...], preferred_element_type=F32).reshape(HY, CZ, LANES)
        back = jnp.concatenate([back, jnp.zeros((HY, PITCH - CZ, LANES), F32)], axis=1)
        grad = gather(back.reshape(rows, LANES), -1)
        square = pre * pre + 0.01
        inverse = lax.rsqrt(square)
        hidden = first_mids(0.505 * pre + 0.495 * (square * inverse))
        grad = first_mids(grad * (0.505 + 0.495 * (pre * inverse)))
        H3[x + 1] = spread(hidden, 1).reshape(HY, PITCH, LANES)[:, :CZ].astype(BF)
        P3[x + 1, pl.ds(2, HY)] = spread(grad, -1).reshape(HY, PITCH, LANES).astype(BF)
        return hidden, grad

    def outer_plane(i):
        hidden, grad = stage_one(3 * i)
        half = HALF * PITCH
        packed = hidden[:half] + lane_roll(hidden[half:], MID)
        packed = packed + lane_roll(grad[:half], 2 * MID) + lane_roll(grad[half:], 3 * MID)
        QS[i] = packed.astype(BF)

    over_rows = (((0,), (0,)), ((), ()))

    def weight_terms(i):
        left_side = jnp.concatenate([H3[i + 1, pl.ds(b, CY)].reshape(CELLS, LANES) for b in range(3)], axis=1)
        right_side = jnp.concatenate(
            [C[i + 2 - a, pl.ds(2, CY)].reshape(CELLS, LANES) for a in range(3)], axis=1
        )
        AO[...] += lax.dot_general(left_side, right_side, over_rows, preferred_element_type=F32)
        left_side = jnp.concatenate(
            [P3[i + 1, pl.ds(2 - b, FY)].reshape(FY * PITCH, LANES) for b in range(3)], axis=1
        )
        right_side = jnp.concatenate([D[i + a].reshape(FY * PITCH, LANES) for a in range(3)], axis=1)
        AI[...] += lax.dot_general(left_side, right_side, over_rows, preferred_element_type=F32)

    def inner_weights(i, _):
        weight_terms(1 + i)
        return 0

    def outer_weights(i, _):
        weight_terms(3 * i)
        return 0

    def halo(index, src, dst, peer):
        copy = pltpu.make_async_remote_copy(
            src_ref=src, dst_ref=dst, send_sem=halo_s.at[index], recv_sem=halo_r.at[index],
            device_id=peer, device_id_type=MESH,
        )
        copy.start()
        halos.append(copy)
        return copy

    halos = []
    mine = pl.ds(align(core * 352), HALO)
    my_lines = pl.ds(2 + core * (CY // 2), CY // 2)
    stage_one(1)
    pl.semaphore_wait(barrier, len(peers))
    first_halos = [
        halo(0, HS.at[1, mine], HL.at[0, core], right),
        halo(1, HS.at[0, mine], HL.at[1, core], left),
        halo(2, C.at[SLAB, my_lines], C.at[0, my_lines], right),
        halo(3, C.at[1, my_lines], C.at[SLAB + 1, my_lines], left),
    ]
    stage_one(2)
    lax.fori_loop(0, 2, inner_weights, 0)
    shares = []
    for side in range(2):
        first_halos[side].wait_recv()
        shares.append(halo(4 + side, HL.at[side, core], HL.at[side, core], other_core))
    for side in range(2):
        first_halos[2 + side].wait_recv()
        rows = C.at[side * (SLAB + 1), my_lines]
        shares.append(halo(6 + side, rows, rows, other_core))
    for side in range(2):
        shares[side].wait_recv()
        HF[0:HALO, :] = HL[side, 0].astype(F32)
        HF[PLANE - HALO : PLANE, :] = HL[side, 1].astype(F32)
        for line in range(FY):
            value = HF[pl.ds(line * FZ, PITCH), :]
            D[side * (SLAB + 1), line] = jnp.where(line_row < FZ, value, 0.0).astype(BF)
    for side in range(2):
        shares[2 + side].wait_recv()
    outer_plane(0)
    second_halos = [halo(8, QS.at[0], QR.at[1], left)]
    outer_plane(1)
    second_halos.append(halo(9, QS.at[1], QR.at[0], right))

    sends = []

    def send(src, dst, send_sem, recv_sem, peer):
        copy = pltpu.make_async_remote_copy(
            src_ref=src, dst_ref=dst, send_sem=send_sem, recv_sem=recv_sem, device_id=peer, device_id_type=MESH
        )
        copy.start()
        sends.append(copy)
        return copy

    def scatter(peers, piece, landing, size, sems):
        return [
            send(piece(align(place * size), size), landing(j), sems[0](j), sems[1](j), peer)
            for j, (peer, place) in enumerate(peers)
        ]

    def total(copies, piece, landing, me, size):
        for copy in copies:
            copy.wait_recv()
        value = piece(align(me * size), size)[...].astype(F32)
        for j in range(len(copies)):
            value = value + landing(j)[...].astype(F32)
        return value

    def spread_out(peers, whole, me, size, sems):
        rows = whole(align(me * size), size)
        return [send(rows, rows, sems[0](j), sems[1](j), peer) for j, (peer, _) in enumerate(peers)]

    class AfSum:
        def __init__(self, p):
            self.p, self.half, self.size = p, AF_ROWS[p] // 2, AF_ROWS[p] // 16
            self.base = AF_BASE[p] + core * self.half
            self.me = xl * 4 + y
            self.landing = lambda j: land_af.at[pl.ds(AF_LAND[p] + j * self.size, self.size)]
            self.core_land = land_core.at[pl.ds(AF_BASE[p] // 2, self.half)]
            self.step = 0

        def piece(self, off, size):
            return B.at[pl.ds(align(self.base + off), size)]

        def whole(self, off, size):
            return R.at[pl.ds(align(self.base + off), size)]

        def advance(self):
            p, me, size = self.p, self.me, self.size
            if self.step == 0:
                give = B.at[pl.ds(align(AF_BASE[p] + (1 - core) * self.half), self.half)]
                self.copies = [send(give, self.core_land, core_s.at[p, 0], core_r.at[p, 0], other_core)]
            elif self.step == 1:
                self.copies[0].wait_recv()
                mine = self.piece(0, self.half)
                mine[...] = (mine[...].astype(F32) + self.core_land[...].astype(F32)).astype(BF)
                sems = (lambda j: rs_s.at[p, j], lambda j: rs_r.at[p, j])
                self.copies = scatter(af_peers, self.piece, self.landing, size, sems)
            elif self.step == 2:
                value = total(self.copies, self.piece, self.landing, me, size)
                value = value + EXTRA[pl.ds(align(self.base + me * size), size), :]
                self.whole(align(me * size), size)[...] = value.astype(BF)
                sems = (lambda j: ag_s.at[p, j], lambda j: ag_r.at[p, j])
                self.copies = spread_out(af_peers, self.whole, me, size, sems)
            elif self.step == 3:
                for copy in self.copies:
                    copy.wait_recv()
                rows = self.whole(0, self.half)
                self.copies = [send(rows, rows, core_s.at[p, 1], core_r.at[p, 1], other_core)]
            else:
                self.copies[0].wait_recv()
                rows = pl.ds(AF_BASE[p], AF_ROWS[p])
                store = pltpu.make_async_copy(R.at[rows], full_ref.at[rows], store_sem.at[p])
                store.start()
                stores.append(store)
            self.step += 1

    class GxSum:
        def __init__(self):
            self.step = 0

        def piece(self, off, size):
            return WB.at[pl.ds(off, size)]

        def whole(self, off, size):
            return WR.at[pl.ds(off, size)]

        def advance(self):
            if self.step == 0:
                sems = (lambda j: ws_s.at[j], lambda j: ws_r.at[j])
                self.copies = scatter(z_peers, self.piece, lambda j: land_z.at[j], W_PART, sems)
            elif self.step == 1:
                WZ[...] = total(self.copies, self.piece, lambda j: land_z.at[j], z, W_PART).astype(BF)
                self.copies = [send(WZ, land_x, wx_s.at[0], wx_r.at[0], x_peer)]
            elif self.step == 2:
                self.copies[0].wait_recv()
                value = WZ[...].astype(F32) + land_x[...].astype(F32)
                self.whole(align(z * W_PART), W_PART)[...] = value.astype(BF)
                sems = (lambda j: wg_s.at[j], lambda j: wg_r.at[j])
                self.copies = spread_out(z_peers, self.whole, z, W_PART, sems)
            else:
                for copy in self.copies:
                    copy.wait_recv()
                store = pltpu.make_async_copy(WR, grads_ref, store_sem.at[5])
                store.start()
                stores.append(store)
            self.step += 1

    stores = []
    out_a, out_b, field_a, field_b, field_c = [AfSum(p) for p in range(5)]
    grads = GxSum()

    lax.fori_loop(0, 2, outer_weights, 0)
    for acc, base in ((AI, 0), (AO, GRAD)):
        for a in range(3):
            for b in range(3):
                WB[pl.ds(base + (a * 3 + b) * 3 * MID, 3 * MID), :] = acc[
                    b * LANES : b * LANES + 3 * MID, a * LANES : (a + 1) * LANES
                ].astype(BF)
    grads.advance()

    def out_plane(slot):
        i = ORDER[slot]
        lhs = jnp.concatenate(
            [H3[i + a, pl.ds(b, CY)].reshape(CELLS, LANES) for a in range(3) for b in range(3)], axis=1
        )
        weights = W2[...].reshape(TAPS * LANES, LANES)
        B[pl.ds(slot * CELLS, CELLS), :] = jnp.dot(lhs, weights, preferred_element_type=F32).astype(BF)

    def field_plane(slot):
        i = ORDER[slot]
        lhs = jnp.concatenate(
            [
                P3[i + 2 - a, pl.ds(2 - b, FY)].reshape(FY * PITCH, LANES)
                for a in range(3)
                for b in range(3)
            ],
            axis=1,
        )
        weights = W1[...].reshape(TAPS * LANES, LANES)
        block = jnp.dot(lhs, weights, preferred_element_type=F32).reshape(FY, PITCH, LANES)
        base = (slot % 2) * FIELD_SLOT
        for line in range(FY):
            FS[pl.ds(base + line * FZ, FZ), :] = block[line, :FZ]
        B[pl.ds(FIELD_BASE + slot * FIELD_SLOT, FIELD_SLOT), :] = FS[pl.ds(base, FIELD_SLOT), :].astype(BF)

    def extra_out(i, _):
        for slot in range(SLAB):
            EXTRA[pl.ds(align(slot * CELLS + i * CZ), CZ), :] = DF[
                pl.ds((i + 2) * FZ * SLAB + 2 * SLAB + ORDER[slot], CZ, stride=SLAB), :
            ]
        return 0

    def extra_field():
        EXTRA[FIELD_BASE:, :] = jnp.zeros((SLAB * FIELD_SLOT, LANES), F32)
        for slot in range(SLAB):
            base = FIELD_BASE + slot * FIELD_SLOT
            for line in range(CY):
                EXTRA[pl.ds(base + (line + 2) * FZ + 2, CZ), :] = C[ORDER[slot] + 1, line + 2].astype(F32)

    out_plane(0)
    out_plane(1)
    out_a.advance()
    field_plane(0)
    out_a.advance()
    field_plane(1)
    field_a.advance()
    lax.fori_loop(0, CY, extra_out, 0)
    extra_field()
    field_a.advance()

    for copy in second_halos:
        copy.wait_recv()

    def unpack(i, _):
        packed = QR[i].astype(F32)
        for r in range(2):
            hidden = first_mids(lane_roll(packed, -r * MID))
            grad = first_mids(lane_roll(packed, -(2 + r) * MID))
            hidden = spread(hidden, 1).reshape(HALF, PITCH, LANES)[:, :CZ]
            H3[5 * i, pl.ds(r * HALF, HALF)] = hidden.astype(BF)
            grad = spread(grad, -1).reshape(HALF, PITCH, LANES)
            P3[5 * i, pl.ds(2 + r * HALF, HALF)] = grad.astype(BF)
        return 0

    lax.fori_loop(0, 2, unpack, 0)
    out_plane(2)
    out_plane(3)
    out_b.advance()
    field_plane(2)
    field_b.advance()
    out_b.advance()
    field_plane(3)
    field_c.advance()
    field_b.advance()
    field_c.advance()
    out_a.advance()
    grads.advance()
    field_a.advance()
    out_b.advance()
    field_b.advance()
    field_c.advance()
    grads.advance()
    out_a.advance()
    field_a.advance()
    out_b.advance()
    out_a.advance()
    field_a.advance()
    field_b.advance()
    out_b.advance()
    field_c.advance()
    grads.advance()
    field_b.advance()
    field_c.advance()
    for store in stores:
        store.wait()
    for copy in halos + sends:
        copy.wait_send()


def finish(full, grads, out_ref, field_ref, inner_ref, outer_ref, f_in, g_in, f_out, w_out, in_sem, out_sem):
    lines = 4
    steps = FY // lines
    rows = lines * FZ

    def source(step, slot):
        base = FIELD_BASE + slot * FIELD_SLOT
        return pltpu.make_async_copy(
            full.at[pl.ds(base + step * rows, rows)], f_in.at[step, slot], in_sem.at[step, slot]
        )

    inputs = [[source(step, slot) for slot in range(SLAB)] for step in range(steps)]
    whole = pltpu.make_async_copy(grads, g_in, in_sem.at[steps, 0])
    for copies in inputs:
        for copy in copies:
            copy.start()
    whole.start()
    stores = []

    def store(src, dst):
        copy = pltpu.make_async_copy(src, dst, out_sem.at[len(stores)])
        copy.start()
        stores.append(copy)

    for slot in range(SLAB):
        store(full.at[pl.ds(slot * CELLS, CELLS)], out_ref.at[pl.ds(ORDER[slot] * CELLS, CELLS)])
    for step in range(steps):
        for slot in range(SLAB):
            inputs[step][slot].wait()
            f_out[pl.ds(step * rows * SLAB + ORDER[slot], rows, stride=SLAB), :] = f_in[step, slot].astype(F32)
        part = pl.ds(step * rows * SLAB, rows * SLAB)
        store(f_out.at[part], field_ref.at[part])
    whole.wait()
    for p, ref in enumerate((inner_ref, outer_ref)):
        part = pl.ds(p * GRAD, GRAD)
        w_out[part, :] = g_in[part, :].astype(F32)
        store(w_out.at[part], ref)
    for copy in stores:
        copy.wait()


def shards(displace, weight_in, weight_out, cotangent):
    hbm = pl.BlockSpec(memory_space=pl.ANY)
    rows = jnp.transpose(displace, (1, 2, 0, 3)).reshape(SLAB * PLANE, LANES)
    win = jnp.transpose(weight_in, (0, 1, 2, 4, 3)).reshape(TAPS, 3 * MID, LANES)
    wout = weight_out.reshape(TAPS, 3 * MID, LANES)
    dma = pltpu.SemaphoreType.DMA
    full, grads = pl.pallas_call(
        kernel,
        out_shape=(
            jax.ShapeDtypeStruct((AF_TOTAL, LANES), BF),
            jax.ShapeDtypeStruct((W_ROWS, LANES), BF),
        ),
        in_specs=[pl.BlockSpec(memory_space=pltpu.HBM)] * 4,
        out_specs=[hbm] * 2,
        scratch_shapes=[
            pltpu.VMEM((SLAB * PLANE, LANES), BF),
            pltpu.VMEM((SLAB + 2, FY, PITCH, LANES), BF),
            pltpu.VMEM((SLAB + 2, FY, CZ, LANES), BF),
            pltpu.VMEM((SLAB + 2, HY, CZ, LANES), BF),
            pltpu.VMEM((SLAB + 2, HY + 4, PITCH, LANES), BF),
            pltpu.VMEM((TAPS * LANES, LANES), BF),
            pltpu.VMEM((TAPS, LANES, LANES), BF),
            pltpu.VMEM((TAPS * LANES, LANES), BF),
            pltpu.VMEM((TAPS, LANES, LANES), BF),
            pltpu.VMEM((3 * LANES, 3 * LANES), F32),
            pltpu.VMEM((3 * LANES, 3 * LANES), F32),
            pltpu.VMEM((SLAB * (PLANE + PITCH - FZ), LANES), F32),
            pltpu.VMEM((2 * FIELD_SLOT, LANES), F32),
            pltpu.VMEM((AF_TOTAL, LANES), F32),
            pltpu.VMEM((AF_TOTAL, LANES), BF),
            pltpu.VMEM((AF_TOTAL, LANES), BF),
            pltpu.VMEM((W_ROWS, LANES), BF),
            pltpu.VMEM((W_PART, LANES), BF),
            pltpu.VMEM((W_ROWS, LANES), BF),
            pltpu.VMEM((2, HALF * PITCH, LANES), BF),
            pltpu.VMEM((2, HALF * PITCH, LANES), BF),
            pltpu.VMEM((2, PLANE, LANES), BF),
            pltpu.VMEM((2, 2, HALO, LANES), BF),
            pltpu.VMEM((PLANE + 16, LANES), F32),
            pltpu.VMEM((AF_TOTAL // 2, LANES), BF),
            pltpu.VMEM((7 * AF_TOTAL // 16, LANES), BF),
            pltpu.VMEM((3, W_PART, LANES), BF),
            pltpu.VMEM((W_PART, LANES), BF),
            dma((4,)), dma((10,)), dma((10,)),
            dma((5, 2)), dma((5, 2)), dma((5, 7)), dma((5, 7)), dma((5, 7)), dma((5, 7)),
            dma((3,)), dma((3,)), dma((1,)), dma((1,)), dma((3,)), dma((3,)), dma((6,)),
        ],
        compiler_params=pltpu.CompilerParams(
            collective_id=0, has_side_effects=True, vmem_limit_bytes=56 * 1024 * 1024
        ),
        cost_estimate=pl.CostEstimate(flops=4_000_000_000, bytes_accessed=8_000_000, transcendentals=400_000),
    )(rows, cotangent, win, wout)
    out, field, inner, outer = pl.pallas_call(
        finish,
        out_shape=(
            jax.ShapeDtypeStruct((SLAB * CELLS, LANES), BF),
            jax.ShapeDtypeStruct((SLAB * PLANE, LANES), F32),
            jax.ShapeDtypeStruct((GRAD, LANES), F32),
            jax.ShapeDtypeStruct((GRAD, LANES), F32),
        ),
        in_specs=[hbm] * 2,
        out_specs=[hbm] * 4,
        scratch_shapes=[
            pltpu.VMEM((5, SLAB, 4 * FZ, LANES), BF),
            pltpu.VMEM((W_ROWS, LANES), BF),
            pltpu.VMEM((SLAB * PLANE, LANES), F32),
            pltpu.VMEM((2 * GRAD, LANES), F32),
            dma((6, SLAB)), dma((11,)),
        ],
        compiler_params=pltpu.CompilerParams(vmem_limit_bytes=56 * 1024 * 1024),
        cost_estimate=pl.CostEstimate(flops=0, bytes_accessed=5_000_000, transcendentals=0),
    )(full, grads)
    out_field = out.reshape(SLAB, CY, CZ, LANES)
    field_grad = jnp.transpose(field.reshape(FY, FZ, SLAB, LANES), (2, 0, 1, 3))
    inner_grad = jnp.transpose(inner.reshape(3, 3, 3, MID, LANES), (0, 1, 2, 4, 3))
    outer_grad = outer.reshape(3, 3, 3, MID, LANES)
    return (out_field, field_grad, inner_grad, outer_grad)


def solution(mesh):
    return jax.shard_map(
        shards,
        mesh=mesh,
        in_specs=(
            P("gx", None, None, None),
            P(None, None, None, None, "af"),
            P(None, None, None, "af", None),
            P("gx", None, None, None),
        ),
        out_specs=(
            P("gx", None, None, None),
            P("gx", None, None, None),
            P(None, None, None, None, "af"),
            P(None, None, None, "af", None),
        ),
        check_vma=False,
    )
```

```python
import jax
import jax.numpy as jnp
from jax import lax
from jax.experimental import pallas as pl
from jax.experimental.pallas import tpu as pltpu
from jax.sharding import PartitionSpec as P

MESH = pl.DeviceIdType.MESH
BF = jnp.bfloat16
F32 = jnp.float32

SLAB = 4
CY, CZ = 16, 32
PITCH = 48
LANES = 128
MID = 32
TAPS = 9
HY, HALF = 18, 9
FY, FZ = 20, 36
PLANE = FY * FZ
CELLS = CY * CZ
ORDER = (1, 2, 0, 3)

OUT_PIECE = 2 * CELLS
FIELD_SLOT = 768
FIELD_BASE = 2 * OUT_PIECE
AF_ROWS = (OUT_PIECE, OUT_PIECE, 2 * FIELD_SLOT, FIELD_SLOT, FIELD_SLOT)
AF_BASE = tuple(sum(AF_ROWS[:p]) for p in range(5))
AF_TOTAL = sum(AF_ROWS)
AF_LAND = tuple(7 * base // 16 for base in AF_BASE)
HALO = 368
GRAD = 3 * TAPS * MID
W_ROWS = 1792
W_PART = W_ROWS // 4


def align(value, by=16):
    return pl.multiple_of(value, by)


def kernel(
    disp, cot, win, wout,
    full_ref, grads_ref,
    raw, D, C, H3, P3, W1T, W1, W2T, W2, AI, AO, DF, FS, EXTRA, B, R, WB, WZ, WR, QS, QR, HS, HL, HF,
    land_core, land_af, land_z, land_x,
    load_sem, halo_s, halo_r, core_s, core_r, rs_s, rs_r, ag_s, ag_r, ws_s, ws_r, wx_s, wx_r, wg_s, wg_r, store_sem,
):
    gx = lax.axis_index("gx")
    af = lax.axis_index("af")
    core = lax.rem(af, 2)
    y = lax.rem(lax.div(af, 2), 4)
    xl = lax.div(af, 8)
    z = lax.rem(gx, 4)
    xh = lax.div(gx, 4)

    af_peers, z_peers = [], []
    for dx, dy in ((1, 2), (0, 2), (1, 1), (1, 3), (0, 1), (0, 3), (1, 0)):
        x2, y2 = lax.rem(xl + dx, 2), lax.rem(y + dy, 4)
        af_peers.append(((gx, (x2 * 4 + y2) * 2 + core), x2 * 4 + y2))
    for dz in (2, 1, 3):
        z2 = lax.rem(z + dz, 4)
        z_peers.append(((xh * 4 + z2, af), z2))
    x_peer = ((1 - xh) * 4 + z, af)
    other_core = (gx, af + 1 - 2 * core)
    right = (lax.rem(gx + 1, 8), af)
    left = (lax.rem(gx + 7, 8), af)

    loads = [
        pltpu.make_async_copy(disp, raw, load_sem.at[0]),
        pltpu.make_async_copy(cot, C.at[pl.ds(1, SLAB), pl.ds(2, CY)], load_sem.at[1]),
        pltpu.make_async_copy(win, W1.at[:, pl.ds(0, 3 * MID)], load_sem.at[2]),
        pltpu.make_async_copy(wout, W2.at[:, pl.ds(0, 3 * MID)], load_sem.at[3]),
    ]
    for load in loads:
        load.start()
    barrier = pltpu.get_barrier_semaphore()
    peers = [peer for peer, _ in af_peers + z_peers] + [x_peer, other_core, left, right]
    for peer in peers:
        pl.semaphore_signal(barrier, inc=1, device_id=peer, device_id_type=MESH)

    C[:, 0:2] = jnp.zeros((6, 2, CZ, LANES), BF)
    C[:, 18:20] = jnp.zeros((6, 2, CZ, LANES), BF)
    P3[:, 0:2] = jnp.zeros((6, 2, PITCH, LANES), BF)
    P3[:, 20:22] = jnp.zeros((6, 2, PITCH, LANES), BF)
    DF[SLAB * PLANE:, :] = jnp.zeros((SLAB * (PITCH - FZ), LANES), F32)
    HF[PLANE:, :] = jnp.zeros((16, LANES), F32)
    zero_rows = jnp.zeros((TAPS, LANES - 3 * MID, LANES), BF)
    W1[:, 3 * MID:] = zero_rows
    W2[:, 3 * MID:] = zero_rows
    AI[...] = jnp.zeros_like(AI)
    AO[...] = jnp.zeros_like(AO)
    WB[2 * GRAD:, :] = jnp.zeros((W_ROWS - 2 * GRAD, LANES), BF)
    FS[2 * PLANE:, :] = jnp.zeros((2 * FIELD_SLOT - 2 * PLANE, LANES), F32)

    loads[0].wait()
    line_row = lax.broadcasted_iota(jnp.int32, (PITCH, LANES), 0)

    def widen(i, _):
        rows = pl.ds(align(i * 4 * FZ * SLAB), 4 * FZ * SLAB)
        DF[rows, :] = raw[rows, :].astype(F32)
        return 0

    lax.fori_loop(0, FY // 4, widen, 0)
    for side, x in enumerate((0, SLAB - 1)):
        HS[side] = DF[pl.ds(x, PLANE, stride=SLAB), :].astype(BF)

    def part(i, _):
        for x in range(SLAB):
            line = DF[pl.ds(i * FZ * SLAB + x, PITCH, stride=SLAB), :]
            D[x + 1, i] = jnp.where(line_row < FZ, line, 0.0).astype(BF)
        return 0

    lax.fori_loop(0, FY, part, 0)
    for load in loads[1:]:
        load.wait()
    for straight, turned in ((W1, W1T), (W2, W2T)):
        for tap in range(TAPS):
            turned[pl.ds(tap * LANES, LANES), :] = straight[tap].T

    def lane_roll(values, count):
        count = count % LANES
        return pltpu.roll(values, count, 1) if count else values

    def row_roll(values, count):
        return pltpu.roll(values, count % values.shape[0], 0)

    def gather(values, direction):
        one = row_roll(lane_roll(values, -MID), -direction)
        two = row_roll(lane_roll(values, -2 * MID), -2 * direction)
        return values + one + two

    def spread(values, direction):
        one = row_roll(lane_roll(values, MID), -direction)
        two = row_roll(lane_roll(values, 2 * MID), -2 * direction)
        return values + one + two

    def first_mids(values):
        lane = lax.broadcasted_iota(jnp.int32, values.shape, 1)
        return jnp.where(lane < MID, values, 0.0)

    def stage_one(x):
        rows = HY * PITCH
        lhs = jnp.concatenate(
            [D[x + a, pl.ds(b, HY)].reshape(rows, LANES) for a in range(3) for b in range(3)], axis=1
        )
        pre = gather(jnp.dot(lhs, W1T[...], preferred_element_type=F32), 1)
        lhs = jnp.concatenate(
            [
                C[x + 2 - a, pl.ds(2 - b, HY)].reshape(HY * CZ, LANES)
                for a in range(3)
                for b in range(3)
            ],
            axis=1,
        )
        back = jnp.dot(lhs, W2T[...], preferred_element_type=F32).reshape(HY, CZ, LANES)
        back = jnp.concatenate([back, jnp.zeros((HY, PITCH - CZ, LANES), F32)], axis=1)
        grad = gather(back.reshape(rows, LANES), -1)
        square = pre * pre + 0.01
        inverse = lax.rsqrt(square)
        hidden = first_mids(0.505 * pre + 0.495 * (square * inverse))
        grad = first_mids(grad * (0.505 + 0.495 * (pre * inverse)))
        H3[x + 1] = spread(hidden, 1).reshape(HY, PITCH, LANES)[:, :CZ].astype(BF)
        P3[x + 1, pl.ds(2, HY)] = spread(grad, -1).reshape(HY, PITCH, LANES).astype(BF)
        return hidden, grad

    def outer_plane(i):
        hidden, grad = stage_one(3 * i)
        half = HALF * PITCH
        packed = hidden[:half] + lane_roll(hidden[half:], MID)
        packed = packed + lane_roll(grad[:half], 2 * MID) + lane_roll(grad[half:], 3 * MID)
        QS[i] = packed.astype(BF)

    over_rows = (((0,), (0,)), ((), ()))

    def weight_terms(i):
        left_side = jnp.concatenate([H3[i + 1, pl.ds(b, CY)].reshape(CELLS, LANES) for b in range(3)], axis=1)
        right_side = jnp.concatenate(
            [C[i + 2 - a, pl.ds(2, CY)].reshape(CELLS, LANES) for a in range(3)], axis=1
        )
        AO[...] += lax.dot_general(left_side, right_side, over_rows, preferred_element_type=F32)
        left_side = jnp.concatenate(
            [P3[i + 1, pl.ds(2 - b, FY)].reshape(FY * PITCH, LANES) for b in range(3)], axis=1
        )
        right_side = jnp.concatenate([D[i + a].reshape(FY * PITCH, LANES) for a in range(3)], axis=1)
        AI[...] += lax.dot_general(left_side, right_side, over_rows, preferred_element_type=F32)

    def inner_weights(i, _):
        weight_terms(1 + i)
        return 0

    def outer_weights(i, _):
        weight_terms(3 * i)
        return 0

    def halo(index, src, dst, peer):
        copy = pltpu.make_async_remote_copy(
            src_ref=src, dst_ref=dst, send_sem=halo_s.at[index], recv_sem=halo_r.at[index],
            device_id=peer, device_id_type=MESH,
        )
        copy.start()
        halos.append(copy)
        return copy

    halos = []
    mine = pl.ds(align(core * 352), HALO)
    my_lines = pl.ds(2 + core * (CY // 2), CY // 2)
    stage_one(1)
    pl.semaphore_wait(barrier, len(peers))
    first_halos = [
        halo(0, HS.at[1, mine], HL.at[0, core], right),
        halo(1, HS.at[0, mine], HL.at[1, core], left),
        halo(2, C.at[SLAB, my_lines], C.at[0, my_lines], right),
        halo(3, C.at[1, my_lines], C.at[SLAB + 1, my_lines], left),
    ]
    stage_one(2)
    lax.fori_loop(0, 2, inner_weights, 0)
    shares = []
    for side in range(2):
        first_halos[side].wait_recv()
        shares.append(halo(4 + side, HL.at[side, core], HL.at[side, core], other_core))
    for side in range(2):
        first_halos[2 + side].wait_recv()
        rows = C.at[side * (SLAB + 1), my_lines]
        shares.append(halo(6 + side, rows, rows, other_core))
    for side in range(2):
        shares[side].wait_recv()
        HF[0:HALO, :] = HL[side, 0].astype(F32)
        HF[PLANE - HALO : PLANE, :] = HL[side, 1].astype(F32)
        for line in range(FY):
            value = HF[pl.ds(line * FZ, PITCH), :]
            D[side * (SLAB + 1), line] = jnp.where(line_row < FZ, value, 0.0).astype(BF)
    for side in range(2):
        shares[2 + side].wait_recv()
    outer_plane(0)
    second_halos = [halo(8, QS.at[0], QR.at[1], left)]
    outer_plane(1)
    second_halos.append(halo(9, QS.at[1], QR.at[0], right))

    sends = []

    def send(src, dst, send_sem, recv_sem, peer):
        copy = pltpu.make_async_remote_copy(
            src_ref=src, dst_ref=dst, send_sem=send_sem, recv_sem=recv_sem, device_id=peer, device_id_type=MESH
        )
        copy.start()
        sends.append(copy)
        return copy

    def scatter(peers, piece, landing, size, sems):
        return [
            send(piece(align(place * size), size), landing(j), sems[0](j), sems[1](j), peer)
            for j, (peer, place) in enumerate(peers)
        ]

    def total(copies, piece, landing, me, size):
        for copy in copies:
            copy.wait_recv()
        value = piece(align(me * size), size)[...].astype(F32)
        for j in range(len(copies)):
            value = value + landing(j)[...].astype(F32)
        return value

    def spread_out(peers, whole, me, size, sems):
        rows = whole(align(me * size), size)
        return [send(rows, rows, sems[0](j), sems[1](j), peer) for j, (peer, _) in enumerate(peers)]

    class AfSum:
        def __init__(self, p):
            self.p, self.half, self.size = p, AF_ROWS[p] // 2, AF_ROWS[p] // 16
            self.base = AF_BASE[p] + core * self.half
            self.me = xl * 4 + y
            self.landing = lambda j: land_af.at[pl.ds(AF_LAND[p] + j * self.size, self.size)]
            self.core_land = land_core.at[pl.ds(AF_BASE[p] // 2, self.half)]
            self.step = 0

        def piece(self, off, size):
            return B.at[pl.ds(align(self.base + off), size)]

        def whole(self, off, size):
            return R.at[pl.ds(align(self.base + off), size)]

        def advance(self):
            p, me, size = self.p, self.me, self.size
            if self.step == 0:
                give = B.at[pl.ds(align(AF_BASE[p] + (1 - core) * self.half), self.half)]
                self.copies = [send(give, self.core_land, core_s.at[p, 0], core_r.at[p, 0], other_core)]
            elif self.step == 1:
                self.copies[0].wait_recv()
                mine = self.piece(0, self.half)
                mine[...] = (mine[...].astype(F32) + self.core_land[...].astype(F32)).astype(BF)
                sems = (lambda j: rs_s.at[p, j], lambda j: rs_r.at[p, j])
                self.copies = scatter(af_peers, self.piece, self.landing, size, sems)
            elif self.step == 2:
                value = total(self.copies, self.piece, self.landing, me, size)
                value = value + EXTRA[pl.ds(align(self.base + me * size), size), :]
                self.whole(align(me * size), size)[...] = value.astype(BF)
                sems = (lambda j: ag_s.at[p, j], lambda j: ag_r.at[p, j])
                self.copies = spread_out(af_peers, self.whole, me, size, sems)
            elif self.step == 3:
                for copy in self.copies:
                    copy.wait_recv()
                rows = self.whole(0, self.half)
                self.copies = [send(rows, rows, core_s.at[p, 1], core_r.at[p, 1], other_core)]
            else:
                self.copies[0].wait_recv()
                rows = pl.ds(AF_BASE[p], AF_ROWS[p])
                store = pltpu.make_async_copy(R.at[rows], full_ref.at[rows], store_sem.at[p])
                store.start()
                stores.append(store)
            self.step += 1

    class GxSum:
        def __init__(self):
            self.step = 0

        def piece(self, off, size):
            return WB.at[pl.ds(off, size)]

        def whole(self, off, size):
            return WR.at[pl.ds(off, size)]

        def advance(self):
            if self.step == 0:
                sems = (lambda j: ws_s.at[j], lambda j: ws_r.at[j])
                self.copies = scatter(z_peers, self.piece, lambda j: land_z.at[j], W_PART, sems)
            elif self.step == 1:
                WZ[...] = total(self.copies, self.piece, lambda j: land_z.at[j], z, W_PART).astype(BF)
                self.copies = [send(WZ, land_x, wx_s.at[0], wx_r.at[0], x_peer)]
            elif self.step == 2:
                self.copies[0].wait_recv()
                value = WZ[...].astype(F32) + land_x[...].astype(F32)
                self.whole(align(z * W_PART), W_PART)[...] = value.astype(BF)
                sems = (lambda j: wg_s.at[j], lambda j: wg_r.at[j])
                self.copies = spread_out(z_peers, self.whole, z, W_PART, sems)
            else:
                for copy in self.copies:
                    copy.wait_recv()
                store = pltpu.make_async_copy(WR, grads_ref, store_sem.at[5])
                store.start()
                stores.append(store)
            self.step += 1

    stores = []
    out_a, out_b, field_a, field_b, field_c = [AfSum(p) for p in range(5)]
    grads = GxSum()

    def out_plane(slot):
        i = ORDER[slot]
        lhs = jnp.concatenate(
            [H3[i + a, pl.ds(b, CY)].reshape(CELLS, LANES) for a in range(3) for b in range(3)], axis=1
        )
        weights = W2[...].reshape(TAPS * LANES, LANES)
        B[pl.ds(slot * CELLS, CELLS), :] = jnp.dot(lhs, weights, preferred_element_type=F32).astype(BF)

    def field_plane(slot):
        i = ORDER[slot]
        lhs = jnp.concatenate(
            [
                P3[i + 2 - a, pl.ds(2 - b, FY)].reshape(FY * PITCH, LANES)
                for a in range(3)
                for b in range(3)
            ],
            axis=1,
        )
        weights = W1[...].reshape(TAPS * LANES, LANES)
        block = jnp.dot(lhs, weights, preferred_element_type=F32).reshape(FY, PITCH, LANES)
        base = (slot % 2) * FIELD_SLOT
        for line in range(FY):
            FS[pl.ds(base + line * FZ, FZ), :] = block[line, :FZ]
        B[pl.ds(FIELD_BASE + slot * FIELD_SLOT, FIELD_SLOT), :] = FS[pl.ds(base, FIELD_SLOT), :].astype(BF)

    def extra_out(i, _):
        for slot in range(SLAB):
            EXTRA[pl.ds(align(slot * CELLS + i * CZ), CZ), :] = DF[
                pl.ds((i + 2) * FZ * SLAB + 2 * SLAB + ORDER[slot], CZ, stride=SLAB), :
            ]
        return 0

    def extra_field():
        EXTRA[FIELD_BASE:, :] = jnp.zeros((SLAB * FIELD_SLOT, LANES), F32)
        for slot in range(SLAB):
            base = FIELD_BASE + slot * FIELD_SLOT
            for line in range(CY):
                EXTRA[pl.ds(base + (line + 2) * FZ + 2, CZ), :] = C[ORDER[slot] + 1, line + 2].astype(F32)

    def unpack(i, _):
        packed = QR[i].astype(F32)
        for r in range(2):
            hidden = first_mids(lane_roll(packed, -r * MID))
            grad = first_mids(lane_roll(packed, -(2 + r) * MID))
            hidden = spread(hidden, 1).reshape(HALF, PITCH, LANES)[:, :CZ]
            H3[5 * i, pl.ds(r * HALF, HALF)] = hidden.astype(BF)
            grad = spread(grad, -1).reshape(HALF, PITCH, LANES)
            P3[5 * i, pl.ds(2 + r * HALF, HALF)] = grad.astype(BF)
        return 0

    out_plane(0)
    out_plane(1)
    out_a.advance()
    field_plane(0)
    field_plane(1)
    field_a.advance()
    out_a.advance()
    lax.fori_loop(0, 2, outer_weights, 0)
    for acc, base in ((AI, 0), (AO, GRAD)):
        for a in range(3):
            for b in range(3):
                WB[pl.ds(base + (a * 3 + b) * 3 * MID, 3 * MID), :] = acc[
                    b * LANES : b * LANES + 3 * MID, a * LANES : (a + 1) * LANES
                ].astype(BF)
    field_a.advance()
    grads.advance()
    lax.fori_loop(0, CY, extra_out, 0)
    extra_field()
    for copy in second_halos:
        copy.wait_recv()
    lax.fori_loop(0, 2, unpack, 0)
    out_plane(2)
    out_plane(3)
    out_b.advance()
    field_plane(2)
    field_b.advance()
    out_b.advance()
    field_plane(3)
    field_c.advance()
    field_b.advance()
    field_c.advance()
    out_a.advance()
    grads.advance()
    field_a.advance()
    out_b.advance()
    field_b.advance()
    field_c.advance()
    grads.advance()
    out_a.advance()
    field_a.advance()
    out_b.advance()
    out_a.advance()
    field_a.advance()
    field_b.advance()
    out_b.advance()
    field_c.advance()
    grads.advance()
    field_b.advance()
    field_c.advance()
    for store in stores:
        store.wait()
    for copy in halos + sends:
        copy.wait_send()


def finish(full, grads, out_ref, field_ref, inner_ref, outer_ref, f_in, g_in, o_in, f_out, w_out, in_sem, out_sem):
    lines = 4
    steps = FY // lines
    rows = lines * FZ

    def source(step, slot):
        base = FIELD_BASE + slot * FIELD_SLOT
        return pltpu.make_async_copy(
            full.at[pl.ds(base + step * rows, rows)], f_in.at[step, slot], in_sem.at[step, slot]
        )

    inputs = [[source(step, slot) for slot in range(SLAB)] for step in range(steps)]
    whole = pltpu.make_async_copy(grads, g_in, in_sem.at[steps, 0])
    planes = pltpu.make_async_copy(full.at[pl.ds(0, SLAB * CELLS)], o_in, in_sem.at[steps, 1])
    for copies in inputs:
        for copy in copies:
            copy.start()
    whole.start()
    planes.start()
    stores = []

    def store(src, dst):
        copy = pltpu.make_async_copy(src, dst, out_sem.at[len(stores)])
        copy.start()
        stores.append(copy)

    for step in range(steps):
        for slot in range(SLAB):
            inputs[step][slot].wait()
            f_out[pl.ds(step * rows * SLAB + ORDER[slot], rows, stride=SLAB), :] = f_in[step, slot].astype(F32)
        part = pl.ds(step * rows * SLAB, rows * SLAB)
        store(f_out.at[part], field_ref.at[part])
    whole.wait()
    for p, ref in enumerate((inner_ref, outer_ref)):
        part = pl.ds(p * GRAD, GRAD)
        w_out[part, :] = g_in[part, :].astype(F32)
        store(w_out.at[part], ref)
    planes.wait()
    for slot in range(SLAB):
        store(o_in.at[pl.ds(slot * CELLS, CELLS)], out_ref.at[pl.ds(ORDER[slot] * CELLS, CELLS)])
    for copy in stores:
        copy.wait()


def shards(displace, weight_in, weight_out, cotangent):
    hbm = pl.BlockSpec(memory_space=pl.ANY)
    rows = jnp.transpose(displace, (1, 2, 0, 3)).reshape(SLAB * PLANE, LANES)
    win = jnp.transpose(weight_in, (0, 1, 2, 4, 3)).reshape(TAPS, 3 * MID, LANES)
    wout = weight_out.reshape(TAPS, 3 * MID, LANES)
    dma = pltpu.SemaphoreType.DMA
    full, grads = pl.pallas_call(
        kernel,
        out_shape=(
            jax.ShapeDtypeStruct((AF_TOTAL, LANES), BF),
            jax.ShapeDtypeStruct((W_ROWS, LANES), BF),
        ),
        in_specs=[pl.BlockSpec(memory_space=pltpu.HBM)] * 4,
        out_specs=[hbm] * 2,
        scratch_shapes=[
            pltpu.VMEM((SLAB * PLANE, LANES), BF),
            pltpu.VMEM((SLAB + 2, FY, PITCH, LANES), BF),
            pltpu.VMEM((SLAB + 2, FY, CZ, LANES), BF),
            pltpu.VMEM((SLAB + 2, HY, CZ, LANES), BF),
            pltpu.VMEM((SLAB + 2, HY + 4, PITCH, LANES), BF),
            pltpu.VMEM((TAPS * LANES, LANES), BF),
            pltpu.VMEM((TAPS, LANES, LANES), BF),
            pltpu.VMEM((TAPS * LANES, LANES), BF),
            pltpu.VMEM((TAPS, LANES, LANES), BF),
            pltpu.VMEM((3 * LANES, 3 * LANES), F32),
            pltpu.VMEM((3 * LANES, 3 * LANES), F32),
            pltpu.VMEM((SLAB * (PLANE + PITCH - FZ), LANES), F32),
            pltpu.VMEM((2 * FIELD_SLOT, LANES), F32),
            pltpu.VMEM((AF_TOTAL, LANES), F32),
            pltpu.VMEM((AF_TOTAL, LANES), BF),
            pltpu.VMEM((AF_TOTAL, LANES), BF),
            pltpu.VMEM((W_ROWS, LANES), BF),
            pltpu.VMEM((W_PART, LANES), BF),
            pltpu.VMEM((W_ROWS, LANES), BF),
            pltpu.VMEM((2, HALF * PITCH, LANES), BF),
            pltpu.VMEM((2, HALF * PITCH, LANES), BF),
            pltpu.VMEM((2, PLANE, LANES), BF),
            pltpu.VMEM((2, 2, HALO, LANES), BF),
            pltpu.VMEM((PLANE + 16, LANES), F32),
            pltpu.VMEM((AF_TOTAL // 2, LANES), BF),
            pltpu.VMEM((7 * AF_TOTAL // 16, LANES), BF),
            pltpu.VMEM((3, W_PART, LANES), BF),
            pltpu.VMEM((W_PART, LANES), BF),
            dma((4,)), dma((10,)), dma((10,)),
            dma((5, 2)), dma((5, 2)), dma((5, 7)), dma((5, 7)), dma((5, 7)), dma((5, 7)),
            dma((3,)), dma((3,)), dma((1,)), dma((1,)), dma((3,)), dma((3,)), dma((6,)),
        ],
        compiler_params=pltpu.CompilerParams(
            collective_id=0, has_side_effects=True, vmem_limit_bytes=56 * 1024 * 1024
        ),
        cost_estimate=pl.CostEstimate(flops=4_000_000_000, bytes_accessed=8_000_000, transcendentals=400_000),
    )(rows, cotangent, win, wout)
    out, field, inner, outer = pl.pallas_call(
        finish,
        out_shape=(
            jax.ShapeDtypeStruct((SLAB * CELLS, LANES), BF),
            jax.ShapeDtypeStruct((SLAB * PLANE, LANES), F32),
            jax.ShapeDtypeStruct((GRAD, LANES), F32),
            jax.ShapeDtypeStruct((GRAD, LANES), F32),
        ),
        in_specs=[hbm] * 2,
        out_specs=[hbm] * 4,
        scratch_shapes=[
            pltpu.VMEM((5, SLAB, 4 * FZ, LANES), BF),
            pltpu.VMEM((W_ROWS, LANES), BF),
            pltpu.VMEM((SLAB * CELLS, LANES), BF),
            pltpu.VMEM((SLAB * PLANE, LANES), F32),
            pltpu.VMEM((2 * GRAD, LANES), F32),
            dma((6, SLAB)), dma((11,)),
        ],
        compiler_params=pltpu.CompilerParams(vmem_limit_bytes=56 * 1024 * 1024),
        cost_estimate=pl.CostEstimate(flops=0, bytes_accessed=5_000_000, transcendentals=0),
    )(full, grads)
    out_field = out.reshape(SLAB, CY, CZ, LANES)
    field_grad = jnp.transpose(field.reshape(FY, FZ, SLAB, LANES), (2, 0, 1, 3))
    inner_grad = jnp.transpose(inner.reshape(3, 3, 3, MID, LANES), (0, 1, 2, 4, 3))
    outer_grad = outer.reshape(3, 3, 3, MID, LANES)
    return (out_field, field_grad, inner_grad, outer_grad)


def solution(mesh):
    return jax.shard_map(
        shards,
        mesh=mesh,
        in_specs=(
            P("gx", None, None, None),
            P(None, None, None, None, "af"),
            P(None, None, None, "af", None),
            P("gx", None, None, None),
        ),
        out_specs=(
            P("gx", None, None, None),
            P("gx", None, None, None),
            P(None, None, None, None, "af"),
            P(None, None, None, "af", None),
        ),
        check_vma=False,
    )
```

```python
import jax
import jax.numpy as jnp
from jax import lax
from jax.experimental import pallas as pl
from jax.experimental.pallas import tpu as pltpu
from jax.sharding import PartitionSpec as P

MESH = pl.DeviceIdType.MESH
BF = jnp.bfloat16
F32 = jnp.float32

SLAB = 4
CY, CZ = 16, 32
PITCH = 48
LANES = 128
MID = 32
TWO = 2 * MID
FY, FZ = 20, 36
HY, DY, OY, GY = 10, 12, 8, 10
DROWS = DY * FZ
BLOCKS = 5
ORDER = (1, 2, 0, 3)

OUT_SLOT = OY * CZ
FIELD_SLOT = 384
FIELD_BASE = SLAB * OUT_SLOT
AF_ROWS = (2 * OUT_SLOT, 2 * OUT_SLOT, 2 * FIELD_SLOT, FIELD_SLOT, FIELD_SLOT)
AF_BASE = tuple(sum(AF_ROWS[:p]) for p in range(5))
AF_TOTAL = sum(AF_ROWS)
AF_LAND = tuple(7 * base // 8 for base in AF_BASE)
GRAD = 27 * MID
W_ROWS = 1792
W_PART = W_ROWS // 4


def align(value, by=16):
    return pl.multiple_of(value, by)


def kernel(
    disp, cot, win, wout,
    full_ref, grads_ref,
    raw, D, C, HA, HB, PA, PB, WIN, WOUT, W1T, W1, W2T, W2, AI, AO, DF, FS, EXTRA, B, R, WB, WZ, WR, QS, QR, HS, HL, HF,
    land_af, land_wc, land_z, land_x,
    load_sem, halo_s, halo_r, core_s, core_r, rs_s, rs_r, ag_s, ag_r, ws_s, ws_r, wx_s, wx_r, wg_s, wg_r, store_sem,
):
    gx = lax.axis_index("gx")
    af = lax.axis_index("af")
    core = lax.rem(af, 2)
    y = lax.rem(lax.div(af, 2), 4)
    xl = lax.div(af, 8)
    z = lax.rem(gx, 4)
    xh = lax.div(gx, 4)

    af_peers, z_peers = [], []
    for dx, dy in ((1, 2), (0, 2), (1, 1), (1, 3), (0, 1), (0, 3), (1, 0)):
        x2, y2 = lax.rem(xl + dx, 2), lax.rem(y + dy, 4)
        af_peers.append(((gx, (x2 * 4 + y2) * 2 + core), x2 * 4 + y2))
    for dz in (2, 1, 3):
        z2 = lax.rem(z + dz, 4)
        z_peers.append(((xh * 4 + z2, af), z2))
    x_peer = ((1 - xh) * 4 + z, af)
    other_core = (gx, af + 1 - 2 * core)
    right = (lax.rem(gx + 1, 8), af)
    left = (lax.rem(gx + 7, 8), af)

    cot_lines = pl.ds(2 - 2 * core, HY)
    loads = [
        pltpu.make_async_copy(disp.at[pl.ds(align(core * 8 * FZ * SLAB), DY * FZ * SLAB)], raw, load_sem.at[0]),
        pltpu.make_async_copy(cot.at[:, pl.ds(6 * core, HY)], C.at[pl.ds(1, SLAB), cot_lines], load_sem.at[1]),
        pltpu.make_async_copy(win, WIN.at[core], load_sem.at[2]),
        pltpu.make_async_copy(wout, WOUT.at[core], load_sem.at[3]),
    ]
    for load in loads:
        load.start()
    barrier = pltpu.get_barrier_semaphore()
    peers = [peer for peer, _ in af_peers + z_peers] + [x_peer, other_core, left, right]
    for peer in peers:
        pl.semaphore_signal(barrier, inc=1, device_id=peer, device_id_type=MESH)

    C[:, pl.ds(10 * core, 2)] = jnp.zeros((6, 2, CZ, LANES), BF)
    PA[:, pl.ds(10 * core, 2)] = jnp.zeros((6, 2, PITCH, LANES), BF)
    PB[:, pl.ds(10 * core + 1, 2)] = jnp.zeros((6, 2, PITCH, LANES), BF)
    DF[DROWS * SLAB:, :] = jnp.zeros((SLAB * (PITCH - FZ), LANES), F32)
    HF[DROWS:, :] = jnp.zeros((16, LANES), F32)
    for straight in (W1, W2):
        for a in range(3):
            straight[pl.ds((a * BLOCKS + 4) * LANES + TWO, TWO), :] = jnp.zeros((TWO, LANES), BF)
    AI[...] = jnp.zeros_like(AI)
    AO[...] = jnp.zeros_like(AO)
    for k in range(2):
        WB[k, 2 * GRAD:, :] = jnp.zeros((W_ROWS - 2 * GRAD, LANES), BF)
    for slot in range(SLAB):
        FS[pl.ds(slot * FIELD_SLOT + GY * FZ, FIELD_SLOT - GY * FZ), :] = jnp.zeros(
            (FIELD_SLOT - GY * FZ, LANES), F32
        )

    loads[0].wait()
    line_row = lax.broadcasted_iota(jnp.int32, (PITCH, LANES), 0)

    def widen(i, _):
        rows = pl.ds(align(i * 4 * FZ * SLAB), 4 * FZ * SLAB)
        DF[rows, :] = raw[rows, :].astype(F32)
        return 0

    lax.fori_loop(0, DY // 4, widen, 0)
    for side, x in enumerate((0, SLAB - 1)):
        HS[side] = DF[pl.ds(x, DROWS, stride=SLAB), :].astype(BF)

    def part(i, _):
        for x in range(SLAB):
            line = DF[pl.ds(i * FZ * SLAB + x, PITCH, stride=SLAB), :]
            D[x + 1, i] = jnp.where(line_row < FZ, line, 0.0).astype(BF)
        return 0

    lax.fori_loop(0, DY, part, 0)
    for load in loads[1:]:
        load.wait()

    def halo(index, src, dst, peer):
        copy = pltpu.make_async_remote_copy(
            src_ref=src, dst_ref=dst, send_sem=halo_s.at[index], recv_sem=halo_r.at[index],
            device_id=peer, device_id_type=MESH,
        )
        copy.start()
        halos.append(copy)
        return copy

    halos = []
    pl.semaphore_wait(barrier, len(peers))
    weights = [
        halo(0, WIN.at[core], WIN.at[core], other_core),
        halo(1, WOUT.at[core], WOUT.at[core], other_core),
    ]
    first_halos = [
        halo(2, HS.at[1], HL.at[0], right),
        halo(3, HS.at[0], HL.at[1], left),
        halo(4, C.at[SLAB, cot_lines], C.at[0, cot_lines], right),
        halo(5, C.at[1, cot_lines], C.at[SLAB + 1, cot_lines], left),
    ]

    def extra_out(i, _):
        for slot in range(SLAB):
            EXTRA[pl.ds(align(slot * OUT_SLOT + i * CZ), CZ), :] = DF[
                pl.ds((i + 2) * FZ * SLAB + 2 * SLAB + ORDER[slot], CZ, stride=SLAB), :
            ]
        return 0

    lax.fori_loop(0, OY, extra_out, 0)
    EXTRA[FIELD_BASE:, :] = jnp.zeros((SLAB * FIELD_SLOT, LANES), F32)
    for slot in range(SLAB):
        base = FIELD_BASE + slot * FIELD_SLOT
        for line in range(GY):
            EXTRA[pl.ds(base + line * FZ + 2, CZ), :] = C[ORDER[slot] + 1, 2 * core + line].astype(F32)

    for copy in weights:
        copy.wait_recv()

    def places(blocks_c2):
        table = {(b, c): b * LANES + c * TWO for b in range(3) for c in range(2)}
        for b, row in enumerate(blocks_c2):
            table[b, 2] = row
        return table

    in_places = places((4 * LANES, 3 * LANES + TWO, 3 * LANES))
    out_places = places((3 * LANES, 3 * LANES + TWO, 4 * LANES))
    for src, straight, turned, table in ((WIN, W1, W1T, in_places), (WOUT, W2, W2T, out_places)):
        for a in range(3):
            for (b, c), row in table.items():
                for k in range(2):
                    straight[pl.ds(a * BLOCKS * LANES + row + k * MID, MID), :] = src[
                        k, pl.ds(((a * 3 + b) * 3 + c) * MID, MID), :
                    ]
        for a in range(3):
            for b in range(3):
                rows = pl.ds((a * 3 + b) * LANES, LANES)
                turned[rows, :LANES] = straight[pl.ds((a * BLOCKS + b) * LANES, LANES), :].T
                row = table[b, 2]
                pair = straight[pl.ds(a * BLOCKS * LANES + row // LANES * LANES, LANES), :]
                if row % LANES:
                    pair = jnp.concatenate([pair[TWO:], pair[:TWO]], axis=0)
                turned[rows, LANES:] = pair.T

    def lane_half(values):
        return pltpu.roll(values, TWO, 1)

    def row_roll(values, count):
        return pltpu.roll(values, count % values.shape[0], 0)

    def gather(values, direction):
        near, far = values[:, :LANES], values[:, LANES:]
        return near + row_roll(lane_half(near), -direction) + row_roll(far, -2 * direction)

    def first_mids(values):
        lane = lax.broadcasted_iota(jnp.int32, values.shape, 1)
        return jnp.where(lane < TWO, values, 0.0)

    rows = HY * PITCH

    def store_hidden(plane, hidden):
        near = hidden + lane_half(row_roll(hidden, -1))
        far = row_roll(hidden, -2).reshape(HY, PITCH, LANES)[:, :CZ].reshape(HY * CZ, LANES)
        later = jnp.concatenate([far[CZ:], jnp.zeros((CZ, LANES), F32)], axis=0)
        HA[plane] = near.reshape(HY, PITCH, LANES)[:, :CZ].astype(BF)
        HB[plane] = (far + lane_half(later)).reshape(HY, CZ, LANES).astype(BF)

    def store_grad(plane, grad):
        near = grad + lane_half(row_roll(grad, 1))
        far = row_roll(grad, 2)
        nothing = jnp.zeros((PITCH, LANES), F32)
        both = jnp.concatenate([nothing, far], axis=0) + lane_half(jnp.concatenate([far, nothing], axis=0))
        PA[plane, pl.ds(2 - 2 * core, HY)] = near.reshape(HY, PITCH, LANES).astype(BF)
        PB[plane, pl.ds(2 - 2 * core, HY + 1)] = both.reshape(HY + 1, PITCH, LANES).astype(BF)

    def stage_one(x):
        lhs = jnp.concatenate(
            [D[x + a, pl.ds(b, HY)].reshape(rows, LANES) for a in range(3) for b in range(3)], axis=1
        )
        pre = gather(jnp.dot(lhs, W1T[...], preferred_element_type=F32), 1)
        lhs = jnp.concatenate(
            [
                C[x + 2 - a, pl.ds(2 - b, HY)].reshape(HY * CZ, LANES)
                for a in range(3)
                for b in range(3)
            ],
            axis=1,
        )
        back = jnp.dot(lhs, W2T[...], preferred_element_type=F32).reshape(HY, CZ, 2 * LANES)
        back = jnp.concatenate([back, jnp.zeros((HY, PITCH - CZ, 2 * LANES), F32)], axis=1)
        grad = gather(back.reshape(rows, 2 * LANES), -1)
        square = pre * pre + 0.01
        inverse = lax.rsqrt(square)
        hidden = first_mids(0.505 * pre + 0.495 * (square * inverse))
        grad = first_mids(grad * (0.505 + 0.495 * (pre * inverse)))
        store_hidden(x + 1, hidden)
        store_grad(x + 1, grad)
        return hidden, grad

    def outer_plane(i):
        hidden, grad = stage_one(3 * i)
        QS[i] = (hidden + lane_half(grad)).astype(BF)

    over_rows = (((0,), (0,)), ((), ()))

    def hidden_blocks(plane):
        blocks = [HA[plane, pl.ds(b, OY)] for b in range(3)] + [HB[plane, pl.ds(b, OY)] for b in (0, 2)]
        return [block.reshape(OUT_SLOT, LANES) for block in blocks]

    def grad_blocks(plane):
        blocks = [PA[plane, pl.ds(2 - b, GY)] for b in range(3)] + [PB[plane, pl.ds(b, GY)] for b in (1, 3)]
        return [block.reshape(GY * PITCH, LANES) for block in blocks]

    def weight_terms(i):
        right_side = jnp.concatenate(
            [C[i + 2 - a, pl.ds(2, OY)].reshape(OUT_SLOT, LANES) for a in range(3)], axis=1
        )
        AO[...] += lax.dot_general(
            jnp.concatenate(hidden_blocks(i + 1), axis=1), right_side, over_rows, preferred_element_type=F32
        )
        right_side = jnp.concatenate(
            [D[i + a, pl.ds(2 * core, GY)].reshape(GY * PITCH, LANES) for a in range(3)], axis=1
        )
        AI[...] += lax.dot_general(
            jnp.concatenate(grad_blocks(i + 1), axis=1), right_side, over_rows, preferred_element_type=F32
        )

    def inner_weights(i, _):
        weight_terms(1 + i)
        return 0

    def outer_weights(i, _):
        weight_terms(3 * i)
        return 0

    stage_one(1)
    stage_one(2)
    lax.fori_loop(0, 2, inner_weights, 0)
    for side in range(2):
        first_halos[side].wait_recv()
        HF[0:DROWS, :] = HL[side].astype(F32)
        for line in range(DY):
            value = HF[pl.ds(line * FZ, PITCH), :]
            D[side * (SLAB + 1), line] = jnp.where(line_row < FZ, value, 0.0).astype(BF)
    for side in range(2):
        first_halos[2 + side].wait_recv()
    outer_plane(0)
    second_halos = [halo(6, QS.at[0], QR.at[1], left)]
    outer_plane(1)
    second_halos.append(halo(7, QS.at[1], QR.at[0], right))

    sends = []

    def send(src, dst, send_sem, recv_sem, peer):
        copy = pltpu.make_async_remote_copy(
            src_ref=src, dst_ref=dst, send_sem=send_sem, recv_sem=recv_sem, device_id=peer, device_id_type=MESH
        )
        copy.start()
        sends.append(copy)
        return copy

    def scatter(peers, piece, landing, size, sems):
        return [
            send(piece(align(place * size), size), landing(j), sems[0](j), sems[1](j), peer)
            for j, (peer, place) in enumerate(peers)
        ]

    def total(copies, piece, landing, me, size):
        for copy in copies:
            copy.wait_recv()
        value = piece(align(me * size), size)[...].astype(F32)
        for j in range(len(copies)):
            value = value + landing(j)[...].astype(F32)
        return value

    def spread_out(peers, whole, me, size, sems):
        rows = whole(align(me * size), size)
        return [send(rows, rows, sems[0](j), sems[1](j), peer) for j, (peer, _) in enumerate(peers)]

    class AfSum:
        def __init__(self, p):
            self.p, self.size = p, AF_ROWS[p] // 8
            self.me = xl * 4 + y
            self.landing = lambda j: land_af.at[pl.ds(AF_LAND[p] + j * self.size, self.size)]
            self.step = 0

        def piece(self, off, size):
            return B.at[pl.ds(align(AF_BASE[self.p] + off), size)]

        def whole(self, off, size):
            return R.at[core, pl.ds(align(AF_BASE[self.p] + off), size)]

        def advance(self):
            p, me, size = self.p, self.me, self.size
            if self.step == 0:
                sems = (lambda j: rs_s.at[p, j], lambda j: rs_r.at[p, j])
                self.copies = scatter(af_peers, self.piece, self.landing, size, sems)
            elif self.step == 1:
                value = total(self.copies, self.piece, self.landing, me, size)
                value = value + EXTRA[pl.ds(align(AF_BASE[p] + me * size), size), :]
                self.whole(align(me * size), size)[...] = value.astype(BF)
                sems = (lambda j: ag_s.at[p, j], lambda j: ag_r.at[p, j])
                self.copies = spread_out(af_peers, self.whole, me, size, sems)
            elif self.step == 2:
                for copy in self.copies:
                    copy.wait_recv()
                rows = self.whole(0, AF_ROWS[p])
                self.copies = [send(rows, rows, core_s.at[p], core_r.at[p], other_core)]
            else:
                self.copies[0].wait_recv()
                rows = pl.ds(AF_BASE[p], AF_ROWS[p])
                store = pltpu.make_async_copy(R.at[:, rows], full_ref.at[:, rows], store_sem.at[p])
                store.start()
                stores.append(store)
            self.step += 1

    class GxSum:
        def __init__(self):
            self.step = 0

        def piece(self, off, size):
            return WB.at[core, pl.ds(off, size)]

        def whole(self, off, size):
            return WR.at[pl.ds(off, size)]

        def advance(self):
            if self.step == 0:
                self.copies = [send(WB.at[1 - core], land_wc, core_s.at[5], core_r.at[5], other_core)]
            elif self.step == 1:
                self.copies[0].wait_recv()
                mine = WB.at[core]
                mine[...] = (mine[...].astype(F32) + land_wc[...].astype(F32)).astype(BF)
                sems = (lambda j: ws_s.at[j], lambda j: ws_r.at[j])
                self.copies = scatter(z_peers, self.piece, lambda j: land_z.at[j], W_PART, sems)
            elif self.step == 2:
                WZ[...] = total(self.copies, self.piece, lambda j: land_z.at[j], z, W_PART).astype(BF)
                self.copies = [send(WZ, land_x, wx_s.at[0], wx_r.at[0], x_peer)]
            elif self.step == 3:
                self.copies[0].wait_recv()
                value = WZ[...].astype(F32) + land_x[...].astype(F32)
                self.whole(align(z * W_PART), W_PART)[...] = value.astype(BF)
                sems = (lambda j: wg_s.at[j], lambda j: wg_r.at[j])
                self.copies = spread_out(z_peers, self.whole, z, W_PART, sems)
            else:
                for copy in self.copies:
                    copy.wait_recv()
                store = pltpu.make_async_copy(WR, grads_ref, store_sem.at[5])
                store.start()
                stores.append(store)
            self.step += 1

    stores = []
    out_a, out_b, field_a, field_b, field_c = [AfSum(p) for p in range(5)]
    grads = GxSum()

    def out_plane(slot):
        i = ORDER[slot]
        lhs = jnp.concatenate([block for a in range(3) for block in hidden_blocks(i + a)], axis=1)
        B[pl.ds(slot * OUT_SLOT, OUT_SLOT), :] = jnp.dot(lhs, W2[...], preferred_element_type=F32).astype(BF)

    def field_plane(slot):
        i = ORDER[slot]
        lhs = jnp.concatenate([block for a in range(3) for block in grad_blocks(i + 2 - a)], axis=1)
        block = jnp.dot(lhs, W1[...], preferred_element_type=F32).reshape(GY, PITCH, LANES)
        base = slot * FIELD_SLOT
        for line in range(GY):
            FS[pl.ds(base + line * FZ, FZ), :] = block[line, :FZ]
        B[pl.ds(FIELD_BASE + base, FIELD_SLOT), :] = FS[pl.ds(base, FIELD_SLOT), :].astype(BF)

    def edge_weights():
        lax.fori_loop(0, 2, outer_weights, 0)
        for acc, table, base in ((AI, in_places, 0), (AO, out_places, GRAD)):
            for a in range(3):
                for (b, c), row in table.items():
                    for k in range(2):
                        WB[k, pl.ds(base + ((a * 3 + b) * 3 + c) * MID, MID), :] = acc[
                            pl.ds(row + k * MID, MID), a * LANES : (a + 1) * LANES
                        ].astype(BF)

    def neighbours_planes():
        for copy in second_halos:
            copy.wait_recv()
        for side in range(2):
            packed = QR[side].astype(F32)
            store_hidden(5 * side, first_mids(packed))
            store_grad(5 * side, first_mids(lane_half(packed)))

    out_plane(0)
    out_plane(1)
    out_a.advance()
    field_plane(0)
    field_plane(1)
    field_a.advance()
    edge_weights()
    grads.advance()
    neighbours_planes()
    out_plane(2)
    out_plane(3)
    out_b.advance()
    field_plane(2)
    field_b.advance()
    field_plane(3)
    field_c.advance()
    grads.advance()
    out_a.advance()
    field_a.advance()
    out_b.advance()
    grads.advance()
    field_b.advance()
    field_c.advance()
    out_a.advance()
    field_a.advance()
    grads.advance()
    out_b.advance()
    out_a.advance()
    field_a.advance()
    field_b.advance()
    out_b.advance()
    field_c.advance()
    grads.advance()
    field_b.advance()
    field_c.advance()
    for store in stores:
        store.wait()
    for copy in halos + sends:
        copy.wait_send()


def finish(full, grads, out_ref, field_ref, inner_ref, outer_ref, f_in, g_in, o_in, f_out, w_out, in_sem, out_sem):
    inputs = [
        pltpu.make_async_copy(
            full.at[core, pl.ds(FIELD_BASE, SLAB * FIELD_SLOT)], f_in.at[core], in_sem.at[core]
        )
        for core in range(2)
    ]
    whole = pltpu.make_async_copy(grads, g_in, in_sem.at[2])
    planes = pltpu.make_async_copy(full.at[:, pl.ds(0, FIELD_BASE)], o_in, in_sem.at[3])
    for copy in inputs + [whole, planes]:
        copy.start()
    stores = []

    def store(src, dst):
        copy = pltpu.make_async_copy(src, dst, out_sem.at[len(stores)])
        copy.start()
        stores.append(copy)

    rows = GY * FZ
    for core in range(2):
        inputs[core].wait()
        for slot in range(SLAB):
            f_out[pl.ds(core * rows * SLAB + ORDER[slot], rows, stride=SLAB), :] = f_in[
                core, pl.ds(slot * FIELD_SLOT, rows), :
            ].astype(F32)
        part = pl.ds(core * rows * SLAB, rows * SLAB)
        store(f_out.at[part], field_ref.at[part])
    whole.wait()
    for p, ref in enumerate((inner_ref, outer_ref)):
        part = pl.ds(p * GRAD, GRAD)
        w_out[part, :] = g_in[part, :].astype(F32)
        store(w_out.at[part], ref)
    planes.wait()
    for slot in range(SLAB):
        for core in range(2):
            store(
                o_in.at[core, pl.ds(slot * OUT_SLOT, OUT_SLOT)],
                out_ref.at[pl.ds((2 * ORDER[slot] + core) * OUT_SLOT, OUT_SLOT)],
            )
    for copy in stores:
        copy.wait()


def shards(displace, weight_in, weight_out, cotangent):
    hbm = pl.BlockSpec(memory_space=pl.ANY)
    rows = jnp.transpose(displace, (1, 2, 0, 3)).reshape(SLAB * FY * FZ, LANES)
    win = jnp.transpose(weight_in, (0, 1, 2, 4, 3)).reshape(GRAD, LANES)
    wout = weight_out.reshape(GRAD, LANES)
    dma = pltpu.SemaphoreType.DMA
    full, grads = pl.pallas_call(
        kernel,
        out_shape=(
            jax.ShapeDtypeStruct((2, AF_TOTAL, LANES), BF),
            jax.ShapeDtypeStruct((W_ROWS, LANES), BF),
        ),
        in_specs=[hbm] * 4,
        out_specs=[hbm] * 2,
        scratch_shapes=[
            pltpu.VMEM((SLAB * DROWS, LANES), BF),
            pltpu.VMEM((SLAB + 2, DY, PITCH, LANES), BF),
            pltpu.VMEM((SLAB + 2, DY, CZ, LANES), BF),
            pltpu.VMEM((SLAB + 2, HY, CZ, LANES), BF),
            pltpu.VMEM((SLAB + 2, HY, CZ, LANES), BF),
            pltpu.VMEM((SLAB + 2, HY + 2, PITCH, LANES), BF),
            pltpu.VMEM((SLAB + 2, HY + 3, PITCH, LANES), BF),
            pltpu.VMEM((2, GRAD, LANES), BF),
            pltpu.VMEM((2, GRAD, LANES), BF),
            pltpu.VMEM((9 * LANES, 2 * LANES), BF),
            pltpu.VMEM((3 * BLOCKS * LANES, LANES), BF),
            pltpu.VMEM((9 * LANES, 2 * LANES), BF),
            pltpu.VMEM((3 * BLOCKS * LANES, LANES), BF),
            pltpu.VMEM((BLOCKS * LANES, 3 * LANES), F32),
            pltpu.VMEM((BLOCKS * LANES, 3 * LANES), F32),
            pltpu.VMEM((SLAB * (DROWS + PITCH - FZ), LANES), F32),
            pltpu.VMEM((SLAB * FIELD_SLOT, LANES), F32),
            pltpu.VMEM((AF_TOTAL, LANES), F32),
            pltpu.VMEM((AF_TOTAL, LANES), BF),
            pltpu.VMEM((2, AF_TOTAL, LANES), BF),
            pltpu.VMEM((2, W_ROWS, LANES), BF),
            pltpu.VMEM((W_PART, LANES), BF),
            pltpu.VMEM((W_ROWS, LANES), BF),
            pltpu.VMEM((2, HY * PITCH, LANES), BF),
            pltpu.VMEM((2, HY * PITCH, LANES), BF),
            pltpu.VMEM((2, DROWS, LANES), BF),
            pltpu.VMEM((2, DROWS, LANES), BF),
            pltpu.VMEM((DROWS + 16, LANES), F32),
            pltpu.VMEM((7 * AF_TOTAL // 8, LANES), BF),
            pltpu.VMEM((W_ROWS, LANES), BF),
            pltpu.VMEM((3, W_PART, LANES), BF),
            pltpu.VMEM((W_PART, LANES), BF),
            dma((4,)), dma((8,)), dma((8,)),
            dma((6,)), dma((6,)), dma((5, 7)), dma((5, 7)), dma((5, 7)), dma((5, 7)),
            dma((3,)), dma((3,)), dma((1,)), dma((1,)), dma((3,)), dma((3,)), dma((6,)),
        ],
        compiler_params=pltpu.CompilerParams(
            collective_id=0, has_side_effects=True, vmem_limit_bytes=56 * 1024 * 1024
        ),
        cost_estimate=pl.CostEstimate(flops=4_000_000_000, bytes_accessed=8_000_000, transcendentals=400_000),
    )(rows, cotangent, win, wout)
    out, field, inner, outer = pl.pallas_call(
        finish,
        out_shape=(
            jax.ShapeDtypeStruct((SLAB * CY * CZ, LANES), BF),
            jax.ShapeDtypeStruct((SLAB * FY * FZ, LANES), F32),
            jax.ShapeDtypeStruct((GRAD, LANES), F32),
            jax.ShapeDtypeStruct((GRAD, LANES), F32),
        ),
        in_specs=[hbm] * 2,
        out_specs=[hbm] * 4,
        scratch_shapes=[
            pltpu.VMEM((2, SLAB * FIELD_SLOT, LANES), BF),
            pltpu.VMEM((W_ROWS, LANES), BF),
            pltpu.VMEM((2, FIELD_BASE, LANES), BF),
            pltpu.VMEM((SLAB * FY * FZ, LANES), F32),
            pltpu.VMEM((2 * GRAD, LANES), F32),
            dma((4,)), dma((12,)),
        ],
        compiler_params=pltpu.CompilerParams(vmem_limit_bytes=56 * 1024 * 1024),
        cost_estimate=pl.CostEstimate(flops=0, bytes_accessed=5_000_000, transcendentals=0),
    )(full, grads)
    out_field = out.reshape(SLAB, CY, CZ, LANES)
    field_grad = jnp.transpose(field.reshape(FY, FZ, SLAB, LANES), (2, 0, 1, 3))
    inner_grad = jnp.transpose(inner.reshape(3, 3, 3, MID, LANES), (0, 1, 2, 4, 3))
    outer_grad = outer.reshape(3, 3, 3, MID, LANES)
    return (out_field, field_grad, inner_grad, outer_grad)


def solution(mesh):
    return jax.shard_map(
        shards,
        mesh=mesh,
        in_specs=(
            P("gx", None, None, None),
            P(None, None, None, None, "af"),
            P(None, None, None, "af", None),
            P("gx", None, None, None),
        ),
        out_specs=(
            P("gx", None, None, None),
            P("gx", None, None, None),
            P(None, None, None, None, "af"),
            P(None, None, None, "af", None),
        ),
        check_vma=False,
    )
```

```python
import jax
import jax.numpy as jnp
from jax import lax
from jax.experimental import pallas as pl
from jax.experimental.pallas import tpu as pltpu
from jax.sharding import PartitionSpec as P

MESH = pl.DeviceIdType.MESH
BF = jnp.bfloat16
F32 = jnp.float32

SLAB = 4
CY, CZ = 16, 32
PITCH = 48
LANES = 128
MID = 32
TWO = 2 * MID
FY, FZ = 20, 36
HY, DY, OY, GY = 10, 12, 8, 10
DROWS = DY * FZ
BLOCKS = 5
ORDER = (1, 2, 0, 3)

OUT_SLOT = OY * CZ
FIELD_SLOT = 384
AF_ROWS = 2 * (OUT_SLOT + FIELD_SLOT)
AF_PIECES = 2
AF_TOTAL = AF_PIECES * AF_ROWS
OUT_BASE = tuple(slot // 2 * AF_ROWS + slot % 2 * OUT_SLOT for slot in range(SLAB))
FIELD_BASE = tuple(slot // 2 * AF_ROWS + 2 * OUT_SLOT + slot % 2 * FIELD_SLOT for slot in range(SLAB))
GRAD = 27 * MID
W_SLOT = 896
W_PART = W_SLOT // 4


def align(value, by=16):
    return pl.multiple_of(value, by)


def kernel(
    disp, cot, win, wout,
    full_ref, grads_ref,
    raw, D, C, HA, HB, PA, PB, WIN, WOUT, W1T, W1, W2T, W2, AI, AO, DF, FS, EXTRA, B, R, WB, WZ, WC, HS, HL, HF,
    land_af, land_wc, land_z, land_x,
    load_sem, halo_s, halo_r, core_s, core_r, rs_s, rs_r, ag_s, ag_r, ws_s, ws_r, wx_s, wx_r, wg_s, wg_r, store_sem,
):
    gx = lax.axis_index("gx")
    af = lax.axis_index("af")
    core = lax.rem(af, 2)
    y = lax.rem(lax.div(af, 2), 4)
    xl = lax.div(af, 8)
    z = lax.rem(gx, 4)
    xh = lax.div(gx, 4)

    af_peers, z_peers = [], []
    for dx, dy in ((1, 2), (0, 2), (1, 1), (1, 3), (0, 1), (0, 3), (1, 0)):
        x2, y2 = lax.rem(xl + dx, 2), lax.rem(y + dy, 4)
        af_peers.append(((gx, (x2 * 4 + y2) * 2 + core), x2 * 4 + y2))
    for dz in (2, 1, 3):
        z2 = lax.rem(z + dz, 4)
        z_peers.append(((xh * 4 + z2, af), z2))
    x_peer = ((1 - xh) * 4 + z, af)
    other_core = (gx, af + 1 - 2 * core)
    right = (lax.rem(gx + 1, 8), af)
    left = (lax.rem(gx + 7, 8), af)

    cot_lines = pl.ds(2 - 2 * core, HY)
    loads = [
        pltpu.make_async_copy(disp.at[pl.ds(align(core * 8 * FZ * SLAB), DY * FZ * SLAB)], raw, load_sem.at[0]),
        pltpu.make_async_copy(cot.at[:, pl.ds(6 * core, HY)], C.at[pl.ds(2, SLAB), cot_lines], load_sem.at[1]),
        pltpu.make_async_copy(win, WIN.at[core], load_sem.at[2]),
        pltpu.make_async_copy(wout, WOUT.at[core], load_sem.at[3]),
    ]
    for load in loads:
        load.start()
    barrier = pltpu.get_barrier_semaphore()
    peers = [peer for peer, _ in af_peers + z_peers] + [x_peer, other_core, left, right]
    for peer in peers:
        pl.semaphore_signal(barrier, inc=1, device_id=peer, device_id_type=MESH)

    C[:, pl.ds(10 * core, 2)] = jnp.zeros((8, 2, CZ, LANES), BF)
    PA[:, pl.ds(10 * core, 2)] = jnp.zeros((6, 2, PITCH, LANES), BF)
    PB[:, pl.ds(10 * core + 1, 2)] = jnp.zeros((6, 2, PITCH, LANES), BF)
    DF[DROWS * SLAB:, :] = jnp.zeros((SLAB * (PITCH - FZ), LANES), F32)
    HF[DROWS:, :] = jnp.zeros((16, LANES), F32)
    for straight in (W1, W2):
        for a in range(3):
            straight[pl.ds((a * BLOCKS + 4) * LANES + TWO, TWO), :] = jnp.zeros((TWO, LANES), BF)
    AI[...] = jnp.zeros_like(AI)
    AO[...] = jnp.zeros_like(AO)
    for k in range(2):
        for p in range(2):
            WB[k, pl.ds(p * W_SLOT + GRAD, W_SLOT - GRAD), :] = jnp.zeros((W_SLOT - GRAD, LANES), BF)
    for slot in range(SLAB):
        FS[pl.ds(slot * FIELD_SLOT + GY * FZ, FIELD_SLOT - GY * FZ), :] = jnp.zeros(
            (FIELD_SLOT - GY * FZ, LANES), F32
        )

    loads[0].wait()
    line_row = lax.broadcasted_iota(jnp.int32, (PITCH, LANES), 0)

    def widen(i, _):
        rows = pl.ds(align(i * 4 * FZ * SLAB), 4 * FZ * SLAB)
        DF[rows, :] = raw[rows, :].astype(F32)
        return 0

    lax.fori_loop(0, DY // 4, widen, 0)
    for x in range(SLAB):
        HS[x] = DF[pl.ds(x, DROWS, stride=SLAB), :].astype(BF)

    def part(i, _):
        for x in range(SLAB):
            line = DF[pl.ds(i * FZ * SLAB + x, PITCH, stride=SLAB), :]
            D[x + 2, i] = jnp.where(line_row < FZ, line, 0.0).astype(BF)
        return 0

    lax.fori_loop(0, DY, part, 0)
    for load in loads[1:]:
        load.wait()

    def halo(index, src, dst, peer):
        copy = pltpu.make_async_remote_copy(
            src_ref=src, dst_ref=dst, send_sem=halo_s.at[index], recv_sem=halo_r.at[index],
            device_id=peer, device_id_type=MESH,
        )
        copy.start()
        halos.append(copy)
        return copy

    halos = []
    pl.semaphore_wait(barrier, len(peers))
    weights = [
        halo(0, WIN.at[core], WIN.at[core], other_core),
        halo(1, WOUT.at[core], WOUT.at[core], other_core),
    ]
    given = ((3, 1, right), (0, 6, left), (2, 0, right), (1, 7, left))
    first_halos = []
    for k, (x, place, peer) in enumerate(given):
        first_halos.append(
            (
                halo(2 + 2 * k, HS.at[x], HL.at[k], peer),
                halo(3 + 2 * k, C.at[x + 2, cot_lines], C.at[place, cot_lines], peer),
            )
        )

    def extra_out(i, _):
        for slot in range(SLAB):
            EXTRA[pl.ds(align(OUT_BASE[slot] + i * CZ), CZ), :] = DF[
                pl.ds((i + 2) * FZ * SLAB + 2 * SLAB + ORDER[slot], CZ, stride=SLAB), :
            ]
        return 0

    lax.fori_loop(0, OY, extra_out, 0)
    for slot in range(SLAB):
        base = FIELD_BASE[slot]
        EXTRA[pl.ds(base, FIELD_SLOT), :] = jnp.zeros((FIELD_SLOT, LANES), F32)
        for line in range(GY):
            EXTRA[pl.ds(base + line * FZ + 2, CZ), :] = C[ORDER[slot] + 2, 2 * core + line].astype(F32)

    for copy in weights:
        copy.wait_recv()

    def places(blocks_c2):
        table = {(b, c): b * LANES + c * TWO for b in range(3) for c in range(2)}
        for b, row in enumerate(blocks_c2):
            table[b, 2] = row
        return table

    in_places = places((4 * LANES, 3 * LANES + TWO, 3 * LANES))
    out_places = places((3 * LANES, 3 * LANES + TWO, 4 * LANES))
    for src, straight, turned, table in ((WIN, W1, W1T, in_places), (WOUT, W2, W2T, out_places)):
        for a in range(3):
            for (b, c), row in table.items():
                for k in range(2):
                    straight[pl.ds(a * BLOCKS * LANES + row + k * MID, MID), :] = src[
                        k, pl.ds(((a * 3 + b) * 3 + c) * MID, MID), :
                    ]
        for a in range(3):
            for b in range(3):
                rows = pl.ds((a * 3 + b) * LANES, LANES)
                turned[rows, :LANES] = straight[pl.ds((a * BLOCKS + b) * LANES, LANES), :].T
                row = table[b, 2]
                pair = straight[pl.ds(a * BLOCKS * LANES + row // LANES * LANES, LANES), :]
                if row % LANES:
                    pair = jnp.concatenate([pair[TWO:], pair[:TWO]], axis=0)
                turned[rows, LANES:] = pair.T

    def lane_half(values):
        return pltpu.roll(values, TWO, 1)

    def row_roll(values, count):
        return pltpu.roll(values, count % values.shape[0], 0)

    def gather(values, direction):
        near, far = values[:, :LANES], values[:, LANES:]
        return near + row_roll(lane_half(near), -direction) + row_roll(far, -2 * direction)

    def first_mids(values):
        lane = lax.broadcasted_iota(jnp.int32, values.shape, 1)
        return jnp.where(lane < TWO, values, 0.0)

    rows = HY * PITCH

    def store_hidden(plane, hidden):
        near = hidden + lane_half(row_roll(hidden, -1))
        far = row_roll(hidden, -2).reshape(HY, PITCH, LANES)[:, :CZ].reshape(HY * CZ, LANES)
        later = jnp.concatenate([far[CZ:], jnp.zeros((CZ, LANES), F32)], axis=0)
        HA[plane] = near.reshape(HY, PITCH, LANES)[:, :CZ].astype(BF)
        HB[plane] = (far + lane_half(later)).reshape(HY, CZ, LANES).astype(BF)

    def store_grad(plane, grad):
        near = grad + lane_half(row_roll(grad, 1))
        far = row_roll(grad, 2)
        nothing = jnp.zeros((PITCH, LANES), F32)
        both = jnp.concatenate([nothing, far], axis=0) + lane_half(jnp.concatenate([far, nothing], axis=0))
        PA[plane, pl.ds(2 - 2 * core, HY)] = near.reshape(HY, PITCH, LANES).astype(BF)
        PB[plane, pl.ds(2 - 2 * core, HY + 1)] = both.reshape(HY + 1, PITCH, LANES).astype(BF)

    def stage_one(x):
        lhs = jnp.concatenate(
            [D[x + 1 + a, pl.ds(b, HY)].reshape(rows, LANES) for a in range(3) for b in range(3)], axis=1
        )
        pre = gather(jnp.dot(lhs, W1T[...], preferred_element_type=F32), 1)
        lhs = jnp.concatenate(
            [
                C[x + 3 - a, pl.ds(2 - b, HY)].reshape(HY * CZ, LANES)
                for a in range(3)
                for b in range(3)
            ],
            axis=1,
        )
        back = jnp.dot(lhs, W2T[...], preferred_element_type=F32).reshape(HY, CZ, 2 * LANES)
        back = jnp.concatenate([back, jnp.zeros((HY, PITCH - CZ, 2 * LANES), F32)], axis=1)
        grad = gather(back.reshape(rows, 2 * LANES), -1)
        square = pre * pre + 0.01
        inverse = lax.rsqrt(square)
        hidden = first_mids(0.505 * pre + 0.495 * (square * inverse))
        grad = first_mids(grad * (0.505 + 0.495 * (pre * inverse)))
        store_hidden(x + 1, hidden)
        store_grad(x + 1, grad)

    def arrived(k):
        first_halos[k][0].wait_recv()
        HF[0:DROWS, :] = HL[k].astype(F32)
        for line in range(DY):
            value = HF[pl.ds(line * FZ, PITCH), :]
            D[given[k][1], line] = jnp.where(line_row < FZ, value, 0.0).astype(BF)
        first_halos[k][1].wait_recv()

    over_rows = (((0,), (0,)), ((), ()))

    def hidden_blocks(plane):
        blocks = [HA[plane, pl.ds(b, OY)] for b in range(3)] + [HB[plane, pl.ds(b, OY)] for b in (0, 2)]
        return [block.reshape(OUT_SLOT, LANES) for block in blocks]

    def grad_blocks(plane):
        blocks = [PA[plane, pl.ds(2 - b, GY)] for b in range(3)] + [PB[plane, pl.ds(b, GY)] for b in (1, 3)]
        return [block.reshape(GY * PITCH, LANES) for block in blocks]

    def outer_terms(i):
        right_side = jnp.concatenate(
            [C[i + 3 - a, pl.ds(2, OY)].reshape(OUT_SLOT, LANES) for a in range(3)], axis=1
        )
        AO[...] += lax.dot_general(
            jnp.concatenate(hidden_blocks(i + 1), axis=1), right_side, over_rows, preferred_element_type=F32
        )

    def inner_terms(i):
        right_side = jnp.concatenate(
            [D[i + 1 + a, pl.ds(2 * core, GY)].reshape(GY * PITCH, LANES) for a in range(3)], axis=1
        )
        AI[...] += lax.dot_general(
            jnp.concatenate(grad_blocks(i + 1), axis=1), right_side, over_rows, preferred_element_type=F32
        )

    def inner_planes_terms(i, _):
        outer_terms(1 + i)
        inner_terms(1 + i)
        return 0

    stage_one(1)
    stage_one(2)
    lax.fori_loop(0, 2, inner_planes_terms, 0)
    for k, x in ((0, 0), (1, 3)):
        arrived(k)
        stage_one(x)

    sends = []

    def send(src, dst, send_sem, recv_sem, peer):
        copy = pltpu.make_async_remote_copy(
            src_ref=src, dst_ref=dst, send_sem=send_sem, recv_sem=recv_sem, device_id=peer, device_id_type=MESH
        )
        copy.start()
        sends.append(copy)
        return copy

    def scatter(peers, piece, landing, size, sems):
        return [
            send(piece(align(place * size), size), landing(j), sems[0](j), sems[1](j), peer)
            for j, (peer, place) in enumerate(peers)
        ]

    def total(copies, piece, landing, me, size):
        for copy in copies:
            copy.wait_recv()
        value = piece(align(me * size), size)[...].astype(F32)
        for j in range(len(copies)):
            value = value + landing(j)[...].astype(F32)
        return value

    def spread_out(peers, whole, me, size, sems):
        rows = whole(align(me * size), size)
        return [send(rows, rows, sems[0](j), sems[1](j), peer) for j, (peer, _) in enumerate(peers)]

    def keep(src, dst, index):
        store = pltpu.make_async_copy(src, dst, store_sem.at[index])
        store.start()
        stores.append(store)

    class AfSum:
        def __init__(self, p):
            self.p, self.size, self.base = p, AF_ROWS // 8, p * AF_ROWS
            self.me = xl * 4 + y
            self.landing = lambda j: land_af.at[p, j]
            self.step = 0

        def piece(self, off, size):
            return B.at[pl.ds(align(self.base + off), size)]

        def whole(self, off, size):
            return R.at[pl.ds(align(self.base + off), size)]

        def advance(self):
            p, me, size = self.p, self.me, self.size
            if self.step == 0:
                sems = (lambda j: rs_s.at[p, j], lambda j: rs_r.at[p, j])
                self.copies = scatter(af_peers, self.piece, self.landing, size, sems)
            elif self.step == 1:
                value = total(self.copies, self.piece, self.landing, me, size)
                value = value + EXTRA[pl.ds(align(self.base + me * size), size), :]
                self.whole(align(me * size), size)[...] = value.astype(BF)
                sems = (lambda j: ag_s.at[p, j], lambda j: ag_r.at[p, j])
                self.copies = spread_out(af_peers, self.whole, me, size, sems)
            elif self.step == 2:
                for copy in self.copies:
                    copy.wait_recv()
                rows = self.whole(0, AF_ROWS)
                there = full_ref.at[core, pl.ds(self.base, AF_ROWS)]
                self.copies = [send(rows, there, core_s.at[p], core_r.at[p], other_core)]
                keep(rows, there, p)
            else:
                self.copies[0].wait_recv()
            self.step += 1

    class GxSum:
        def __init__(self, p):
            self.p, self.base = p, p * W_SLOT
            self.landing = lambda j: land_z.at[p, j]
            self.step = 0

        def piece(self, off, size):
            return WB.at[core, pl.ds(align(self.base + off), size)]

        def advance(self):
            p, rows = self.p, pl.ds(self.base, W_SLOT)
            if self.step == 0:
                self.copies = [
                    send(WB.at[1 - core, rows], land_wc.at[p], core_s.at[2 + p], core_r.at[2 + p], other_core)
                ]
            elif self.step == 1:
                self.copies[0].wait_recv()
                mine = WB.at[core, rows]
                mine[...] = (mine[...].astype(F32) + land_wc[p].astype(F32)).astype(BF)
                sems = (lambda j: ws_s.at[p, j], lambda j: ws_r.at[p, j])
                self.copies = scatter(z_peers, self.piece, self.landing, W_PART, sems)
            elif self.step == 2:
                WZ[p] = total(self.copies, self.piece, self.landing, z, W_PART).astype(BF)
                self.copies = [send(WZ.at[p], land_x.at[p], wx_s.at[p], wx_r.at[p], x_peer)]
            elif self.step == 3:
                self.copies[0].wait_recv()
                value = WZ[p].astype(F32) + land_x[p].astype(F32)
                WC[p] = value.astype(BF)
                there = grads_ref.at[pl.ds(align(self.base + z * W_PART), W_PART)]
                self.copies = [
                    send(WC.at[p], there, wg_s.at[p, j], wg_r.at[p, j], peer) for j, (peer, _) in enumerate(z_peers)
                ]
                keep(WC.at[p], there, 2 + p)
            else:
                for copy in self.copies:
                    copy.wait_recv()
            self.step += 1

    stores = []
    inner_planes, outer_planes = AfSum(0), AfSum(1)
    inner_sum, outer_sum = GxSum(0), GxSum(1)

    def out_plane(slot):
        i = ORDER[slot]
        lhs = jnp.concatenate([block for a in range(3) for block in hidden_blocks(i + a)], axis=1)
        B[pl.ds(OUT_BASE[slot], OUT_SLOT), :] = jnp.dot(lhs, W2[...], preferred_element_type=F32).astype(BF)

    def field_plane(slot):
        i = ORDER[slot]
        lhs = jnp.concatenate([block for a in range(3) for block in grad_blocks(i + 2 - a)], axis=1)
        block = jnp.dot(lhs, W1[...], preferred_element_type=F32).reshape(GY, PITCH, LANES)
        base = slot * FIELD_SLOT
        for line in range(GY):
            FS[pl.ds(base + line * FZ, FZ), :] = block[line, :FZ]
        B[pl.ds(FIELD_BASE[slot], FIELD_SLOT), :] = FS[pl.ds(base, FIELD_SLOT), :].astype(BF)

    def collect(acc, table, base):
        for a in range(3):
            for (b, c), row in table.items():
                for k in range(2):
                    WB[k, pl.ds(base + ((a * 3 + b) * 3 + c) * MID, MID), :] = acc[
                        pl.ds(row + k * MID, MID), a * LANES : (a + 1) * LANES
                    ].astype(BF)

    def edge_outer():
        outer_terms(0)
        outer_terms(3)
        collect(AO, out_places, W_SLOT)

    def edge_inner():
        inner_terms(0)
        inner_terms(3)
        collect(AI, in_places, 0)

    def far_planes():
        for k, x in ((2, -1), (3, 4)):
            arrived(k)
            stage_one(x)

    edge_outer()
    outer_sum.advance()
    edge_inner()
    inner_sum.advance()
    out_plane(0)
    out_plane(1)
    field_plane(0)
    field_plane(1)
    inner_planes.advance()
    far_planes()
    outer_sum.advance()
    inner_sum.advance()
    out_plane(2)
    out_plane(3)
    field_plane(2)
    field_plane(3)
    outer_planes.advance()
    inner_planes.advance()
    outer_sum.advance()
    inner_sum.advance()
    outer_planes.advance()
    inner_planes.advance()
    outer_sum.advance()
    inner_sum.advance()
    outer_planes.advance()
    inner_planes.advance()
    outer_planes.advance()
    outer_sum.advance()
    inner_sum.advance()
    for store in stores:
        store.wait()
    for copy in halos + sends:
        copy.wait_send()


def finish(full, grads, out_ref, field_ref, inner_ref, outer_ref, f_in, g_in, f_out, w_out, in_sem, out_sem):
    inputs = [pltpu.make_async_copy(full.at[core], f_in.at[core], in_sem.at[core]) for core in range(2)]
    whole = pltpu.make_async_copy(grads, g_in, in_sem.at[2])
    for copy in inputs + [whole]:
        copy.start()
    stores = []

    def store(src, dst):
        copy = pltpu.make_async_copy(src, dst, out_sem.at[len(stores)])
        copy.start()
        stores.append(copy)

    rows = GY * FZ
    for core in range(2):
        inputs[core].wait()
        for slot in range(SLAB):
            f_out[pl.ds(core * rows * SLAB + ORDER[slot], rows, stride=SLAB), :] = f_in[
                core, pl.ds(FIELD_BASE[slot], rows), :
            ].astype(F32)
        part = pl.ds(core * rows * SLAB, rows * SLAB)
        store(f_out.at[part], field_ref.at[part])
        for slot in range(SLAB):
            store(
                f_in.at[core, pl.ds(OUT_BASE[slot], OUT_SLOT)],
                out_ref.at[pl.ds((2 * ORDER[slot] + core) * OUT_SLOT, OUT_SLOT)],
            )
    whole.wait()
    for p, ref in enumerate((inner_ref, outer_ref)):
        part = pl.ds(p * GRAD, GRAD)
        w_out[part, :] = g_in[pl.ds(p * W_SLOT, GRAD), :].astype(F32)
        store(w_out.at[part], ref)
    for copy in stores:
        copy.wait()


def shards(displace, weight_in, weight_out, cotangent):
    hbm = pl.BlockSpec(memory_space=pl.ANY)
    rows = jnp.transpose(displace, (1, 2, 0, 3)).reshape(SLAB * FY * FZ, LANES)
    win = jnp.transpose(weight_in, (0, 1, 2, 4, 3)).reshape(GRAD, LANES)
    wout = weight_out.reshape(GRAD, LANES)
    dma = pltpu.SemaphoreType.DMA
    full, grads = pl.pallas_call(
        kernel,
        out_shape=(
            jax.ShapeDtypeStruct((2, AF_TOTAL, LANES), BF),
            jax.ShapeDtypeStruct((2 * W_SLOT, LANES), BF),
        ),
        in_specs=[hbm] * 4,
        out_specs=[hbm] * 2,
        scratch_shapes=[
            pltpu.VMEM((SLAB * DROWS, LANES), BF),
            pltpu.VMEM((SLAB + 4, DY, PITCH, LANES), BF),
            pltpu.VMEM((SLAB + 4, DY, CZ, LANES), BF),
            pltpu.VMEM((SLAB + 2, HY, CZ, LANES), BF),
            pltpu.VMEM((SLAB + 2, HY, CZ, LANES), BF),
            pltpu.VMEM((SLAB + 2, HY + 2, PITCH, LANES), BF),
            pltpu.VMEM((SLAB + 2, HY + 3, PITCH, LANES), BF),
            pltpu.VMEM((2, GRAD, LANES), BF),
            pltpu.VMEM((2, GRAD, LANES), BF),
            pltpu.VMEM((9 * LANES, 2 * LANES), BF),
            pltpu.VMEM((3 * BLOCKS * LANES, LANES), BF),
            pltpu.VMEM((9 * LANES, 2 * LANES), BF),
            pltpu.VMEM((3 * BLOCKS * LANES, LANES), BF),
            pltpu.VMEM((BLOCKS * LANES, 3 * LANES), F32),
            pltpu.VMEM((BLOCKS * LANES, 3 * LANES), F32),
            pltpu.VMEM((SLAB * (DROWS + PITCH - FZ), LANES), F32),
            pltpu.VMEM((SLAB * FIELD_SLOT, LANES), F32),
            pltpu.VMEM((AF_TOTAL, LANES), F32),
            pltpu.VMEM((AF_TOTAL, LANES), BF),
            pltpu.VMEM((AF_TOTAL, LANES), BF),
            pltpu.VMEM((2, 2 * W_SLOT, LANES), BF),
            pltpu.VMEM((2, W_PART, LANES), BF),
            pltpu.VMEM((2, W_PART, LANES), BF),
            pltpu.VMEM((SLAB, DROWS, LANES), BF),
            pltpu.VMEM((SLAB, DROWS, LANES), BF),
            pltpu.VMEM((DROWS + 16, LANES), F32),
            pltpu.VMEM((AF_PIECES, 7, AF_ROWS // 8, LANES), BF),
            pltpu.VMEM((2, W_SLOT, LANES), BF),
            pltpu.VMEM((2, 3, W_PART, LANES), BF),
            pltpu.VMEM((2, W_PART, LANES), BF),
            dma((4,)), dma((10,)), dma((10,)),
            dma((4,)), dma((4,)), dma((2, 7)), dma((2, 7)), dma((2, 7)), dma((2, 7)),
            dma((2, 3)), dma((2, 3)), dma((2,)), dma((2,)), dma((2, 3)), dma((2, 3)), dma((4,)),
        ],
        compiler_params=pltpu.CompilerParams(
            collective_id=0, has_side_effects=True, vmem_limit_bytes=56 * 1024 * 1024
        ),
        cost_estimate=pl.CostEstimate(flops=4_000_000_000, bytes_accessed=8_000_000, transcendentals=400_000),
    )(rows, cotangent, win, wout)
    out, field, inner, outer = pl.pallas_call(
        finish,
        out_shape=(
            jax.ShapeDtypeStruct((SLAB * CY * CZ, LANES), BF),
            jax.ShapeDtypeStruct((SLAB * FY * FZ, LANES), F32),
            jax.ShapeDtypeStruct((GRAD, LANES), F32),
            jax.ShapeDtypeStruct((GRAD, LANES), F32),
        ),
        in_specs=[hbm] * 2,
        out_specs=[hbm] * 4,
        scratch_shapes=[
            pltpu.VMEM((2, AF_TOTAL, LANES), BF),
            pltpu.VMEM((2 * W_SLOT, LANES), BF),
            pltpu.VMEM((SLAB * FY * FZ, LANES), F32),
            pltpu.VMEM((2 * GRAD, LANES), F32),
            dma((3,)), dma((12,)),
        ],
        compiler_params=pltpu.CompilerParams(vmem_limit_bytes=56 * 1024 * 1024),
        cost_estimate=pl.CostEstimate(flops=0, bytes_accessed=5_000_000, transcendentals=0),
    )(full, grads)
    out_field = out.reshape(SLAB, CY, CZ, LANES)
    field_grad = jnp.transpose(field.reshape(FY, FZ, SLAB, LANES), (2, 0, 1, 3))
    inner_grad = jnp.transpose(inner.reshape(3, 3, 3, MID, LANES), (0, 1, 2, 4, 3))
    outer_grad = outer.reshape(3, 3, 3, MID, LANES)
    return (out_field, field_grad, inner_grad, outer_grad)


def solution(mesh):
    return jax.shard_map(
        shards,
        mesh=mesh,
        in_specs=(
            P("gx", None, None, None),
            P(None, None, None, None, "af"),
            P(None, None, None, "af", None),
            P("gx", None, None, None),
        ),
        out_specs=(
            P("gx", None, None, None),
            P("gx", None, None, None),
            P(None, None, None, None, "af"),
            P(None, None, None, "af", None),
        ),
        check_vma=False,
    )
```

```python
import jax
import jax.numpy as jnp
from jax import lax
from jax.experimental import pallas as pl
from jax.experimental.pallas import tpu as pltpu
from jax.sharding import PartitionSpec as P

MESH = pl.DeviceIdType.MESH
BF = jnp.bfloat16
F32 = jnp.float32

SLAB = 4
CY, CZ = 16, 32
PITCH = 48
LANES = 128
MID = 32
TWO = 2 * MID
FY, FZ = 20, 36
HY, DY, OY, GY = 10, 12, 8, 10
DROWS = DY * FZ
BLOCKS = 5
ORDER = (1, 2, 0, 3)

OUT_SLOT = OY * CZ
FIELD_SLOT = 384
PLANE_ROWS = OUT_SLOT + FIELD_SLOT
AF_ROWS = (2 * PLANE_ROWS, PLANE_ROWS, PLANE_ROWS)
AF_BASE = (0, 2 * PLANE_ROWS, 3 * PLANE_ROWS)
AF_TOTAL = SLAB * PLANE_ROWS
AF_LAND = tuple(7 * base // 8 for base in AF_BASE)
OUT_BASE = tuple(slot * PLANE_ROWS for slot in range(SLAB))
FIELD_BASE = tuple(slot * PLANE_ROWS + OUT_SLOT for slot in range(SLAB))
GRAD = 27 * MID
W_SLOT = 896
W_PART = W_SLOT // 4


def align(value, by=16):
    return pl.multiple_of(value, by)


def kernel(
    disp, cot, win, wout,
    full_ref, grads_ref,
    raw, D, C, HA, HB, PA, PB, WIN, WOUT, W1T, W1, W2T, W2, AI, AO, DF, FS, EXTRA, B, R, WB, WZ, WC, HS, HL, HF,
    land_af, land_wc, land_z, land_x,
    load_sem, halo_s, halo_r, core_s, core_r, rs_s, rs_r, ag_s, ag_r, ws_s, ws_r, wx_s, wx_r, wg_s, wg_r, store_sem,
):
    gx = lax.axis_index("gx")
    af = lax.axis_index("af")
    core = lax.rem(af, 2)
    y = lax.rem(lax.div(af, 2), 4)
    xl = lax.div(af, 8)
    z = lax.rem(gx, 4)
    xh = lax.div(gx, 4)

    af_peers, z_peers = [], []
    for dx, dy in ((1, 2), (0, 2), (1, 1), (1, 3), (0, 1), (0, 3), (1, 0)):
        x2, y2 = lax.rem(xl + dx, 2), lax.rem(y + dy, 4)
        af_peers.append(((gx, (x2 * 4 + y2) * 2 + core), x2 * 4 + y2))
    for dz in (2, 1, 3):
        z2 = lax.rem(z + dz, 4)
        z_peers.append(((xh * 4 + z2, af), z2))
    x_peer = ((1 - xh) * 4 + z, af)
    other_core = (gx, af + 1 - 2 * core)
    right = (lax.rem(gx + 1, 8), af)
    left = (lax.rem(gx + 7, 8), af)

    cot_lines = pl.ds(2 - 2 * core, HY)
    loads = [
        pltpu.make_async_copy(disp.at[pl.ds(align(core * 8 * FZ * SLAB), DY * FZ * SLAB)], raw, load_sem.at[0]),
        pltpu.make_async_copy(cot.at[:, pl.ds(6 * core, HY)], C.at[pl.ds(2, SLAB), cot_lines], load_sem.at[1]),
        pltpu.make_async_copy(win, WIN.at[core], load_sem.at[2]),
        pltpu.make_async_copy(wout, WOUT.at[core], load_sem.at[3]),
    ]
    for load in loads:
        load.start()
    barrier = pltpu.get_barrier_semaphore()
    peers = [peer for peer, _ in af_peers + z_peers] + [x_peer, other_core, left, right]
    for peer in peers:
        pl.semaphore_signal(barrier, inc=1, device_id=peer, device_id_type=MESH)

    C[:, pl.ds(10 * core, 2)] = jnp.zeros((8, 2, CZ, LANES), BF)
    PA[:, pl.ds(10 * core, 2)] = jnp.zeros((6, 2, PITCH, LANES), BF)
    PB[:, pl.ds(10 * core + 1, 2)] = jnp.zeros((6, 2, PITCH, LANES), BF)
    DF[DROWS * SLAB:, :] = jnp.zeros((SLAB * (PITCH - FZ), LANES), F32)
    HF[DROWS:, :] = jnp.zeros((16, LANES), F32)
    for straight in (W1, W2):
        for a in range(3):
            straight[pl.ds((a * BLOCKS + 4) * LANES + TWO, TWO), :] = jnp.zeros((TWO, LANES), BF)
    AI[...] = jnp.zeros_like(AI)
    AO[...] = jnp.zeros_like(AO)
    for k in range(2):
        for p in range(2):
            WB[k, pl.ds(p * W_SLOT + GRAD, W_SLOT - GRAD), :] = jnp.zeros((W_SLOT - GRAD, LANES), BF)
    for slot in range(SLAB):
        FS[pl.ds(slot * FIELD_SLOT + GY * FZ, FIELD_SLOT - GY * FZ), :] = jnp.zeros(
            (FIELD_SLOT - GY * FZ, LANES), F32
        )

    loads[0].wait()
    line_row = lax.broadcasted_iota(jnp.int32, (PITCH, LANES), 0)

    def widen(i, _):
        rows = pl.ds(align(i * 4 * FZ * SLAB), 4 * FZ * SLAB)
        DF[rows, :] = raw[rows, :].astype(F32)
        return 0

    lax.fori_loop(0, DY // 4, widen, 0)
    for x in range(SLAB):
        HS[x] = DF[pl.ds(x, DROWS, stride=SLAB), :].astype(BF)

    def part(i, _):
        for x in range(SLAB):
            line = DF[pl.ds(i * FZ * SLAB + x, PITCH, stride=SLAB), :]
            D[x + 2, i] = jnp.where(line_row < FZ, line, 0.0).astype(BF)
        return 0

    lax.fori_loop(0, DY, part, 0)
    for load in loads[1:]:
        load.wait()

    def halo(index, src, dst, peer):
        copy = pltpu.make_async_remote_copy(
            src_ref=src, dst_ref=dst, send_sem=halo_s.at[index], recv_sem=halo_r.at[index],
            device_id=peer, device_id_type=MESH,
        )
        copy.start()
        halos.append(copy)
        return copy

    halos = []
    pl.semaphore_wait(barrier, len(peers))
    weights = [
        halo(0, WIN.at[core], WIN.at[core], other_core),
        halo(1, WOUT.at[core], WOUT.at[core], other_core),
    ]
    given = ((3, 1, right), (0, 6, left), (2, 0, right), (1, 7, left))
    first_halos = []
    for k, (x, place, peer) in enumerate(given):
        first_halos.append(
            (
                halo(2 + 2 * k, HS.at[x], HL.at[k], peer),
                halo(3 + 2 * k, C.at[x + 2, cot_lines], C.at[place, cot_lines], peer),
            )
        )

    def extra_out(i, _):
        for slot in range(SLAB):
            EXTRA[pl.ds(align(OUT_BASE[slot] + i * CZ), CZ), :] = DF[
                pl.ds((i + 2) * FZ * SLAB + 2 * SLAB + ORDER[slot], CZ, stride=SLAB), :
            ]
        return 0

    lax.fori_loop(0, OY, extra_out, 0)
    for slot in range(SLAB):
        base = FIELD_BASE[slot]
        EXTRA[pl.ds(base, FIELD_SLOT), :] = jnp.zeros((FIELD_SLOT, LANES), F32)
        for line in range(GY):
            EXTRA[pl.ds(base + line * FZ + 2, CZ), :] = C[ORDER[slot] + 2, 2 * core + line].astype(F32)

    for copy in weights:
        copy.wait_recv()

    def places(blocks_c2):
        table = {(b, c): b * LANES + c * TWO for b in range(3) for c in range(2)}
        for b, row in enumerate(blocks_c2):
            table[b, 2] = row
        return table

    in_places = places((4 * LANES, 3 * LANES + TWO, 3 * LANES))
    out_places = places((3 * LANES, 3 * LANES + TWO, 4 * LANES))
    for src, straight, turned, table in ((WIN, W1, W1T, in_places), (WOUT, W2, W2T, out_places)):
        for a in range(3):
            for (b, c), row in table.items():
                for k in range(2):
                    straight[pl.ds(a * BLOCKS * LANES + row + k * MID, MID), :] = src[
                        k, pl.ds(((a * 3 + b) * 3 + c) * MID, MID), :
                    ]
        for a in range(3):
            for b in range(3):
                rows = pl.ds((a * 3 + b) * LANES, LANES)
                turned[rows, :LANES] = straight[pl.ds((a * BLOCKS + b) * LANES, LANES), :].T
                row = table[b, 2]
                pair = straight[pl.ds(a * BLOCKS * LANES + row // LANES * LANES, LANES), :]
                if row % LANES:
                    pair = jnp.concatenate([pair[TWO:], pair[:TWO]], axis=0)
                turned[rows, LANES:] = pair.T

    def lane_half(values):
        return pltpu.roll(values, TWO, 1)

    def row_roll(values, count):
        return pltpu.roll(values, count % values.shape[0], 0)

    def gather(values, direction):
        near, far = values[:, :LANES], values[:, LANES:]
        return near + row_roll(lane_half(near), -direction) + row_roll(far, -2 * direction)

    def first_mids(values):
        lane = lax.broadcasted_iota(jnp.int32, values.shape, 1)
        return jnp.where(lane < TWO, values, 0.0)

    rows = HY * PITCH

    def store_hidden(plane, hidden):
        near = hidden + lane_half(row_roll(hidden, -1))
        far = row_roll(hidden, -2).reshape(HY, PITCH, LANES)[:, :CZ].reshape(HY * CZ, LANES)
        later = jnp.concatenate([far[CZ:], jnp.zeros((CZ, LANES), F32)], axis=0)
        HA[plane] = near.reshape(HY, PITCH, LANES)[:, :CZ].astype(BF)
        HB[plane] = (far + lane_half(later)).reshape(HY, CZ, LANES).astype(BF)

    def store_grad(plane, grad):
        near = grad + lane_half(row_roll(grad, 1))
        far = row_roll(grad, 2)
        nothing = jnp.zeros((PITCH, LANES), F32)
        both = jnp.concatenate([nothing, far], axis=0) + lane_half(jnp.concatenate([far, nothing], axis=0))
        PA[plane, pl.ds(2 - 2 * core, HY)] = near.reshape(HY, PITCH, LANES).astype(BF)
        PB[plane, pl.ds(2 - 2 * core, HY + 1)] = both.reshape(HY + 1, PITCH, LANES).astype(BF)

    def stage_one(x):
        lhs = jnp.concatenate(
            [D[x + 1 + a, pl.ds(b, HY)].reshape(rows, LANES) for a in range(3) for b in range(3)], axis=1
        )
        pre = gather(jnp.dot(lhs, W1T[...], preferred_element_type=F32), 1)
        lhs = jnp.concatenate(
            [
                C[x + 3 - a, pl.ds(2 - b, HY)].reshape(HY * CZ, LANES)
                for a in range(3)
                for b in range(3)
            ],
            axis=1,
        )
        back = jnp.dot(lhs, W2T[...], preferred_element_type=F32).reshape(HY, CZ, 2 * LANES)
        back = jnp.concatenate([back, jnp.zeros((HY, PITCH - CZ, 2 * LANES), F32)], axis=1)
        grad = gather(back.reshape(rows, 2 * LANES), -1)
        square = pre * pre + 0.01
        inverse = lax.rsqrt(square)
        hidden = first_mids(0.505 * pre + 0.495 * (square * inverse))
        grad = first_mids(grad * (0.505 + 0.495 * (pre * inverse)))
        store_hidden(x + 1, hidden)
        store_grad(x + 1, grad)

    def arrived(k):
        first_halos[k][0].wait_recv()
        HF[0:DROWS, :] = HL[k].astype(F32)
        for line in range(DY):
            value = HF[pl.ds(line * FZ, PITCH), :]
            D[given[k][1], line] = jnp.where(line_row < FZ, value, 0.0).astype(BF)
        first_halos[k][1].wait_recv()

    over_rows = (((0,), (0,)), ((), ()))

    def hidden_blocks(plane):
        blocks = [HA[plane, pl.ds(b, OY)] for b in range(3)] + [HB[plane, pl.ds(b, OY)] for b in (0, 2)]
        return [block.reshape(OUT_SLOT, LANES) for block in blocks]

    def grad_blocks(plane):
        blocks = [PA[plane, pl.ds(2 - b, GY)] for b in range(3)] + [PB[plane, pl.ds(b, GY)] for b in (1, 3)]
        return [block.reshape(GY * PITCH, LANES) for block in blocks]

    def outer_terms(i):
        right_side = jnp.concatenate(
            [C[i + 3 - a, pl.ds(2, OY)].reshape(OUT_SLOT, LANES) for a in range(3)], axis=1
        )
        AO[...] += lax.dot_general(
            jnp.concatenate(hidden_blocks(i + 1), axis=1), right_side, over_rows, preferred_element_type=F32
        )

    def inner_terms(i):
        right_side = jnp.concatenate(
            [D[i + 1 + a, pl.ds(2 * core, GY)].reshape(GY * PITCH, LANES) for a in range(3)], axis=1
        )
        AI[...] += lax.dot_general(
            jnp.concatenate(grad_blocks(i + 1), axis=1), right_side, over_rows, preferred_element_type=F32
        )

    def inner_planes_terms(i, _):
        outer_terms(1 + i)
        inner_terms(1 + i)
        return 0

    stage_one(1)
    stage_one(2)
    lax.fori_loop(0, 2, inner_planes_terms, 0)
    for k, x in ((0, 0), (1, 3)):
        arrived(k)
        stage_one(x)

    sends = []

    def send(src, dst, send_sem, recv_sem, peer):
        copy = pltpu.make_async_remote_copy(
            src_ref=src, dst_ref=dst, send_sem=send_sem, recv_sem=recv_sem, device_id=peer, device_id_type=MESH
        )
        copy.start()
        sends.append(copy)
        return copy

    def scatter(peers, piece, landing, size, sems):
        return [
            send(piece(align(place * size), size), landing(j), sems[0](j), sems[1](j), peer)
            for j, (peer, place) in enumerate(peers)
        ]

    def total(copies, piece, landing, me, size):
        for copy in copies:
            copy.wait_recv()
        value = piece(align(me * size), size)[...].astype(F32)
        for j in range(len(copies)):
            value = value + landing(j)[...].astype(F32)
        return value

    def spread_out(peers, whole, me, size, sems):
        rows = whole(align(me * size), size)
        return [send(rows, rows, sems[0](j), sems[1](j), peer) for j, (peer, _) in enumerate(peers)]

    def keep(src, dst, index):
        store = pltpu.make_async_copy(src, dst, store_sem.at[index])
        store.start()
        stores.append(store)

    class AfSum:
        def __init__(self, p):
            self.p, self.rows, self.size, self.base = p, AF_ROWS[p], AF_ROWS[p] // 8, AF_BASE[p]
            self.me = xl * 4 + y
            self.landing = lambda j: land_af.at[pl.ds(AF_LAND[p] + j * self.size, self.size)]
            self.step = 0

        def piece(self, off, size):
            return B.at[pl.ds(align(self.base + off), size)]

        def whole(self, off, size):
            return R.at[pl.ds(align(self.base + off), size)]

        def advance(self):
            p, me, size = self.p, self.me, self.size
            if self.step == 0:
                sems = (lambda j: rs_s.at[p, j], lambda j: rs_r.at[p, j])
                self.copies = scatter(af_peers, self.piece, self.landing, size, sems)
            elif self.step == 1:
                value = total(self.copies, self.piece, self.landing, me, size)
                value = value + EXTRA[pl.ds(align(self.base + me * size), size), :]
                self.whole(align(me * size), size)[...] = value.astype(BF)
                sems = (lambda j: ag_s.at[p, j], lambda j: ag_r.at[p, j])
                self.copies = spread_out(af_peers, self.whole, me, size, sems)
            elif self.step == 2:
                for copy in self.copies:
                    copy.wait_recv()
                rows = self.whole(0, self.rows)
                there = full_ref.at[core, pl.ds(self.base, self.rows)]
                self.copies = [send(rows, there, core_s.at[p], core_r.at[p], other_core)]
                keep(rows, there, p)
            else:
                self.copies[0].wait_recv()
            self.step += 1

    class GxSum:
        def __init__(self, p):
            self.p, self.base = p, p * W_SLOT
            self.landing = lambda j: land_z.at[p, j]
            self.step = 0

        def piece(self, off, size):
            return WB.at[core, pl.ds(align(self.base + off), size)]

        def advance(self):
            p, rows = self.p, pl.ds(self.base, W_SLOT)
            if self.step == 0:
                self.copies = [
                    send(WB.at[1 - core, rows], land_wc.at[p], core_s.at[3 + p], core_r.at[3 + p], other_core)
                ]
            elif self.step == 1:
                self.copies[0].wait_recv()
                mine = WB.at[core, rows]
                mine[...] = (mine[...].astype(F32) + land_wc[p].astype(F32)).astype(BF)
                sems = (lambda j: ws_s.at[p, j], lambda j: ws_r.at[p, j])
                self.copies = scatter(z_peers, self.piece, self.landing, W_PART, sems)
            elif self.step == 2:
                WZ[p] = total(self.copies, self.piece, self.landing, z, W_PART).astype(BF)
                self.copies = [send(WZ.at[p], land_x.at[p], wx_s.at[p], wx_r.at[p], x_peer)]
            elif self.step == 3:
                self.copies[0].wait_recv()
                value = WZ[p].astype(F32) + land_x[p].astype(F32)
                WC[p] = value.astype(BF)
                there = grads_ref.at[pl.ds(align(self.base + z * W_PART), W_PART)]
                self.copies = [
                    send(WC.at[p], there, wg_s.at[p, j], wg_r.at[p, j], peer) for j, (peer, _) in enumerate(z_peers)
                ]
                keep(WC.at[p], there, 3 + p)
            else:
                for copy in self.copies:
                    copy.wait_recv()
            self.step += 1

    stores = []
    inner_planes, low_plane, high_plane = AfSum(0), AfSum(1), AfSum(2)
    inner_sum, outer_sum = GxSum(0), GxSum(1)

    def out_plane(slot):
        i = ORDER[slot]
        lhs = jnp.concatenate([block for a in range(3) for block in hidden_blocks(i + a)], axis=1)
        B[pl.ds(OUT_BASE[slot], OUT_SLOT), :] = jnp.dot(lhs, W2[...], preferred_element_type=F32).astype(BF)

    def field_plane(slot):
        i = ORDER[slot]
        lhs = jnp.concatenate([block for a in range(3) for block in grad_blocks(i + 2 - a)], axis=1)
        block = jnp.dot(lhs, W1[...], preferred_element_type=F32).reshape(GY, PITCH, LANES)
        base = slot * FIELD_SLOT
        for line in range(GY):
            FS[pl.ds(base + line * FZ, FZ), :] = block[line, :FZ]
        B[pl.ds(FIELD_BASE[slot], FIELD_SLOT), :] = FS[pl.ds(base, FIELD_SLOT), :].astype(BF)

    def collect(acc, table, base):
        for a in range(3):
            for (b, c), row in table.items():
                for k in range(2):
                    WB[k, pl.ds(base + ((a * 3 + b) * 3 + c) * MID, MID), :] = acc[
                        pl.ds(row + k * MID, MID), a * LANES : (a + 1) * LANES
                    ].astype(BF)

    def edge_outer():
        outer_terms(0)
        outer_terms(3)
        collect(AO, out_places, W_SLOT)

    def edge_inner():
        inner_terms(0)
        inner_terms(3)
        collect(AI, in_places, 0)

    def far_plane(k, x):
        arrived(k)
        stage_one(x)

    edge_outer()
    outer_sum.advance()
    out_plane(0)
    out_plane(1)
    field_plane(0)
    field_plane(1)
    inner_planes.advance()
    edge_inner()
    inner_sum.advance()
    far_plane(2, -1)
    out_plane(2)
    field_plane(2)
    low_plane.advance()
    outer_sum.advance()
    inner_sum.advance()
    far_plane(3, 4)
    out_plane(3)
    field_plane(3)
    high_plane.advance()
    inner_planes.advance()
    outer_sum.advance()
    inner_sum.advance()
    low_plane.advance()
    high_plane.advance()
    inner_planes.advance()
    outer_sum.advance()
    inner_sum.advance()
    low_plane.advance()
    high_plane.advance()
    inner_planes.advance()
    low_plane.advance()
    high_plane.advance()
    outer_sum.advance()
    inner_sum.advance()
    for store in stores:
        store.wait()
    for copy in halos + sends:
        copy.wait_send()


def finish(full, grads, out_ref, field_ref, inner_ref, outer_ref, f_in, g_in, f_out, w_out, in_sem, out_sem):
    inputs = [
        [
            pltpu.make_async_copy(
                full.at[core, pl.ds(slot * PLANE_ROWS, PLANE_ROWS)],
                f_in.at[core, pl.ds(slot * PLANE_ROWS, PLANE_ROWS)],
                in_sem.at[core, slot],
            )
            for slot in range(SLAB)
        ]
        for core in range(2)
    ]
    whole = pltpu.make_async_copy(grads, g_in, in_sem.at[2, 0])
    for copy in inputs[0] + inputs[1] + [whole]:
        copy.start()
    stores = []

    def store(src, dst):
        copy = pltpu.make_async_copy(src, dst, out_sem.at[len(stores)])
        copy.start()
        stores.append(copy)

    rows = GY * FZ
    for core in range(2):
        for slot in range(SLAB):
            inputs[core][slot].wait()
            f_out[pl.ds(core * rows * SLAB + ORDER[slot], rows, stride=SLAB), :] = f_in[
                core, pl.ds(FIELD_BASE[slot], rows), :
            ].astype(F32)
        part = pl.ds(core * rows * SLAB, rows * SLAB)
        store(f_out.at[part], field_ref.at[part])
        for slot in range(SLAB):
            store(
                f_in.at[core, pl.ds(OUT_BASE[slot], OUT_SLOT)],
                out_ref.at[pl.ds((2 * ORDER[slot] + core) * OUT_SLOT, OUT_SLOT)],
            )
    whole.wait()
    for p, ref in enumerate((inner_ref, outer_ref)):
        part = pl.ds(p * GRAD, GRAD)
        w_out[part, :] = g_in[pl.ds(p * W_SLOT, GRAD), :].astype(F32)
        store(w_out.at[part], ref)
    for copy in stores:
        copy.wait()


def shards(displace, weight_in, weight_out, cotangent):
    hbm = pl.BlockSpec(memory_space=pl.ANY)
    rows = jnp.transpose(displace, (1, 2, 0, 3)).reshape(SLAB * FY * FZ, LANES)
    win = jnp.transpose(weight_in, (0, 1, 2, 4, 3)).reshape(GRAD, LANES)
    wout = weight_out.reshape(GRAD, LANES)
    dma = pltpu.SemaphoreType.DMA
    full, grads = pl.pallas_call(
        kernel,
        out_shape=(
            jax.ShapeDtypeStruct((2, AF_TOTAL, LANES), BF),
            jax.ShapeDtypeStruct((2 * W_SLOT, LANES), BF),
        ),
        in_specs=[hbm] * 4,
        out_specs=[hbm] * 2,
        scratch_shapes=[
            pltpu.VMEM((SLAB * DROWS, LANES), BF),
            pltpu.VMEM((SLAB + 4, DY, PITCH, LANES), BF),
            pltpu.VMEM((SLAB + 4, DY, CZ, LANES), BF),
            pltpu.VMEM((SLAB + 2, HY, CZ, LANES), BF),
            pltpu.VMEM((SLAB + 2, HY, CZ, LANES), BF),
            pltpu.VMEM((SLAB + 2, HY + 2, PITCH, LANES), BF),
            pltpu.VMEM((SLAB + 2, HY + 3, PITCH, LANES), BF),
            pltpu.VMEM((2, GRAD, LANES), BF),
            pltpu.VMEM((2, GRAD, LANES), BF),
            pltpu.VMEM((9 * LANES, 2 * LANES), BF),
            pltpu.VMEM((3 * BLOCKS * LANES, LANES), BF),
            pltpu.VMEM((9 * LANES, 2 * LANES), BF),
            pltpu.VMEM((3 * BLOCKS * LANES, LANES), BF),
            pltpu.VMEM((BLOCKS * LANES, 3 * LANES), F32),
            pltpu.VMEM((BLOCKS * LANES, 3 * LANES), F32),
            pltpu.VMEM((SLAB * (DROWS + PITCH - FZ), LANES), F32),
            pltpu.VMEM((SLAB * FIELD_SLOT, LANES), F32),
            pltpu.VMEM((AF_TOTAL, LANES), F32),
            pltpu.VMEM((AF_TOTAL, LANES), BF),
            pltpu.VMEM((AF_TOTAL, LANES), BF),
            pltpu.VMEM((2, 2 * W_SLOT, LANES), BF),
            pltpu.VMEM((2, W_PART, LANES), BF),
            pltpu.VMEM((2, W_PART, LANES), BF),
            pltpu.VMEM((SLAB, DROWS, LANES), BF),
            pltpu.VMEM((SLAB, DROWS, LANES), BF),
            pltpu.VMEM((DROWS + 16, LANES), F32),
            pltpu.VMEM((7 * AF_TOTAL // 8, LANES), BF),
            pltpu.VMEM((2, W_SLOT, LANES), BF),
            pltpu.VMEM((2, 3, W_PART, LANES), BF),
            pltpu.VMEM((2, W_PART, LANES), BF),
            dma((4,)), dma((10,)), dma((10,)),
            dma((5,)), dma((5,)), dma((3, 7)), dma((3, 7)), dma((3, 7)), dma((3, 7)),
            dma((2, 3)), dma((2, 3)), dma((2,)), dma((2,)), dma((2, 3)), dma((2, 3)), dma((5,)),
        ],
        compiler_params=pltpu.CompilerParams(
            collective_id=0, has_side_effects=True, vmem_limit_bytes=56 * 1024 * 1024
        ),
        cost_estimate=pl.CostEstimate(flops=4_000_000_000, bytes_accessed=8_000_000, transcendentals=400_000),
    )(rows, cotangent, win, wout)
    out, field, inner, outer = pl.pallas_call(
        finish,
        out_shape=(
            jax.ShapeDtypeStruct((SLAB * CY * CZ, LANES), BF),
            jax.ShapeDtypeStruct((SLAB * FY * FZ, LANES), F32),
            jax.ShapeDtypeStruct((GRAD, LANES), F32),
            jax.ShapeDtypeStruct((GRAD, LANES), F32),
        ),
        in_specs=[hbm] * 2,
        out_specs=[hbm] * 4,
        scratch_shapes=[
            pltpu.VMEM((2, AF_TOTAL, LANES), BF),
            pltpu.VMEM((2 * W_SLOT, LANES), BF),
            pltpu.VMEM((SLAB * FY * FZ, LANES), F32),
            pltpu.VMEM((2 * GRAD, LANES), F32),
            dma((3, SLAB)), dma((12,)),
        ],
        compiler_params=pltpu.CompilerParams(vmem_limit_bytes=56 * 1024 * 1024),
        cost_estimate=pl.CostEstimate(flops=0, bytes_accessed=5_000_000, transcendentals=0),
    )(full, grads)
    out_field = out.reshape(SLAB, CY, CZ, LANES)
    field_grad = jnp.transpose(field.reshape(FY, FZ, SLAB, LANES), (2, 0, 1, 3))
    inner_grad = jnp.transpose(inner.reshape(3, 3, 3, MID, LANES), (0, 1, 2, 4, 3))
    outer_grad = outer.reshape(3, 3, 3, MID, LANES)
    return (out_field, field_grad, inner_grad, outer_grad)


def solution(mesh):
    return jax.shard_map(
        shards,
        mesh=mesh,
        in_specs=(
            P("gx", None, None, None),
            P(None, None, None, None, "af"),
            P(None, None, None, "af", None),
            P("gx", None, None, None),
        ),
        out_specs=(
            P("gx", None, None, None),
            P("gx", None, None, None),
            P(None, None, None, None, "af"),
            P(None, None, None, "af", None),
        ),
        check_vma=False,
    )
```

```python
import jax
import jax.numpy as jnp
from jax import lax
from jax.experimental import pallas as pl
from jax.experimental.pallas import tpu as pltpu
from jax.sharding import PartitionSpec as P

MESH = pl.DeviceIdType.MESH
BF = jnp.bfloat16
F32 = jnp.float32

SLAB = 4
CY, CZ = 16, 32
PITCH = 48
LANES = 128
MID = 32
TWO = 2 * MID
FY, FZ = 20, 36
HY, DY, OY, GY = 10, 12, 8, 10
DROWS = DY * FZ
BLOCKS = 5
ORDER = (1, 2, 0, 3)

OUT_SLOT = OY * CZ
FIELD_SLOT = 384
PLANE_ROWS = OUT_SLOT + FIELD_SLOT
AF_ROWS = (2 * PLANE_ROWS, PLANE_ROWS, PLANE_ROWS)
AF_BASE = (0, 2 * PLANE_ROWS, 3 * PLANE_ROWS)
AF_TOTAL = SLAB * PLANE_ROWS
AF_LAND = tuple(7 * base // 8 for base in AF_BASE)
OUT_BASE = tuple(slot * PLANE_ROWS for slot in range(SLAB))
FIELD_BASE = tuple(slot * PLANE_ROWS + OUT_SLOT for slot in range(SLAB))
GRAD = 27 * MID
W_SLOT = 896
W_PART = W_SLOT // 4


def align(value, by=16):
    return pl.multiple_of(value, by)


def kernel(
    disp, cot, win, wout,
    full_ref, grads_ref,
    raw, D, C, HA, HB, PA, PB, WIN, WOUT, W1T, W1, W2T, W2, AI, AO, DF, FS, EXTRA, B, R, WB, WZ, WC, HS, HL, HF,
    land_af, land_wc, land_z, land_x,
    load_sem, halo_s, halo_r, core_s, core_r, rs_s, rs_r, ag_s, ag_r, ws_s, ws_r, wx_s, wx_r, wg_s, wg_r, store_sem,
):
    gx = lax.axis_index("gx")
    af = lax.axis_index("af")
    core = lax.rem(af, 2)
    y = lax.rem(lax.div(af, 2), 4)
    xl = lax.div(af, 8)
    z = lax.rem(gx, 4)
    xh = lax.div(gx, 4)

    af_peers, z_peers = [], []
    for dx, dy in ((1, 2), (0, 2), (1, 1), (1, 3), (0, 1), (0, 3), (1, 0)):
        x2, y2 = lax.rem(xl + dx, 2), lax.rem(y + dy, 4)
        af_peers.append(((gx, (x2 * 4 + y2) * 2 + core), x2 * 4 + y2))
    for dz in (2, 1, 3):
        z2 = lax.rem(z + dz, 4)
        z_peers.append(((xh * 4 + z2, af), z2))
    x_peer = ((1 - xh) * 4 + z, af)
    other_core = (gx, af + 1 - 2 * core)
    right = (lax.rem(gx + 1, 8), af)
    left = (lax.rem(gx + 7, 8), af)

    cot_lines = pl.ds(2 - 2 * core, HY)
    loads = [
        pltpu.make_async_copy(disp.at[pl.ds(align(core * 8 * FZ * SLAB), DY * FZ * SLAB)], raw, load_sem.at[0]),
        pltpu.make_async_copy(cot.at[:, pl.ds(6 * core, HY)], C.at[pl.ds(2, SLAB), cot_lines], load_sem.at[1]),
        pltpu.make_async_copy(win, WIN.at[core], load_sem.at[2]),
        pltpu.make_async_copy(wout, WOUT.at[core], load_sem.at[3]),
    ]
    for load in loads:
        load.start()
    barrier = pltpu.get_barrier_semaphore()
    peers = [peer for peer, _ in af_peers + z_peers] + [x_peer, other_core, left, right]
    for peer in peers:
        pl.semaphore_signal(barrier, inc=1, device_id=peer, device_id_type=MESH)

    C[:, pl.ds(10 * core, 2)] = jnp.zeros((8, 2, CZ, LANES), BF)
    PA[:, pl.ds(10 * core, 2)] = jnp.zeros((6, 2, PITCH, LANES), BF)
    PB[:, pl.ds(10 * core + 1, 2)] = jnp.zeros((6, 2, PITCH, LANES), BF)
    DF[DROWS * SLAB:, :] = jnp.zeros((SLAB * (PITCH - FZ), LANES), F32)
    HF[DROWS:, :] = jnp.zeros((16, LANES), F32)
    for straight in (W1, W2):
        for a in range(3):
            straight[pl.ds((a * BLOCKS + 4) * LANES + TWO, TWO), :] = jnp.zeros((TWO, LANES), BF)
    AI[...] = jnp.zeros_like(AI)
    AO[...] = jnp.zeros_like(AO)
    for k in range(2):
        for p in range(2):
            WB[k, pl.ds(p * W_SLOT + GRAD, W_SLOT - GRAD), :] = jnp.zeros((W_SLOT - GRAD, LANES), BF)
    for slot in range(SLAB):
        FS[pl.ds(slot * FIELD_SLOT + GY * FZ, FIELD_SLOT - GY * FZ), :] = jnp.zeros(
            (FIELD_SLOT - GY * FZ, LANES), F32
        )

    loads[0].wait()
    line_row = lax.broadcasted_iota(jnp.int32, (PITCH, LANES), 0)

    def widen(i, _):
        rows = pl.ds(align(i * 4 * FZ * SLAB), 4 * FZ * SLAB)
        DF[rows, :] = raw[rows, :].astype(F32)
        return 0

    lax.fori_loop(0, DY // 4, widen, 0)
    for x in range(SLAB):
        HS[x] = DF[pl.ds(x, DROWS, stride=SLAB), :].astype(BF)

    def part(i, _):
        for x in range(SLAB):
            line = DF[pl.ds(i * FZ * SLAB + x, PITCH, stride=SLAB), :]
            D[x + 2, i] = jnp.where(line_row < FZ, line, 0.0).astype(BF)
        return 0

    lax.fori_loop(0, DY, part, 0)
    for load in loads[1:]:
        load.wait()

    def halo(index, src, dst, peer):
        copy = pltpu.make_async_remote_copy(
            src_ref=src, dst_ref=dst, send_sem=halo_s.at[index], recv_sem=halo_r.at[index],
            device_id=peer, device_id_type=MESH,
        )
        copy.start()
        halos.append(copy)
        return copy

    halos = []
    pl.semaphore_wait(barrier, len(peers))
    weights = [
        halo(0, WIN.at[core], WIN.at[core], other_core),
        halo(1, WOUT.at[core], WOUT.at[core], other_core),
    ]
    given = ((3, 1, right), (0, 6, left), (2, 0, right), (1, 7, left))
    first_halos = []
    for k, (x, place, peer) in enumerate(given):
        first_halos.append(
            (
                halo(2 + 2 * k, HS.at[x], HL.at[k], peer),
                halo(3 + 2 * k, C.at[x + 2, cot_lines], C.at[place, cot_lines], peer),
            )
        )

    def extra_out(i, _):
        for slot in range(SLAB):
            EXTRA[pl.ds(align(OUT_BASE[slot] + i * CZ), CZ), :] = DF[
                pl.ds((i + 2) * FZ * SLAB + 2 * SLAB + ORDER[slot], CZ, stride=SLAB), :
            ]
        return 0

    lax.fori_loop(0, OY, extra_out, 0)
    for slot in range(SLAB):
        base = FIELD_BASE[slot]
        EXTRA[pl.ds(base, FIELD_SLOT), :] = jnp.zeros((FIELD_SLOT, LANES), F32)
        for line in range(GY):
            EXTRA[pl.ds(base + line * FZ + 2, CZ), :] = C[ORDER[slot] + 2, 2 * core + line].astype(F32)

    for copy in weights:
        copy.wait_recv()

    def places(blocks_c2):
        table = {(b, c): b * LANES + c * TWO for b in range(3) for c in range(2)}
        for b, row in enumerate(blocks_c2):
            table[b, 2] = row
        return table

    in_places = places((4 * LANES, 3 * LANES + TWO, 3 * LANES))
    out_places = places((3 * LANES, 3 * LANES + TWO, 4 * LANES))
    for src, straight, turned, table in ((WIN, W1, W1T, in_places), (WOUT, W2, W2T, out_places)):
        for a in range(3):
            for (b, c), row in table.items():
                for k in range(2):
                    straight[pl.ds(a * BLOCKS * LANES + row + k * MID, MID), :] = src[
                        k, pl.ds(((a * 3 + b) * 3 + c) * MID, MID), :
                    ]
        for a in range(3):
            for b in range(3):
                rows = pl.ds((a * 3 + b) * LANES, LANES)
                turned[rows, :LANES] = straight[pl.ds((a * BLOCKS + b) * LANES, LANES), :].T
                row = table[b, 2]
                pair = straight[pl.ds(a * BLOCKS * LANES + row // LANES * LANES, LANES), :]
                if row % LANES:
                    pair = jnp.concatenate([pair[TWO:], pair[:TWO]], axis=0)
                turned[rows, LANES:] = pair.T

    def lane_half(values):
        return pltpu.roll(values, TWO, 1)

    def row_roll(values, count):
        return pltpu.roll(values, count % values.shape[0], 0)

    def gather(values, direction):
        near, far = values[:, :LANES], values[:, LANES:]
        return near + row_roll(lane_half(near), -direction) + row_roll(far, -2 * direction)

    def first_mids(values):
        lane = lax.broadcasted_iota(jnp.int32, values.shape, 1)
        return jnp.where(lane < TWO, values, 0.0)

    rows = HY * PITCH

    def store_hidden(plane, hidden):
        near = hidden + lane_half(row_roll(hidden, -1))
        far = row_roll(hidden, -2).reshape(HY, PITCH, LANES)[:, :CZ].reshape(HY * CZ, LANES)
        later = jnp.concatenate([far[CZ:], jnp.zeros((CZ, LANES), F32)], axis=0)
        HA[plane] = near.reshape(HY, PITCH, LANES)[:, :CZ].astype(BF)
        HB[plane] = (far + lane_half(later)).reshape(HY, CZ, LANES).astype(BF)

    def store_grad(plane, grad):
        near = grad + lane_half(row_roll(grad, 1))
        far = row_roll(grad, 2)
        nothing = jnp.zeros((PITCH, LANES), F32)
        both = jnp.concatenate([nothing, far], axis=0) + lane_half(jnp.concatenate([far, nothing], axis=0))
        PA[plane, pl.ds(2 - 2 * core, HY)] = near.reshape(HY, PITCH, LANES).astype(BF)
        PB[plane, pl.ds(2 - 2 * core, HY + 1)] = both.reshape(HY + 1, PITCH, LANES).astype(BF)

    def stage_one(x):
        lhs = jnp.concatenate(
            [D[x + 1 + a, pl.ds(b, HY)].reshape(rows, LANES) for a in range(3) for b in range(3)], axis=1
        )
        pre = gather(jnp.dot(lhs, W1T[...], preferred_element_type=F32), 1)
        lhs = jnp.concatenate(
            [
                C[x + 3 - a, pl.ds(2 - b, HY)].reshape(HY * CZ, LANES)
                for a in range(3)
                for b in range(3)
            ],
            axis=1,
        )
        back = jnp.dot(lhs, W2T[...], preferred_element_type=F32).reshape(HY, CZ, 2 * LANES)
        back = jnp.concatenate([back, jnp.zeros((HY, PITCH - CZ, 2 * LANES), F32)], axis=1)
        grad = gather(back.reshape(rows, 2 * LANES), -1)
        square = pre * pre + 0.01
        inverse = lax.rsqrt(square)
        hidden = first_mids(0.505 * pre + 0.495 * (square * inverse))
        grad = first_mids(grad * (0.505 + 0.495 * (pre * inverse)))
        store_hidden(x + 1, hidden)
        store_grad(x + 1, grad)

    def arrived(k):
        first_halos[k][0].wait_recv()
        HF[0:DROWS, :] = HL[k].astype(F32)
        for line in range(DY):
            value = HF[pl.ds(line * FZ, PITCH), :]
            D[given[k][1], line] = jnp.where(line_row < FZ, value, 0.0).astype(BF)
        first_halos[k][1].wait_recv()

    over_rows = (((0,), (0,)), ((), ()))

    def hidden_blocks(plane):
        blocks = [HA[plane, pl.ds(b, OY)] for b in range(3)] + [HB[plane, pl.ds(b, OY)] for b in (0, 2)]
        return [block.reshape(OUT_SLOT, LANES) for block in blocks]

    def grad_blocks(plane):
        blocks = [PA[plane, pl.ds(2 - b, GY)] for b in range(3)] + [PB[plane, pl.ds(b, GY)] for b in (1, 3)]
        return [block.reshape(GY * PITCH, LANES) for block in blocks]

    def outer_terms(i):
        right_side = jnp.concatenate(
            [C[i + 3 - a, pl.ds(2, OY)].reshape(OUT_SLOT, LANES) for a in range(3)], axis=1
        )
        AO[...] += lax.dot_general(
            jnp.concatenate(hidden_blocks(i + 1), axis=1), right_side, over_rows, preferred_element_type=F32
        )

    def inner_terms(i):
        right_side = jnp.concatenate(
            [D[i + 1 + a, pl.ds(2 * core, GY)].reshape(GY * PITCH, LANES) for a in range(3)], axis=1
        )
        AI[...] += lax.dot_general(
            jnp.concatenate(grad_blocks(i + 1), axis=1), right_side, over_rows, preferred_element_type=F32
        )

    def inner_planes_terms(i, _):
        outer_terms(1 + i)
        inner_terms(1 + i)
        return 0

    stage_one(1)
    stage_one(2)
    lax.fori_loop(0, 2, inner_planes_terms, 0)
    for k, x in ((0, 0), (1, 3)):
        arrived(k)
        stage_one(x)

    def send(src, dst, send_sem, recv_sem, peer):
        copy = pltpu.make_async_remote_copy(
            src_ref=src, dst_ref=dst, send_sem=send_sem, recv_sem=recv_sem, device_id=peer, device_id_type=MESH
        )
        copy.start()
        return copy

    def scatter(peers, piece, landing, size, sems):
        return [
            send(piece(align(place * size), size), landing(j), sems[0](j), sems[1](j), peer)
            for j, (peer, place) in enumerate(peers)
        ]

    def total(copies, piece, landing, me, size):
        for copy in copies:
            copy.wait_recv()
        value = piece(align(me * size), size)[...].astype(F32)
        for j in range(len(copies)):
            value = value + landing(j)[...].astype(F32)
        return value

    def spread_out(peers, whole, me, size, sems):
        rows = whole(align(me * size), size)
        return [send(rows, rows, sems[0](j), sems[1](j), peer) for j, (peer, _) in enumerate(peers)]

    def keep(src, dst, index):
        store = pltpu.make_async_copy(src, dst, store_sem.at[index])
        store.start()
        stores.append(store)

    class Sum:
        def __init__(self):
            self.step, self.copies, self.before = 0, [], []

        def advance(self):
            for copy in self.before:
                copy.wait_send()
            self.before = self.copies
            self.take()
            self.step += 1

    class AfSum(Sum):
        def __init__(self, p):
            self.p, self.rows, self.size, self.base = p, AF_ROWS[p], AF_ROWS[p] // 8, AF_BASE[p]
            self.me = xl * 4 + y
            self.landing = lambda j: land_af.at[pl.ds(AF_LAND[p] + j * self.size, self.size)]
            super().__init__()

        def piece(self, off, size):
            return B.at[pl.ds(align(self.base + off), size)]

        def whole(self, off, size):
            return R.at[pl.ds(align(self.base + off), size)]

        def take(self):
            p, me, size = self.p, self.me, self.size
            if self.step == 0:
                sems = (lambda j: rs_s.at[p, j], lambda j: rs_r.at[p, j])
                self.copies = scatter(af_peers, self.piece, self.landing, size, sems)
            elif self.step == 1:
                value = total(self.copies, self.piece, self.landing, me, size)
                value = value + EXTRA[pl.ds(align(self.base + me * size), size), :]
                self.whole(align(me * size), size)[...] = value.astype(BF)
                sems = (lambda j: ag_s.at[p, j], lambda j: ag_r.at[p, j])
                self.copies = spread_out(af_peers, self.whole, me, size, sems)
            elif self.step == 2:
                for copy in self.copies:
                    copy.wait_recv()
                rows = self.whole(0, self.rows)
                there = full_ref.at[core, pl.ds(self.base, self.rows)]
                self.copies = [send(rows, there, core_s.at[p], core_r.at[p], other_core)]
                keep(rows, there, p)
            else:
                self.copies[0].wait_recv()

    class GxSum(Sum):
        def __init__(self, p):
            self.p, self.base = p, p * W_SLOT
            self.landing = lambda j: land_z.at[p, j]
            super().__init__()

        def piece(self, off, size):
            return WB.at[core, pl.ds(align(self.base + off), size)]

        def take(self):
            p, rows = self.p, pl.ds(self.base, W_SLOT)
            if self.step == 0:
                self.copies = [
                    send(WB.at[1 - core, rows], land_wc.at[p], core_s.at[3 + p], core_r.at[3 + p], other_core)
                ]
            elif self.step == 1:
                self.copies[0].wait_recv()
                mine = WB.at[core, rows]
                mine[...] = (mine[...].astype(F32) + land_wc[p].astype(F32)).astype(BF)
                sems = (lambda j: ws_s.at[p, j], lambda j: ws_r.at[p, j])
                self.copies = scatter(z_peers, self.piece, self.landing, W_PART, sems)
            elif self.step == 2:
                WZ[p] = total(self.copies, self.piece, self.landing, z, W_PART).astype(BF)
                self.copies = [send(WZ.at[p], land_x.at[p], wx_s.at[p], wx_r.at[p], x_peer)]
            elif self.step == 3:
                self.copies[0].wait_recv()
                value = WZ[p].astype(F32) + land_x[p].astype(F32)
                WC[p] = value.astype(BF)
                there = grads_ref.at[pl.ds(align(self.base + z * W_PART), W_PART)]
                self.copies = [
                    send(WC.at[p], there, wg_s.at[p, j], wg_r.at[p, j], peer) for j, (peer, _) in enumerate(z_peers)
                ]
                keep(WC.at[p], there, 3 + p)
            else:
                for copy in self.copies:
                    copy.wait_recv()

    stores = []
    inner_planes, low_plane, high_plane = AfSum(0), AfSum(1), AfSum(2)
    inner_sum, outer_sum = GxSum(0), GxSum(1)

    def out_plane(slot):
        i = ORDER[slot]
        lhs = jnp.concatenate([block for a in range(3) for block in hidden_blocks(i + a)], axis=1)
        B[pl.ds(OUT_BASE[slot], OUT_SLOT), :] = jnp.dot(lhs, W2[...], preferred_element_type=F32).astype(BF)

    def field_plane(slot):
        i = ORDER[slot]
        lhs = jnp.concatenate([block for a in range(3) for block in grad_blocks(i + 2 - a)], axis=1)
        block = jnp.dot(lhs, W1[...], preferred_element_type=F32).reshape(GY, PITCH, LANES)
        base = slot * FIELD_SLOT
        for line in range(GY):
            FS[pl.ds(base + line * FZ, FZ), :] = block[line, :FZ]
        B[pl.ds(FIELD_BASE[slot], FIELD_SLOT), :] = FS[pl.ds(base, FIELD_SLOT), :].astype(BF)

    def collect(acc, table, base):
        for a in range(3):
            for (b, c), row in table.items():
                for k in range(2):
                    WB[k, pl.ds(base + ((a * 3 + b) * 3 + c) * MID, MID), :] = acc[
                        pl.ds(row + k * MID, MID), a * LANES : (a + 1) * LANES
                    ].astype(BF)

    def edge_outer():
        outer_terms(0)
        outer_terms(3)
        collect(AO, out_places, W_SLOT)

    def edge_inner():
        inner_terms(0)
        inner_terms(3)
        collect(AI, in_places, 0)

    def far_plane(k, x):
        arrived(k)
        stage_one(x)

    edge_outer()
    outer_sum.advance()
    out_plane(0)
    out_plane(1)
    field_plane(0)
    field_plane(1)
    inner_planes.advance()
    edge_inner()
    inner_sum.advance()
    far_plane(2, -1)
    out_plane(2)
    field_plane(2)
    low_plane.advance()
    outer_sum.advance()
    inner_sum.advance()
    far_plane(3, 4)
    out_plane(3)
    field_plane(3)
    high_plane.advance()
    for copy in halos:
        copy.wait_send()
    inner_planes.advance()
    outer_sum.advance()
    inner_sum.advance()
    low_plane.advance()
    high_plane.advance()
    inner_planes.advance()
    outer_sum.advance()
    inner_sum.advance()
    low_plane.advance()
    high_plane.advance()
    inner_planes.advance()
    low_plane.advance()
    high_plane.advance()
    outer_sum.advance()
    inner_sum.advance()
    for store in stores:
        store.wait()
    for item in (inner_planes, low_plane, high_plane, inner_sum, outer_sum):
        for copy in item.before:
            copy.wait_send()


def finish(full, grads, out_ref, field_ref, inner_ref, outer_ref, f_in, g_in, f_out, w_out, in_sem, out_sem):
    inputs = [pltpu.make_async_copy(full.at[core], f_in.at[core], in_sem.at[core]) for core in range(2)]
    whole = pltpu.make_async_copy(grads, g_in, in_sem.at[2])
    for copy in inputs + [whole]:
        copy.start()
    stores = []

    def store(src, dst):
        copy = pltpu.make_async_copy(src, dst, out_sem.at[len(stores)])
        copy.start()
        stores.append(copy)

    rows = GY * FZ
    for core in range(2):
        inputs[core].wait()
        for slot in range(SLAB):
            f_out[pl.ds(core * rows * SLAB + ORDER[slot], rows, stride=SLAB), :] = f_in[
                core, pl.ds(FIELD_BASE[slot], rows), :
            ].astype(F32)
        part = pl.ds(core * rows * SLAB, rows * SLAB)
        store(f_out.at[part], field_ref.at[part])
        for slot in range(SLAB):
            store(
                f_in.at[core, pl.ds(OUT_BASE[slot], OUT_SLOT)],
                out_ref.at[pl.ds((2 * ORDER[slot] + core) * OUT_SLOT, OUT_SLOT)],
            )
    whole.wait()
    for p, ref in enumerate((inner_ref, outer_ref)):
        part = pl.ds(p * GRAD, GRAD)
        w_out[part, :] = g_in[pl.ds(p * W_SLOT, GRAD), :].astype(F32)
        store(w_out.at[part], ref)
    for copy in stores:
        copy.wait()


def shards(displace, weight_in, weight_out, cotangent):
    hbm = pl.BlockSpec(memory_space=pl.ANY)
    rows = jnp.transpose(displace, (1, 2, 0, 3)).reshape(SLAB * FY * FZ, LANES)
    win = jnp.transpose(weight_in, (0, 1, 2, 4, 3)).reshape(GRAD, LANES)
    wout = weight_out.reshape(GRAD, LANES)
    dma = pltpu.SemaphoreType.DMA
    full, grads = pl.pallas_call(
        kernel,
        out_shape=(
            jax.ShapeDtypeStruct((2, AF_TOTAL, LANES), BF),
            jax.ShapeDtypeStruct((2 * W_SLOT, LANES), BF),
        ),
        in_specs=[hbm] * 4,
        out_specs=[hbm] * 2,
        scratch_shapes=[
            pltpu.VMEM((SLAB * DROWS, LANES), BF),
            pltpu.VMEM((SLAB + 4, DY, PITCH, LANES), BF),
            pltpu.VMEM((SLAB + 4, DY, CZ, LANES), BF),
            pltpu.VMEM((SLAB + 2, HY, CZ, LANES), BF),
            pltpu.VMEM((SLAB + 2, HY, CZ, LANES), BF),
            pltpu.VMEM((SLAB + 2, HY + 2, PITCH, LANES), BF),
            pltpu.VMEM((SLAB + 2, HY + 3, PITCH, LANES), BF),
            pltpu.VMEM((2, GRAD, LANES), BF),
            pltpu.VMEM((2, GRAD, LANES), BF),
            pltpu.VMEM((9 * LANES, 2 * LANES), BF),
            pltpu.VMEM((3 * BLOCKS * LANES, LANES), BF),
            pltpu.VMEM((9 * LANES, 2 * LANES), BF),
            pltpu.VMEM((3 * BLOCKS * LANES, LANES), BF),
            pltpu.VMEM((BLOCKS * LANES, 3 * LANES), F32),
            pltpu.VMEM((BLOCKS * LANES, 3 * LANES), F32),
            pltpu.VMEM((SLAB * (DROWS + PITCH - FZ), LANES), F32),
            pltpu.VMEM((SLAB * FIELD_SLOT, LANES), F32),
            pltpu.VMEM((AF_TOTAL, LANES), F32),
            pltpu.VMEM((AF_TOTAL, LANES), BF),
            pltpu.VMEM((AF_TOTAL, LANES), BF),
            pltpu.VMEM((2, 2 * W_SLOT, LANES), BF),
            pltpu.VMEM((2, W_PART, LANES), BF),
            pltpu.VMEM((2, W_PART, LANES), BF),
            pltpu.VMEM((SLAB, DROWS, LANES), BF),
            pltpu.VMEM((SLAB, DROWS, LANES), BF),
            pltpu.VMEM((DROWS + 16, LANES), F32),
            pltpu.VMEM((7 * AF_TOTAL // 8, LANES), BF),
            pltpu.VMEM((2, W_SLOT, LANES), BF),
            pltpu.VMEM((2, 3, W_PART, LANES), BF),
            pltpu.VMEM((2, W_PART, LANES), BF),
            dma((4,)), dma((10,)), dma((10,)),
            dma((5,)), dma((5,)), dma((3, 7)), dma((3, 7)), dma((3, 7)), dma((3, 7)),
            dma((2, 3)), dma((2, 3)), dma((2,)), dma((2,)), dma((2, 3)), dma((2, 3)), dma((5,)),
        ],
        compiler_params=pltpu.CompilerParams(
            collective_id=0, has_side_effects=True, vmem_limit_bytes=56 * 1024 * 1024
        ),
        cost_estimate=pl.CostEstimate(flops=4_000_000_000, bytes_accessed=8_000_000, transcendentals=400_000),
    )(rows, cotangent, win, wout)
    out, field, inner, outer = pl.pallas_call(
        finish,
        out_shape=(
            jax.ShapeDtypeStruct((SLAB * CY * CZ, LANES), BF),
            jax.ShapeDtypeStruct((SLAB * FY * FZ, LANES), F32),
            jax.ShapeDtypeStruct((GRAD, LANES), F32),
            jax.ShapeDtypeStruct((GRAD, LANES), F32),
        ),
        in_specs=[hbm] * 2,
        out_specs=[hbm] * 4,
        scratch_shapes=[
            pltpu.VMEM((2, AF_TOTAL, LANES), BF),
            pltpu.VMEM((2 * W_SLOT, LANES), BF),
            pltpu.VMEM((SLAB * FY * FZ, LANES), F32),
            pltpu.VMEM((2 * GRAD, LANES), F32),
            dma((3,)), dma((12,)),
        ],
        compiler_params=pltpu.CompilerParams(vmem_limit_bytes=56 * 1024 * 1024),
        cost_estimate=pl.CostEstimate(flops=0, bytes_accessed=5_000_000, transcendentals=0),
    )(full, grads)
    out_field = out.reshape(SLAB, CY, CZ, LANES)
    field_grad = jnp.transpose(field.reshape(FY, FZ, SLAB, LANES), (2, 0, 1, 3))
    inner_grad = jnp.transpose(inner.reshape(3, 3, 3, MID, LANES), (0, 1, 2, 4, 3))
    outer_grad = outer.reshape(3, 3, 3, MID, LANES)
    return (out_field, field_grad, inner_grad, outer_grad)


def solution(mesh):
    return jax.shard_map(
        shards,
        mesh=mesh,
        in_specs=(
            P("gx", None, None, None),
            P(None, None, None, None, "af"),
            P(None, None, None, "af", None),
            P("gx", None, None, None),
        ),
        out_specs=(
            P("gx", None, None, None),
            P("gx", None, None, None),
            P(None, None, None, None, "af"),
            P(None, None, None, "af", None),
        ),
        check_vma=False,
    )
```

```python
import jax
import jax.numpy as jnp
from jax import lax
from jax.experimental import pallas as pl
from jax.experimental.pallas import tpu as pltpu
from jax.sharding import PartitionSpec as P

MESH = pl.DeviceIdType.MESH
BF = jnp.bfloat16
F32 = jnp.float32

SLAB = 4
CY, CZ = 16, 32
PITCH = 48
LANES = 128
MID = 32
TWO = 2 * MID
FY, FZ = 20, 36
HY, DY, OY, GY = 10, 12, 8, 10
DROWS = DY * FZ
BLOCKS = 5
ORDER = (1, 2, 0, 3)

OUT_SLOT = OY * CZ
FIELD_SLOT = 384
AF_ROWS = 2 * (OUT_SLOT + FIELD_SLOT)
AF_PIECES = 2
AF_TOTAL = AF_PIECES * AF_ROWS
OUT_BASE = tuple(slot // 2 * AF_ROWS + slot % 2 * OUT_SLOT for slot in range(SLAB))
FIELD_BASE = tuple(slot // 2 * AF_ROWS + 2 * OUT_SLOT + slot % 2 * FIELD_SLOT for slot in range(SLAB))
GRAD = 27 * MID
W_SLOT = 896
W_PART = W_SLOT // 4


def align(value, by=16):
    return pl.multiple_of(value, by)


def kernel(
    disp, cot, win, wout,
    full_ref, grads_ref,
    raw, D, C, HA, HB, PA, PB, WIN, WOUT, W1T, W1, W2T, W2, AI, AO, DF, FS, EXTRA, B, R, WB, WZ, WC, HS, HL, HF,
    land_af, land_wc, land_z, land_x,
    load_sem, halo_s, halo_r, core_s, core_r, rs_s, rs_r, ag_s, ag_r, ws_s, ws_r, wx_s, wx_r, wg_s, wg_r, store_sem,
):
    gx = lax.axis_index("gx")
    af = lax.axis_index("af")
    core = lax.rem(af, 2)
    y = lax.rem(lax.div(af, 2), 4)
    xl = lax.div(af, 8)
    z = lax.rem(gx, 4)
    xh = lax.div(gx, 4)

    af_peers, z_peers = [], []
    for dx, dy in ((1, 2), (0, 2), (1, 1), (1, 3), (0, 1), (0, 3), (1, 0)):
        x2, y2 = lax.rem(xl + dx, 2), lax.rem(y + dy, 4)
        af_peers.append(((gx, (x2 * 4 + y2) * 2 + core), x2 * 4 + y2))
    for dz in (2, 1, 3):
        z2 = lax.rem(z + dz, 4)
        z_peers.append(((xh * 4 + z2, af), z2))
    x_peer = ((1 - xh) * 4 + z, af)
    other_core = (gx, af + 1 - 2 * core)
    right = (lax.rem(gx + 1, 8), af)
    left = (lax.rem(gx + 7, 8), af)

    cot_lines = pl.ds(2 - 2 * core, HY)
    loads = [
        pltpu.make_async_copy(disp.at[pl.ds(align(core * 8 * FZ * SLAB), DY * FZ * SLAB)], raw, load_sem.at[0]),
        pltpu.make_async_copy(cot.at[:, pl.ds(6 * core, HY)], C.at[pl.ds(2, SLAB), cot_lines], load_sem.at[1]),
        pltpu.make_async_copy(win, WIN.at[core], load_sem.at[2]),
        pltpu.make_async_copy(wout, WOUT.at[core], load_sem.at[3]),
    ]
    for load in loads:
        load.start()
    barrier = pltpu.get_barrier_semaphore()
    peers = [peer for peer, _ in af_peers + z_peers] + [x_peer, other_core, left, right]
    for peer in peers:
        pl.semaphore_signal(barrier, inc=1, device_id=peer, device_id_type=MESH)

    C[:, pl.ds(10 * core, 2)] = jnp.zeros((8, 2, CZ, LANES), BF)
    PA[:, pl.ds(10 * core, 2)] = jnp.zeros((6, 2, PITCH, LANES), BF)
    PB[:, pl.ds(10 * core + 1, 2)] = jnp.zeros((6, 2, PITCH, LANES), BF)
    DF[DROWS * SLAB:, :] = jnp.zeros((SLAB * (PITCH - FZ), LANES), F32)
    HF[DROWS:, :] = jnp.zeros((16, LANES), F32)
    for straight in (W1, W2):
        for a in range(3):
            straight[pl.ds((a * BLOCKS + 4) * LANES + TWO, TWO), :] = jnp.zeros((TWO, LANES), BF)
    AI[...] = jnp.zeros_like(AI)
    AO[...] = jnp.zeros_like(AO)
    for k in range(2):
        for p in range(2):
            WB[k, pl.ds(p * W_SLOT + GRAD, W_SLOT - GRAD), :] = jnp.zeros((W_SLOT - GRAD, LANES), BF)
    for slot in range(SLAB):
        FS[pl.ds(slot * FIELD_SLOT + GY * FZ, FIELD_SLOT - GY * FZ), :] = jnp.zeros(
            (FIELD_SLOT - GY * FZ, LANES), F32
        )

    loads[0].wait()
    line_row = lax.broadcasted_iota(jnp.int32, (PITCH, LANES), 0)

    def widen(i, _):
        rows = pl.ds(align(i * 4 * FZ * SLAB), 4 * FZ * SLAB)
        DF[rows, :] = raw[rows, :].astype(F32)
        return 0

    lax.fori_loop(0, DY // 4, widen, 0)
    for x in range(SLAB):
        HS[x] = DF[pl.ds(x, DROWS, stride=SLAB), :].astype(BF)

    def part(i, _):
        for x in range(SLAB):
            line = DF[pl.ds(i * FZ * SLAB + x, PITCH, stride=SLAB), :]
            D[x + 2, i] = jnp.where(line_row < FZ, line, 0.0).astype(BF)
        return 0

    lax.fori_loop(0, DY, part, 0)
    for load in loads[1:]:
        load.wait()

    def halo(index, src, dst, peer):
        copy = pltpu.make_async_remote_copy(
            src_ref=src, dst_ref=dst, send_sem=halo_s.at[index], recv_sem=halo_r.at[index],
            device_id=peer, device_id_type=MESH,
        )
        copy.start()
        halos.append(copy)
        return copy

    halos = []
    pl.semaphore_wait(barrier, len(peers))
    weights = [
        halo(0, WIN.at[core], WIN.at[core], other_core),
        halo(1, WOUT.at[core], WOUT.at[core], other_core),
    ]
    given = ((3, 1, right), (0, 6, left), (2, 0, right), (1, 7, left))
    first_halos = []
    for k, (x, place, peer) in enumerate(given):
        first_halos.append(
            (
                halo(2 + 2 * k, HS.at[x], HL.at[k], peer),
                halo(3 + 2 * k, C.at[x + 2, cot_lines], C.at[place, cot_lines], peer),
            )
        )

    def extra_out(i, _):
        for slot in range(SLAB):
            EXTRA[pl.ds(align(OUT_BASE[slot] + i * CZ), CZ), :] = DF[
                pl.ds((i + 2) * FZ * SLAB + 2 * SLAB + ORDER[slot], CZ, stride=SLAB), :
            ]
        return 0

    lax.fori_loop(0, OY, extra_out, 0)
    for slot in range(SLAB):
        base = FIELD_BASE[slot]
        EXTRA[pl.ds(base, FIELD_SLOT), :] = jnp.zeros((FIELD_SLOT, LANES), F32)
        for line in range(GY):
            EXTRA[pl.ds(base + line * FZ + 2, CZ), :] = C[ORDER[slot] + 2, 2 * core + line].astype(F32)

    for copy in weights:
        copy.wait_recv()

    def places(blocks_c2):
        table = {(b, c): b * LANES + c * TWO for b in range(3) for c in range(2)}
        for b, row in enumerate(blocks_c2):
            table[b, 2] = row
        return table

    in_places = places((4 * LANES, 3 * LANES + TWO, 3 * LANES))
    out_places = places((3 * LANES, 3 * LANES + TWO, 4 * LANES))
    for src, straight, turned, table in ((WIN, W1, W1T, in_places), (WOUT, W2, W2T, out_places)):
        for a in range(3):
            for (b, c), row in table.items():
                for k in range(2):
                    straight[pl.ds(a * BLOCKS * LANES + row + k * MID, MID), :] = src[
                        k, pl.ds(((a * 3 + b) * 3 + c) * MID, MID), :
                    ]
        for a in range(3):
            for b in range(3):
                rows = pl.ds((a * 3 + b) * LANES, LANES)
                turned[rows, :LANES] = straight[pl.ds((a * BLOCKS + b) * LANES, LANES), :].T
                row = table[b, 2]
                pair = straight[pl.ds(a * BLOCKS * LANES + row // LANES * LANES, LANES), :]
                if row % LANES:
                    pair = jnp.concatenate([pair[TWO:], pair[:TWO]], axis=0)
                turned[rows, LANES:] = pair.T

    def lane_half(values):
        return pltpu.roll(values, TWO, 1)

    def row_roll(values, count):
        return pltpu.roll(values, count % values.shape[0], 0)

    def gather(values, direction):
        near, far = values[:, :LANES], values[:, LANES:]
        return near + row_roll(lane_half(near), -direction) + row_roll(far, -2 * direction)

    def first_mids(values):
        lane = lax.broadcasted_iota(jnp.int32, values.shape, 1)
        return jnp.where(lane < TWO, values, 0.0)

    rows = HY * PITCH

    def store_hidden(plane, hidden):
        near = hidden + lane_half(row_roll(hidden, -1))
        far = row_roll(hidden, -2).reshape(HY, PITCH, LANES)[:, :CZ].reshape(HY * CZ, LANES)
        later = jnp.concatenate([far[CZ:], jnp.zeros((CZ, LANES), F32)], axis=0)
        HA[plane] = near.reshape(HY, PITCH, LANES)[:, :CZ].astype(BF)
        HB[plane] = (far + lane_half(later)).reshape(HY, CZ, LANES).astype(BF)

    def store_grad(plane, grad):
        near = grad + lane_half(row_roll(grad, 1))
        far = row_roll(grad, 2)
        nothing = jnp.zeros((PITCH, LANES), F32)
        both = jnp.concatenate([nothing, far], axis=0) + lane_half(jnp.concatenate([far, nothing], axis=0))
        PA[plane, pl.ds(2 - 2 * core, HY)] = near.reshape(HY, PITCH, LANES).astype(BF)
        PB[plane, pl.ds(2 - 2 * core, HY + 1)] = both.reshape(HY + 1, PITCH, LANES).astype(BF)

    def stage_one(x):
        lhs = jnp.concatenate(
            [D[x + 1 + a, pl.ds(b, HY)].reshape(rows, LANES) for a in range(3) for b in range(3)], axis=1
        )
        pre = gather(jnp.dot(lhs, W1T[...], preferred_element_type=F32), 1)
        lhs = jnp.concatenate(
            [
                C[x + 3 - a, pl.ds(2 - b, HY)].reshape(HY * CZ, LANES)
                for a in range(3)
                for b in range(3)
            ],
            axis=1,
        )
        back = jnp.dot(lhs, W2T[...], preferred_element_type=F32).reshape(HY, CZ, 2 * LANES)
        back = jnp.concatenate([back, jnp.zeros((HY, PITCH - CZ, 2 * LANES), F32)], axis=1)
        grad = gather(back.reshape(rows, 2 * LANES), -1)
        square = pre * pre + 0.01
        inverse = lax.rsqrt(square)
        hidden = first_mids(0.505 * pre + 0.495 * (square * inverse))
        grad = first_mids(grad * (0.505 + 0.495 * (pre * inverse)))
        store_hidden(x + 1, hidden)
        store_grad(x + 1, grad)

    def arrived(k):
        first_halos[k][0].wait_recv()
        HF[0:DROWS, :] = HL[k].astype(F32)
        for line in range(DY):
            value = HF[pl.ds(line * FZ, PITCH), :]
            D[given[k][1], line] = jnp.where(line_row < FZ, value, 0.0).astype(BF)
        first_halos[k][1].wait_recv()

    over_rows = (((0,), (0,)), ((), ()))

    def hidden_blocks(plane):
        blocks = [HA[plane, pl.ds(b, OY)] for b in range(3)] + [HB[plane, pl.ds(b, OY)] for b in (0, 2)]
        return [block.reshape(OUT_SLOT, LANES) for block in blocks]

    def grad_blocks(plane):
        blocks = [PA[plane, pl.ds(2 - b, GY)] for b in range(3)] + [PB[plane, pl.ds(b, GY)] for b in (1, 3)]
        return [block.reshape(GY * PITCH, LANES) for block in blocks]

    def outer_terms(i):
        right_side = jnp.concatenate(
            [C[i + 3 - a, pl.ds(2, OY)].reshape(OUT_SLOT, LANES) for a in range(3)], axis=1
        )
        AO[...] += lax.dot_general(
            jnp.concatenate(hidden_blocks(i + 1), axis=1), right_side, over_rows, preferred_element_type=F32
        )

    def inner_terms(i):
        right_side = jnp.concatenate(
            [D[i + 1 + a, pl.ds(2 * core, GY)].reshape(GY * PITCH, LANES) for a in range(3)], axis=1
        )
        AI[...] += lax.dot_general(
            jnp.concatenate(grad_blocks(i + 1), axis=1), right_side, over_rows, preferred_element_type=F32
        )

    def inner_planes_terms(i, _):
        outer_terms(1 + i)
        inner_terms(1 + i)
        return 0

    stage_one(1)
    stage_one(2)
    lax.fori_loop(0, 2, inner_planes_terms, 0)
    for k, x in ((0, 0), (1, 3)):
        arrived(k)
        stage_one(x)

    sends = []

    def send(src, dst, send_sem, recv_sem, peer):
        copy = pltpu.make_async_remote_copy(
            src_ref=src, dst_ref=dst, send_sem=send_sem, recv_sem=recv_sem, device_id=peer, device_id_type=MESH
        )
        copy.start()
        sends.append(copy)
        return copy

    def scatter(peers, piece, landing, size, sems):
        return [
            send(piece(align(place * size), size), landing(j), sems[0](j), sems[1](j), peer)
            for j, (peer, place) in enumerate(peers)
        ]

    def total(copies, piece, landing, me, size):
        for copy in copies:
            copy.wait_recv()
        value = piece(align(me * size), size)[...].astype(F32)
        for j in range(len(copies)):
            value = value + landing(j)[...].astype(F32)
        return value

    def spread_out(peers, whole, me, size, sems):
        rows = whole(align(me * size), size)
        return [send(rows, rows, sems[0](j), sems[1](j), peer) for j, (peer, _) in enumerate(peers)]

    def keep(src, dst, index):
        store = pltpu.make_async_copy(src, dst, store_sem.at[index])
        store.start()
        stores.append(store)

    class AfSum:
        def __init__(self, p):
            self.p, self.size, self.base = p, AF_ROWS // 8, p * AF_ROWS
            self.me = xl * 4 + y
            self.landing = lambda j: land_af.at[p, j]
            self.step = 0

        def piece(self, off, size):
            return B.at[pl.ds(align(self.base + off), size)]

        def whole(self, off, size):
            return R.at[pl.ds(align(self.base + off), size)]

        def advance(self):
            p, me, size = self.p, self.me, self.size
            if self.step == 0:
                sems = (lambda j: rs_s.at[p, j], lambda j: rs_r.at[p, j])
                self.copies = scatter(af_peers, self.piece, self.landing, size, sems)
            elif self.step == 1:
                value = total(self.copies, self.piece, self.landing, me, size)
                value = value + EXTRA[pl.ds(align(self.base + me * size), size), :]
                self.whole(align(me * size), size)[...] = value.astype(BF)
                sems = (lambda j: ag_s.at[p, j], lambda j: ag_r.at[p, j])
                self.copies = spread_out(af_peers, self.whole, me, size, sems)
            elif self.step == 2:
                for copy in self.copies:
                    copy.wait_recv()
                rows = self.whole(0, AF_ROWS)
                there = full_ref.at[core, pl.ds(self.base, AF_ROWS)]
                self.copies = [send(rows, there, core_s.at[p], core_r.at[p], other_core)]
                keep(rows, there, p)
            else:
                self.copies[0].wait_recv()
            self.step += 1

    class GxSum:
        def __init__(self, p):
            self.p, self.base = p, p * W_SLOT
            self.landing = lambda j: land_z.at[p, j]
            self.step = 0

        def piece(self, off, size):
            return WB.at[core, pl.ds(align(self.base + off), size)]

        def advance(self):
            p, rows = self.p, pl.ds(self.base, W_SLOT)
            if self.step == 0:
                self.copies = [
                    send(WB.at[1 - core, rows], land_wc.at[p], core_s.at[2 + p], core_r.at[2 + p], other_core)
                ]
            elif self.step == 1:
                self.copies[0].wait_recv()
                mine = WB.at[core, rows]
                mine[...] = (mine[...].astype(F32) + land_wc[p].astype(F32)).astype(BF)
                sems = (lambda j: ws_s.at[p, j], lambda j: ws_r.at[p, j])
                self.copies = scatter(z_peers, self.piece, self.landing, W_PART, sems)
            elif self.step == 2:
                WZ[p] = total(self.copies, self.piece, self.landing, z, W_PART).astype(BF)
                self.copies = [send(WZ.at[p], land_x.at[p], wx_s.at[p], wx_r.at[p], x_peer)]
            elif self.step == 3:
                self.copies[0].wait_recv()
                value = WZ[p].astype(F32) + land_x[p].astype(F32)
                WC[p] = value.astype(BF)
                there = grads_ref.at[pl.ds(align(self.base + z * W_PART), W_PART)]
                self.copies = [
                    send(WC.at[p], there, wg_s.at[p, j], wg_r.at[p, j], peer) for j, (peer, _) in enumerate(z_peers)
                ]
                keep(WC.at[p], there, 2 + p)
            else:
                for copy in self.copies:
                    copy.wait_recv()
            self.step += 1

    stores = []
    inner_planes, outer_planes = AfSum(0), AfSum(1)
    inner_sum, outer_sum = GxSum(0), GxSum(1)

    def out_plane(slot):
        i = ORDER[slot]
        lhs = jnp.concatenate([block for a in range(3) for block in hidden_blocks(i + a)], axis=1)
        B[pl.ds(OUT_BASE[slot], OUT_SLOT), :] = jnp.dot(lhs, W2[...], preferred_element_type=F32).astype(BF)

    def field_plane(slot):
        i = ORDER[slot]
        lhs = jnp.concatenate([block for a in range(3) for block in grad_blocks(i + 2 - a)], axis=1)
        block = jnp.dot(lhs, W1[...], preferred_element_type=F32).reshape(GY, PITCH, LANES)
        base = slot * FIELD_SLOT
        for line in range(GY):
            FS[pl.ds(base + line * FZ, FZ), :] = block[line, :FZ]
        B[pl.ds(FIELD_BASE[slot], FIELD_SLOT), :] = FS[pl.ds(base, FIELD_SLOT), :].astype(BF)

    def collect(acc, table, base):
        for a in range(3):
            for (b, c), row in table.items():
                for k in range(2):
                    WB[k, pl.ds(base + ((a * 3 + b) * 3 + c) * MID, MID), :] = acc[
                        pl.ds(row + k * MID, MID), a * LANES : (a + 1) * LANES
                    ].astype(BF)

    def edge_outer():
        outer_terms(0)
        outer_terms(3)
        collect(AO, out_places, W_SLOT)

    def edge_inner():
        inner_terms(0)
        inner_terms(3)
        collect(AI, in_places, 0)

    def far_planes():
        for k, x in ((2, -1), (3, 4)):
            arrived(k)
            stage_one(x)

    edge_outer()
    outer_sum.advance()
    out_plane(0)
    out_plane(1)
    field_plane(0)
    field_plane(1)
    inner_planes.advance()
    edge_inner()
    inner_sum.advance()
    far_planes()
    outer_sum.advance()
    inner_sum.advance()
    out_plane(2)
    out_plane(3)
    field_plane(2)
    field_plane(3)
    outer_planes.advance()
    inner_planes.advance()
    outer_sum.advance()
    inner_sum.advance()
    outer_planes.advance()
    inner_planes.advance()
    outer_sum.advance()
    inner_sum.advance()
    outer_planes.advance()
    inner_planes.advance()
    outer_planes.advance()
    outer_sum.advance()
    inner_sum.advance()
    for store in stores:
        store.wait()
    for copy in halos + sends:
        copy.wait_send()


def finish(full, grads, out_ref, field_ref, inner_ref, outer_ref, f_in, g_in, f_out, w_out, in_sem, out_sem):
    inputs = [pltpu.make_async_copy(full.at[core], f_in.at[core], in_sem.at[core]) for core in range(2)]
    whole = pltpu.make_async_copy(grads, g_in, in_sem.at[2])
    for copy in inputs + [whole]:
        copy.start()
    stores = []

    def store(src, dst):
        copy = pltpu.make_async_copy(src, dst, out_sem.at[len(stores)])
        copy.start()
        stores.append(copy)

    rows = GY * FZ
    for core in range(2):
        inputs[core].wait()
        for slot in range(SLAB):
            f_out[pl.ds(core * rows * SLAB + ORDER[slot], rows, stride=SLAB), :] = f_in[
                core, pl.ds(FIELD_BASE[slot], rows), :
            ].astype(F32)
        part = pl.ds(core * rows * SLAB, rows * SLAB)
        store(f_out.at[part], field_ref.at[part])
        for slot in range(SLAB):
            store(
                f_in.at[core, pl.ds(OUT_BASE[slot], OUT_SLOT)],
                out_ref.at[pl.ds((2 * ORDER[slot] + core) * OUT_SLOT, OUT_SLOT)],
            )
    whole.wait()
    for p, ref in enumerate((inner_ref, outer_ref)):
        part = pl.ds(p * GRAD, GRAD)
        w_out[part, :] = g_in[pl.ds(p * W_SLOT, GRAD), :].astype(F32)
        store(w_out.at[part], ref)
    for copy in stores:
        copy.wait()


def shards(displace, weight_in, weight_out, cotangent):
    hbm = pl.BlockSpec(memory_space=pl.ANY)
    rows = jnp.transpose(displace, (1, 2, 0, 3)).reshape(SLAB * FY * FZ, LANES)
    win = jnp.transpose(weight_in, (0, 1, 2, 4, 3)).reshape(GRAD, LANES)
    wout = weight_out.reshape(GRAD, LANES)
    dma = pltpu.SemaphoreType.DMA
    full, grads = pl.pallas_call(
        kernel,
        out_shape=(
            jax.ShapeDtypeStruct((2, AF_TOTAL, LANES), BF),
            jax.ShapeDtypeStruct((2 * W_SLOT, LANES), BF),
        ),
        in_specs=[hbm] * 4,
        out_specs=[hbm] * 2,
        scratch_shapes=[
            pltpu.VMEM((SLAB * DROWS, LANES), BF),
            pltpu.VMEM((SLAB + 4, DY, PITCH, LANES), BF),
            pltpu.VMEM((SLAB + 4, DY, CZ, LANES), BF),
            pltpu.VMEM((SLAB + 2, HY, CZ, LANES), BF),
            pltpu.VMEM((SLAB + 2, HY, CZ, LANES), BF),
            pltpu.VMEM((SLAB + 2, HY + 2, PITCH, LANES), BF),
            pltpu.VMEM((SLAB + 2, HY + 3, PITCH, LANES), BF),
            pltpu.VMEM((2, GRAD, LANES), BF),
            pltpu.VMEM((2, GRAD, LANES), BF),
            pltpu.VMEM((9 * LANES, 2 * LANES), BF),
            pltpu.VMEM((3 * BLOCKS * LANES, LANES), BF),
            pltpu.VMEM((9 * LANES, 2 * LANES), BF),
            pltpu.VMEM((3 * BLOCKS * LANES, LANES), BF),
            pltpu.VMEM((BLOCKS * LANES, 3 * LANES), F32),
            pltpu.VMEM((BLOCKS * LANES, 3 * LANES), F32),
            pltpu.VMEM((SLAB * (DROWS + PITCH - FZ), LANES), F32),
            pltpu.VMEM((SLAB * FIELD_SLOT, LANES), F32),
            pltpu.VMEM((AF_TOTAL, LANES), F32),
            pltpu.VMEM((AF_TOTAL, LANES), BF),
            pltpu.VMEM((AF_TOTAL, LANES), BF),
            pltpu.VMEM((2, 2 * W_SLOT, LANES), BF),
            pltpu.VMEM((2, W_PART, LANES), BF),
            pltpu.VMEM((2, W_PART, LANES), BF),
            pltpu.VMEM((SLAB, DROWS, LANES), BF),
            pltpu.VMEM((SLAB, DROWS, LANES), BF),
            pltpu.VMEM((DROWS + 16, LANES), F32),
            pltpu.VMEM((AF_PIECES, 7, AF_ROWS // 8, LANES), BF),
            pltpu.VMEM((2, W_SLOT, LANES), BF),
            pltpu.VMEM((2, 3, W_PART, LANES), BF),
            pltpu.VMEM((2, W_PART, LANES), BF),
            dma((4,)), dma((10,)), dma((10,)),
            dma((4,)), dma((4,)), dma((2, 7)), dma((2, 7)), dma((2, 7)), dma((2, 7)),
            dma((2, 3)), dma((2, 3)), dma((2,)), dma((2,)), dma((2, 3)), dma((2, 3)), dma((4,)),
        ],
        compiler_params=pltpu.CompilerParams(
            collective_id=0, has_side_effects=True, vmem_limit_bytes=56 * 1024 * 1024
        ),
        cost_estimate=pl.CostEstimate(flops=4_000_000_000, bytes_accessed=8_000_000, transcendentals=400_000),
    )(rows, cotangent, win, wout)
    out, field, inner, outer = pl.pallas_call(
        finish,
        out_shape=(
            jax.ShapeDtypeStruct((SLAB * CY * CZ, LANES), BF),
            jax.ShapeDtypeStruct((SLAB * FY * FZ, LANES), F32),
            jax.ShapeDtypeStruct((GRAD, LANES), F32),
            jax.ShapeDtypeStruct((GRAD, LANES), F32),
        ),
        in_specs=[hbm] * 2,
        out_specs=[hbm] * 4,
        scratch_shapes=[
            pltpu.VMEM((2, AF_TOTAL, LANES), BF),
            pltpu.VMEM((2 * W_SLOT, LANES), BF),
            pltpu.VMEM((SLAB * FY * FZ, LANES), F32),
            pltpu.VMEM((2 * GRAD, LANES), F32),
            dma((3,)), dma((12,)),
        ],
        compiler_params=pltpu.CompilerParams(vmem_limit_bytes=56 * 1024 * 1024),
        cost_estimate=pl.CostEstimate(flops=0, bytes_accessed=5_000_000, transcendentals=0),
    )(full, grads)
    out_field = out.reshape(SLAB, CY, CZ, LANES)
    field_grad = jnp.transpose(field.reshape(FY, FZ, SLAB, LANES), (2, 0, 1, 3))
    inner_grad = jnp.transpose(inner.reshape(3, 3, 3, MID, LANES), (0, 1, 2, 4, 3))
    outer_grad = outer.reshape(3, 3, 3, MID, LANES)
    return (out_field, field_grad, inner_grad, outer_grad)


def solution(mesh):
    return jax.shard_map(
        shards,
        mesh=mesh,
        in_specs=(
            P("gx", None, None, None),
            P(None, None, None, None, "af"),
            P(None, None, None, "af", None),
            P("gx", None, None, None),
        ),
        out_specs=(
            P("gx", None, None, None),
            P("gx", None, None, None),
            P(None, None, None, None, "af"),
            P(None, None, None, "af", None),
        ),
        check_vma=False,
    )
```
